256 devices in a mesh: dp: 8 (over x, core), fsdp: 32 (over y, z).
Axes of the slice: x: 4, y: 4, z: 8, core: 2. Of those that a mesh axis runs over, the one named last changes fastest.
Arguments:
- tokens: bfloat16 [1024, 4096], P(('dp', 'fsdp')), may hold values from -6 to 6
- cotangent: bfloat16 [1024, 4096], P(('dp', 'fsdp')), may hold values from -6 to 6
- gate_blocks: bfloat16 [7168, 4096], P('fsdp'), may hold values from -0.125 to 0.125
- up_blocks: bfloat16 [7168, 4096], P('fsdp'), may hold values from -0.125 to 0.125
- down_blocks: bfloat16 [7168, 4096], P('fsdp'), may hold values from -0.0625 to 0.0625
- block_index: int32 [3, 7168], P(None, 'fsdp'), may hold values from 0 to 63, as said below
Outputs:
- layer_out: bfloat16 [1024, 4096], P(('dp', 'fsdp'))
- input_grad: bfloat16 [1024, 4096], P(('dp', 'fsdp'))
- gate_grad: bfloat16 [7168, 4096], P('fsdp', 'dp')
- up_grad: bfloat16 [7168, 4096], P('fsdp', 'dp')
- down_grad: bfloat16 [7168, 4096], P('fsdp', 'dp')
The draws below stay inside these ranges and needn't reach their ends.
Inputs may be any that keep to these rules, and one draw needn't show every extreme that they name: `block_index`: slot q of each matrix lies in hidden block-column q // 32; the 32 slots of one hidden block-column name distinct feature blocks.
All inputs are finite; a program needn't handle non-finite values.
Results may differ from the reference program's by a relative error of at most 0.022.
Values may be sent and summed in bfloat16 or wider, within the bound.
No kernel may reach another device: no remote copies, remote signals or barrier semaphores. Data moves between devices by JAX's collectives and lax.ppermute only.
A program may use at most 128 MiB of HBM per device.

```python
import jax
import jax.numpy as jnp
from jax import lax

D = 4096
FF = 14336
BLK = 64
TOK_REP = 128
DB = 64
KEEP = 32
HCOL = 224
SLOTS = 7168
TOKENS = 1024
N_DP = 8


def draw_block_index(key, part):
    key = jax.random.fold_in(key, 7)
    scores = jax.random.randint(key, (3, HCOL, DB), 0, 1 << 20)
    scores = scores * DB + jnp.arange(DB, dtype=jnp.int32)
    ordering = jnp.argsort(scores, axis=-1, stable=True).astype(jnp.int32)
    return ordering[:, :, :KEEP].reshape(3, HCOL * KEEP)


def steps_of(stream_key, extent, pieces, smallest, top_value):
    gain, own = 1.0, jax.random.fold_in(stream_key, 6)
    for axis_at, parts in pieces:
        draws = jnp.exp(jax.random.uniform(jax.random.fold_in(own, axis_at), (parts,), jnp.float32, smallest / len(pieces), top_value / len(pieces)))
        gain = gain * jnp.repeat(draws, extent[axis_at] // parts).reshape([-1 if axis == axis_at else 1 for axis in range(len(extent))])
    return gain


def bell_draw(rng, extent, width, bound, cuts=(), kind=jnp.bfloat16):
    drawn = width * jax.random.normal(rng, extent, jnp.float32)
    if cuts:
        drawn = drawn * steps_of(rng, extent, cuts, -0.22, 0.18)
    return jnp.clip(drawn, -bound, bound).astype(kind)


def setup_inputs(seed: int = 0) -> dict:
    seeds = jax.random.split(jax.random.key(seed), 7)
    tokens = bell_draw(seeds[0], (TOKENS, D), 1.0, 6.0, ((0, 256),))
    cotangent = bell_draw(seeds[1], (TOKENS, D), 1.0, 6.0, ((0, 256),))
    gate_blocks = bell_draw(seeds[2], (SLOTS, BLK * BLK), (D // 2) ** -0.5, 0.125, ((0, 32),))
    up_blocks = bell_draw(seeds[3], (SLOTS, BLK * BLK), (D // 2) ** -0.5, 0.125, ((0, 32),))
    down_blocks = bell_draw(seeds[4], (SLOTS, BLK * BLK), (FF // 2) ** -0.5, 0.0625, ((0, 32),))
    block_index = draw_block_index(jax.random.fold_in(seeds[6], 71), 0)
    return {"tokens": tokens, "cotangent": cotangent, "gate_blocks": gate_blocks, "up_blocks": up_blocks, "down_blocks": down_blocks, "block_index": block_index}


def inward_filled(blocks, block_rows, column):
    shaped = blocks.reshape(blocks.shape[0], BLK, BLK)
    filled = jnp.zeros((D // BLK, BLK, FF // BLK, BLK), blocks.dtype)
    return filled.at[block_rows, :, column, :].set(shaped).reshape(D, FF)


def outward_filled(blocks, block_rows, column):
    shaped = blocks.reshape(blocks.shape[0], BLK, BLK)
    filled = jnp.zeros((FF // BLK, BLK, D // BLK, BLK), blocks.dtype)
    return filled.at[column, :, block_rows, :].set(shaped).reshape(FF, D)


def pick_inward(grad_full, block_rows, column):
    shaped = grad_full.reshape(D // BLK, BLK, FF // BLK, BLK)
    picked = shaped[block_rows, :, column, :]
    return picked.reshape(picked.shape[0], BLK * BLK)


def pick_outward(grad_full, block_rows, column):
    shaped = grad_full.reshape(FF // BLK, BLK, D // BLK, BLK)
    picked = shaped[column, :, block_rows, :]
    return picked.reshape(picked.shape[0], BLK * BLK)


def to_wire(values):
    return lax.optimization_barrier(values.astype(jnp.bfloat16)).astype(jnp.float32)


def reference(tokens, cotangent, gate_blocks, up_blocks, down_blocks, block_index):
    column = jnp.arange(SLOTS, dtype=jnp.int32) // KEEP
    gate_dense = inward_filled(gate_blocks, block_index[0], column)
    up_dense = inward_filled(up_blocks, block_index[1], column)
    down_dense = outward_filled(down_blocks, block_index[2], column)
    gate_linear = jnp.dot(tokens, gate_dense, preferred_element_type=jnp.float32)
    up_linear = jnp.dot(tokens, up_dense, preferred_element_type=jnp.float32)
    gate_sigmoid = jax.nn.sigmoid(gate_linear)
    hidden = (gate_linear * gate_sigmoid * up_linear).astype(jnp.bfloat16)
    layer_out = jnp.dot(hidden, down_dense, preferred_element_type=jnp.float32).astype(jnp.bfloat16)
    hidden_delta = jnp.dot(cotangent, down_dense.T, preferred_element_type=jnp.float32)
    gate_delta = (hidden_delta * up_linear * gate_sigmoid * (1.0 + gate_linear * (1.0 - gate_sigmoid))).astype(jnp.bfloat16)
    up_delta = (hidden_delta * gate_linear * gate_sigmoid).astype(jnp.bfloat16)
    input_grad = (jnp.dot(gate_delta, gate_dense.T, preferred_element_type=jnp.float32)
                  + jnp.dot(up_delta, up_dense.T, preferred_element_type=jnp.float32)).astype(jnp.bfloat16)
    gate_summed = jnp.zeros((SLOTS, BLK * BLK), jnp.float32)
    up_summed = jnp.zeros((SLOTS, BLK * BLK), jnp.float32)
    down_summed = jnp.zeros((SLOTS, BLK * BLK), jnp.float32)
    for replica in range(N_DP):
        first_row = replica * TOK_REP
        part_tokens = tokens[first_row:first_row + TOK_REP]
        part_gate = gate_delta[first_row:first_row + TOK_REP]
        part_up = up_delta[first_row:first_row + TOK_REP]
        part_hidden = hidden[first_row:first_row + TOK_REP]
        part_cotangent = cotangent[first_row:first_row + TOK_REP]
        gate_full = jnp.dot(part_tokens.T, part_gate, preferred_element_type=jnp.float32)
        gate_summed = gate_summed + to_wire(pick_inward(gate_full, block_index[0], column))
        up_full = jnp.dot(part_tokens.T, part_up, preferred_element_type=jnp.float32)
        up_summed = up_summed + to_wire(pick_inward(up_full, block_index[1], column))
        down_full = jnp.dot(part_hidden.T, part_cotangent, preferred_element_type=jnp.float32)
        down_summed = down_summed + to_wire(pick_outward(down_full, block_index[2], column))
    mean_factor = 1.0 / N_DP
    gate_grad = (gate_summed * mean_factor).astype(jnp.bfloat16)
    up_grad = (up_summed * mean_factor).astype(jnp.bfloat16)
    down_grad = (down_summed * mean_factor).astype(jnp.bfloat16)
    return (layer_out, input_grad, gate_grad, up_grad, down_grad)
```

```python
import jax
import jax.numpy as jnp
import numpy as np
from jax import lax
from jax.experimental import pallas as pl
from jax.experimental.pallas import tpu as pltpu
from jax.sharding import PartitionSpec as P

D = 4096
BLK = 64
KEEP = 32
COLS = 7
SLOT = COLS * KEEP
TOK = 128
HALF = 32
FEAT = 64 * HALF
WIDE = COLS * 128
NX, NC, NY, NZ = 4, 2, 4, 8
BF = jnp.bfloat16
F32 = jnp.float32


def swap_matrix():
    m = np.zeros((256, 256), np.float32)
    for a in range(16):
        for b in range(16):
            m[a * 16 + b, b * 16 + a] = 1
    return m


def feature_split():
    m = np.zeros((256, 256), np.float32)
    for i in range(4):
        for p in range(2):
            for k in range(HALF):
                m[i * 64 + 2 * k + p, p * 128 + i * 32 + k] = 1
    return m


def hidden_split():
    m = np.zeros((512, 256), np.float32)
    for j in range(4):
        for p in range(2):
            for k in range(HALF):
                m[j * 128 + 2 * k + p, p * 128 + j * 32 + k] = 1
    return m


def hidden_join():
    m = np.zeros((256, 512), np.float32)
    for j in range(4):
        for p in range(2):
            for k in range(HALF):
                for h in range(2):
                    m[p * 128 + j * 32 + k, j * 128 + h * 64 + 2 * k + p] = 1
    return m


SWAP = swap_matrix()
FSPLIT = feature_split()
HSPLIT = hidden_split()
HJOIN = hidden_join()


def mm(a, b):
    return jnp.dot(a, b, preferred_element_type=F32)


def mm_nt(a, b):
    return lax.dot_general(a, b, (((1,), (1,)), ((), ())), preferred_element_type=F32)


def low_half(shape):
    return lax.broadcasted_iota(jnp.int32, shape, 1) < 64


def prep_kernel(idx, g_ref, u_ref, d_ref, swap, pg, pu, pd, scr):
    j = pl.program_id(0)
    pd[...] = jnp.zeros_like(pd)

    @pl.when(j < COLS)
    def _():
        pg[...] = jnp.zeros_like(pg)
        pu[...] = jnp.zeros_like(pu)
        for m, src in enumerate((g_ref, u_ref, d_ref)):
            for qh in range(2):
                rows = slice(qh * 16, qh * 16 + 16)
                halves = [
                    jnp.concatenate(
                        [src[rows, (kh * 16 + k) * 128:(kh * 16 + k + 1) * 128] for k in range(16)], axis=0
                    )
                    for kh in range(2)
                ]
                tiles = scr.at[2 * m + qh]
                tiles[...] = mm(swap[...], jnp.concatenate(halves, axis=1)).astype(BF)
                for q in range(16):
                    i = idx[m, j * KEEP + qh * 16 + q]
                    for kh in range(2):
                        tile = tiles[q * 16:q * 16 + 16, kh * 128:kh * 128 + 128]
                        if m == 2:
                            pd[kh * 16:kh * 16 + 16, pl.ds(pl.multiple_of(i * 128, 128), 128)] = tile
                        else:
                            dst = pg if m == 0 else pu
                            dst[pl.ds(pl.multiple_of(i * 32 + kh * 16, 16), 16), :] = tile


def prep(idx, gate, up, down):
    blocks = pl.BlockSpec((KEEP, D), lambda j, s: (jnp.minimum(j, COLS - 1), 0))
    panel = pl.BlockSpec((FEAT, 128), lambda j, s: (0, jnp.minimum(j, COLS - 1)))
    return pl.pallas_call(
        prep_kernel,
        grid_spec=pltpu.PrefetchScalarGridSpec(
            num_scalar_prefetch=1,
            grid=(COLS + 1,),
            in_specs=[blocks, blocks, blocks, pl.BlockSpec((256, 256), lambda j, s: (0, 0))],
            out_specs=[panel, panel, pl.BlockSpec((KEEP, 2 * D), lambda j, s: (j, 0))],
            scratch_shapes=[pltpu.VMEM((6, 256, 256), BF)],
        ),
        out_shape=[
            jax.ShapeDtypeStruct((FEAT, WIDE), BF),
            jax.ShapeDtypeStruct((FEAT, WIDE), BF),
            jax.ShapeDtypeStruct((256, 2 * D), BF),
        ],
        compiler_params=pltpu.CompilerParams(vmem_limit_bytes=40 << 20),
        cost_estimate=pl.CostEstimate(flops=3_000_000_000, bytes_accessed=17_000_000, transcendentals=0),
        name="prep",
    )(idx, gate, up, down, jnp.asarray(SWAP, BF))


def forward_kernel(t0, t1, t2, t3, pg, pu, pd, fsplit, fsplit_t, hsplit, hsplit_t,
                   xxt, gl2, ul2, hht, o0, o1, o2, o3, tok, xx, hid, hh):
    for n, piece in enumerate((t0, t1, t2, t3)):
        tok[n * 32:n * 32 + 32, :] = piece[...]
    for c in range(16):
        chunk = tok[:, c * 256:c * 256 + 256]
        split = mm(chunk, fsplit[...]).astype(BF)
        turned = mm_nt(fsplit_t[...], chunk).astype(BF)
        for p in range(2):
            xx[p * 128:p * 128 + 128, c * 128:c * 128 + 128] = split[:, p * 128:p * 128 + 128]
            xxt[c * 128:c * 128 + 128, p * 128:p * 128 + 128] = turned[p * 128:p * 128 + 128, :]
    low = low_half((TOK, 128))
    hid[:, WIDE:] = jnp.zeros((TOK, 128), BF)
    for n in range(0, WIDE, 256):
        width = min(256, WIDE - n)
        gate = mm(xx[...], pg[:, n:n + width])
        up = mm(xx[...], pu[:, n:n + width])
        for s in range(0, width, 128):
            cols = slice(n + s, n + s + 128)
            gl = jnp.where(low, gate[:TOK, s:s + 128], gate[TOK:, s:s + 128])
            gl = gl + pltpu.roll(gl, 64, 1)
            ul = jnp.where(low, up[:TOK, s:s + 128], up[TOK:, s:s + 128])
            ul = ul + pltpu.roll(ul, 64, 1)
            gl2[:, cols] = gl
            ul2[:, cols] = ul
            hid[:, cols] = (gl * (1.0 / (1.0 + jnp.exp(-gl))) * ul).astype(BF)
    for g in range(2):
        group = hid[:, g * 512:g * 512 + 512]
        split = mm(group, hsplit[...]).astype(BF)
        turned = mm_nt(hsplit_t[...], group).astype(BF)
        for p in range(2):
            hh[p * 128:p * 128 + 128, g * 128:g * 128 + 128] = split[:, p * 128:p * 128 + 128]
            hht[g * 128:g * 128 + 128, p * 128:p * 128 + 128] = turned[p * 128:p * 128 + 128, :]

    def step(n, carry):
        out = mm(hh[...], pd[:, pl.ds(pl.multiple_of(n * 1024, 1024), 1024)])
        parts = []
        for m in range(4):
            a0, a1 = out[:TOK, m * 256:m * 256 + 128], out[TOK:, m * 256:m * 256 + 128]
            b0, b1 = out[:TOK, m * 256 + 128:m * 256 + 256], out[TOK:, m * 256 + 128:m * 256 + 256]
            parts.append(jnp.where(low, a0, b1) + pltpu.roll(jnp.where(low, b0, a1), 64, 1))
        whole = jnp.concatenate(parts, axis=1).astype(BF)
        for r, dst in enumerate((o0, o1, o2, o3)):
            dst[:, pl.ds(pl.multiple_of(n * 512, 512), 512)] = whole[r * 32:r * 32 + 32, :]
        return carry

    lax.fori_loop(0, 8, step, 0)


def vm(n):
    return [pl.BlockSpec(memory_space=pltpu.VMEM)] * n


def forward(pieces, pg, pu, pd):
    piece = jax.ShapeDtypeStruct((32, D), BF)
    lin = jax.ShapeDtypeStruct((TOK, WIDE), F32)
    return pl.pallas_call(
        forward_kernel,
        in_specs=vm(11),
        out_specs=vm(8),
        out_shape=[jax.ShapeDtypeStruct((FEAT, 256), BF), lin, lin, jax.ShapeDtypeStruct((256, 256), BF)] + [piece] * 4,
        scratch_shapes=[
            pltpu.VMEM((TOK, D), BF),
            pltpu.VMEM((256, FEAT), BF),
            pltpu.VMEM((TOK, 1024), BF),
            pltpu.VMEM((256, 256), BF),
        ],
        compiler_params=pltpu.CompilerParams(vmem_limit_bytes=50 << 20),
        cost_estimate=pl.CostEstimate(flops=4_000_000_000, bytes_accessed=17_000_000, transcendentals=200_000),
        name="forward",
    )(*pieces, pg, pu, pd, jnp.asarray(FSPLIT, BF), jnp.asarray(FSPLIT.T, BF), jnp.asarray(HSPLIT, BF),
      jnp.asarray(HSPLIT.T, BF))


def emit(place, swap, tiles, swapped, own, sib, group):
    swapped[...] = mm(swap[...], tiles[...]).astype(BF)
    rows = pl.ds(pl.multiple_of(group * 16, 16), 16)
    for rel, dst in enumerate((own, sib)):
        for dx in range(NX):
            r = 2 * lax.rem(place[1] + dx, NX) + (place[0] + rel) % 2
            top = lax.rem(r, 4) * 64
            lanes = pl.ds(pl.multiple_of((r // 4) * 128, 128), 128)
            for k in range(4):
                dst[dx, rows, k * 128:k * 128 + 128] = swapped[pl.ds(pl.multiple_of(top + k * 16, 16), 16), lanes]


def down_kernel(idx, place, c0, c1, c2, c3, hht, swap, cx, own, sib, part, tiles, swapped):
    low = low_half((32, 128))
    for n, piece in enumerate((c0, c1, c2, c3)):
        for m in range(32):
            c = piece[:, m * 128:m * 128 + 128].astype(F32)
            rolled = pltpu.roll(c, 64, 1)
            zero = jnp.zeros_like(c)
            first = slice(2 * m * 128, 2 * m * 128 + 128)
            second = slice(2 * m * 128 + 128, 2 * m * 128 + 256)
            top = slice(n * 32, n * 32 + 32)
            bottom = slice(TOK + n * 32, TOK + n * 32 + 32)
            cx[top, first] = jnp.where(low, c, zero).astype(BF)
            cx[bottom, first] = jnp.where(low, zero, rolled).astype(BF)
            cx[top, second] = jnp.where(low, rolled, zero).astype(BF)
            cx[bottom, second] = jnp.where(low, zero, c).astype(BF)

    def product(n, carry):
        lanes = pl.ds(pl.multiple_of(n * 512, 512), 512)
        part[:, lanes] = mm(hht[...], cx[:, lanes]).astype(BF)
        return carry

    lax.fori_loop(0, 16, product, 0)

    def pick(group, carry):
        row = (group // 2) * 32
        for q in range(16):
            i = idx[2, group * 16 + q]
            for kh in range(2):
                tiles[q * 16:q * 16 + 16, kh * 128:kh * 128 + 128] = part[
                    pl.ds(pl.multiple_of(row + kh * 16, 16), 16), pl.ds(pl.multiple_of(i * 128, 128), 128)
                ]
        emit(place, swap, tiles, swapped, own, sib, group)
        return carry

    lax.fori_loop(0, 2 * COLS, pick, 0)


def smem(n):
    return [pl.BlockSpec(memory_space=pltpu.SMEM)] * n


WIRE = jax.ShapeDtypeStruct((NX, SLOT, 512), BF)


def down_grads(idx, place, pieces, hht):
    return pl.pallas_call(
        down_kernel,
        in_specs=smem(2) + vm(6),
        out_specs=vm(3),
        out_shape=[jax.ShapeDtypeStruct((256, 2 * D), BF), WIRE, WIRE],
        scratch_shapes=[pltpu.VMEM((256, 2 * D), BF), pltpu.VMEM((256, 256), BF), pltpu.VMEM((256, 256), BF)],
        compiler_params=pltpu.CompilerParams(vmem_limit_bytes=50 << 20),
        cost_estimate=pl.CostEstimate(flops=1_700_000_000, bytes_accessed=7_000_000, transcendentals=0),
        name="down_grads",
    )(idx, place, *pieces, hht, jnp.asarray(SWAP, BF))


def delta_kernel(cx, pd, gl2, ul2, pg, pu, hjoin, fjoin, gdx, udx, i0, i1, i2, i3):
    def product(n, acc):
        lanes = pl.ds(pl.multiple_of(n * 1024, 1024), 1024)
        return acc + mm_nt(cx[:, lanes], pd[:, lanes])

    hd = lax.fori_loop(0, 8, product, jnp.zeros((256, 256), F32))
    high = hd.astype(BF)
    rest = (hd - high.astype(F32)).astype(BF)
    low = low_half((TOK, 128))
    for g in range(2):
        cols = slice(g * 128, g * 128 + 128)
        joined = sum(
            mm(jnp.concatenate([part[:TOK, cols], part[TOK:, cols]], axis=1), hjoin[...]) for part in (high, rest)
        )
        for jl in range(4):
            j = g * 4 + jl
            if j < COLS:
                lanes = slice(j * 128, j * 128 + 128)
                delta = joined[:, jl * 128:jl * 128 + 128]
                gl, ul = gl2[:, lanes], ul2[:, lanes]
                sig = 1.0 / (1.0 + jnp.exp(-gl))
                gd = delta * ul * sig * (1.0 + gl * (1.0 - sig))
                ud = delta * gl * sig
                for dst, val in ((gdx, gd), (udx, ud)):
                    dst[:TOK, lanes] = jnp.where(low, val, 0.0).astype(BF)
                    dst[TOK:, lanes] = jnp.where(low, 0.0, val).astype(BF)

    def back(n, carry):
        rows = pl.ds(pl.multiple_of(n * 256, 256), 256)
        acc = (mm_nt(gdx[...], pg[rows, :]) + mm_nt(udx[...], pu[rows, :])).astype(BF)
        for c in range(2):
            cols = slice(c * 128, c * 128 + 128)
            pair = jnp.concatenate([acc[:TOK, cols], acc[TOK:, cols]], axis=1)
            whole = mm(pair, fjoin[...]).astype(BF)
            lanes = pl.ds(pl.multiple_of(n * 512 + c * 256, 256), 256)
            for r, dst in enumerate((i0, i1, i2, i3)):
                dst[:, lanes] = whole[r * 32:r * 32 + 32, :]
        return carry

    lax.fori_loop(0, 8, back, 0)


def deltas(cx, pd, gl2, ul2, pg, pu):
    piece = jax.ShapeDtypeStruct((32, D), BF)
    wide = jax.ShapeDtypeStruct((256, WIDE), BF)
    return pl.pallas_call(
        delta_kernel,
        in_specs=vm(8),
        out_specs=vm(6),
        out_shape=[wide, wide] + [piece] * 4,
        compiler_params=pltpu.CompilerParams(vmem_limit_bytes=50 << 20),
        cost_estimate=pl.CostEstimate(flops=3_500_000_000, bytes_accessed=18_000_000, transcendentals=200_000),
        name="deltas",
    )(cx, pd, gl2, ul2, pg, pu, jnp.asarray(HJOIN, BF), jnp.asarray(FSPLIT.T, BF))


def inward_kernel(idx, place, xxt, gdx, udx, swap, own_g, sib_g, own_u, sib_u, part, tiles, swapped):
    for m, (delta, own, sib) in enumerate(((gdx, own_g, sib_g), (udx, own_u, sib_u))):
        def product(n, carry):
            rows = pl.ds(pl.multiple_of(n * 256, 256), 256)
            part[rows, :] = mm(xxt[rows, :], delta[...]).astype(BF)
            return carry

        lax.fori_loop(0, 8, product, 0)
        for j in range(COLS):
            def pick(half, carry):
                for q in range(16):
                    i = idx[m, j * KEEP + half * 16 + q]
                    for kh in range(2):
                        tiles[q * 16:q * 16 + 16, kh * 128:kh * 128 + 128] = part[
                            pl.ds(pl.multiple_of(i * 32 + kh * 16, 16), 16), j * 128:j * 128 + 128
                        ]
                emit(place, swap, tiles, swapped, own, sib, 2 * j + half)
                return carry

            lax.fori_loop(0, 2, pick, 0)


def inward_grads(idx, place, xxt, gdx, udx):
    return pl.pallas_call(
        inward_kernel,
        in_specs=smem(2) + vm(4),
        out_specs=vm(4),
        out_shape=[WIRE] * 4,
        scratch_shapes=[pltpu.VMEM((FEAT, WIDE), BF), pltpu.VMEM((256, 256), BF), pltpu.VMEM((256, 256), BF)],
        compiler_params=pltpu.CompilerParams(vmem_limit_bytes=50 << 20),
        cost_estimate=pl.CostEstimate(flops=3_000_000_000, bytes_accessed=10_000_000, transcendentals=0),
        name="inward_grads",
    )(idx, place, xxt, gdx, udx, jnp.asarray(SWAP, BF))


def from_z(value, step):
    pairs = [(y * NZ + (z + step) % NZ, y * NZ + z) for y in range(NY) for z in range(NZ)]
    return lax.ppermute(value, "fsdp", pairs)


def from_y(value, step):
    pairs = [((y + step) % NY * NZ + z, y * NZ + z) for y in range(NY) for z in range(NZ)]
    return lax.ppermute(value, "fsdp", pairs)


def from_x(value, step):
    pairs = [((x + step) % NX * NC + c, x * NC + c) for x in range(NX) for c in range(NC)]
    return lax.ppermute(value, "dp", pairs)


def from_core(value):
    pairs = [(x * NC + 1 - c, x * NC + c) for x in range(NX) for c in range(NC)]
    return lax.ppermute(value, "dp", pairs)


def gather_z(value):
    up, down = [value], [value]
    for step in range(4):
        up.append(from_z(up[-1], 1))
        if step < 3:
            down.append(from_z(down[-1], -1))
    return up + down[:0:-1]


def reduce_grads(own, sib):
    other = from_core(sib)
    parts = [(own[d].astype(F32) + other[d].astype(F32)).astype(BF) for d in range(NX)]
    got = [from_x(parts[d], -d) for d in range(1, NX)]
    total = sum((g.astype(F32) for g in got), parts[0].astype(F32))
    return (total * (1.0 / (NX * NC))).astype(BF)


def reduce_y(pieces):
    got = [from_y(pieces[d], -d) for d in range(1, NY)]
    return sum((g.astype(F32) for g in got), pieces[0].astype(F32)).astype(BF)


def body(tokens, cotangent, gate_blocks, up_blocks, down_blocks, block_index):
    rows = tokens.shape[0]
    at = lax.axis_index("fsdp")
    here = lax.axis_index("dp")
    place = jnp.stack([here % NC, here // NC]).astype(jnp.int32)

    pg, pu, pd = prep(block_index, gate_blocks, up_blocks, down_blocks)

    ring = jnp.stack(gather_z(jnp.concatenate([tokens, cotangent], axis=0)))
    ring = jnp.roll(ring, at % NZ, axis=0)
    tok_z = ring[:, :rows].reshape(NZ * rows, D)
    cot_z = ring[:, rows:].reshape(NZ * rows, D)
    tok = [tok_z] + [from_y(tok_z, s) for s in range(1, NY)]
    cot = [cot_z] + [from_y(cot_z, s) for s in range(1, NY)]

    xxt, gl2, ul2, hht, *out_parts = forward(tok, pg, pu, pd)
    out_y = reduce_y(out_parts)
    cx, own_d, sib_d = down_grads(block_index, place, cot, hht)
    down_grad = reduce_grads(own_d, sib_d)
    gdx, udx, *in_parts = deltas(cx, pd, gl2, ul2, pg, pu)
    in_y = reduce_y(in_parts)
    own_g, sib_g, own_u, sib_u = inward_grads(block_index, place, xxt, gdx, udx)
    gate_grad = reduce_grads(own_g, sib_g)
    up_grad = reduce_grads(own_u, sib_u)

    both = jnp.concatenate([out_y.reshape(NZ, rows, D), in_y.reshape(NZ, rows, D)], axis=1)
    groups = [[y * NZ + z for z in range(NZ)] for y in range(NY)]
    got = lax.all_to_all(both, "fsdp", 0, 0, axis_index_groups=groups, tiled=True)
    total = got.astype(F32).sum(axis=0).astype(BF)
    return (total[:rows], total[rows:], gate_grad, up_grad, down_grad)


def solution(mesh):
    return jax.shard_map(
        body,
        mesh=mesh,
        in_specs=(
            P(("dp", "fsdp"), None),
            P(("dp", "fsdp"), None),
            P("fsdp", None),
            P("fsdp", None),
            P("fsdp", None),
            P(None, "fsdp"),
        ),
        out_specs=(
            P(("dp", "fsdp"), None),
            P(("dp", "fsdp"), None),
            P("fsdp", "dp"),
            P("fsdp", "dp"),
            P("fsdp", "dp"),
        ),
        check_vma=False,
    )
```

```python
import functools

import jax
import jax.numpy as jnp
import numpy as np
from jax import lax
from jax.experimental import pallas as pl
from jax.experimental.pallas import tpu as pltpu
from jax.sharding import PartitionSpec as P

D = 4096
BLK = 64
KEEP = 32
COLS = 7
SLOT = COLS * KEEP
TOK = 128
FEAT = 2048
WIDE = COLS * 128
NX, NC, NY, NZ = 4, 2, 4, 8
BF = jnp.bfloat16
F32 = jnp.float32

TILE_ROWS = [[8 * x + 4 * c + k4 for x in range(NX) for k4 in range(4)] for c in range(NC)]
ORDER = TILE_ROWS[0] + TILE_ROWS[1]


def swap_matrix():
    m = np.zeros((256, 256), np.float32)
    for a in range(16):
        for b in range(16):
            m[a * 16 + b, b * 16 + a] = 1
    return m


def feature_split():
    m = np.zeros((256, 256), np.float32)
    for i in range(4):
        for p in range(2):
            for n, k in enumerate(ORDER):
                m[i * 64 + 2 * k + p, p * 128 + i * 32 + n] = 1
    return m


def feature_turn(core):
    m = np.zeros((256, 256), np.float32)
    for rel in range(2):
        for p in range(2):
            for i in range(4):
                for n, k in enumerate(TILE_ROWS[core ^ rel]):
                    m[rel * 128 + p * 64 + i * 16 + n, i * 64 + 2 * k + p] = 1
    return m


def hidden_split():
    m = np.zeros((512, 256), np.float32)
    for j in range(4):
        for p in range(2):
            for n, k in enumerate(ORDER):
                m[j * 128 + 2 * k + p, p * 128 + j * 32 + n] = 1
    return m


def hidden_turn(core):
    m = np.zeros((256, 512), np.float32)
    for rel in range(2):
        for p in range(2):
            for j in range(4):
                for n, k in enumerate(TILE_ROWS[core ^ rel]):
                    m[rel * 128 + p * 64 + j * 16 + n, j * 128 + 2 * k + p] = 1
    return m


def hidden_join():
    m = np.zeros((256, 512), np.float32)
    for j in range(4):
        for p in range(2):
            for n, k in enumerate(ORDER):
                for h in range(2):
                    m[p * 128 + j * 32 + n, j * 128 + h * 64 + 2 * k + p] = 1
    return m


def wire_swap(x):
    m = np.zeros((256, 256), np.float32)
    for rel in range(NX):
        for k4 in range(4):
            for q in range(16):
                m[rel * 64 + k4 * 16 + q, q * 16 + (rel ^ x) * 4 + k4] = 1
    return m


SWAP = swap_matrix()
FSPLIT = feature_split()
FTURN = np.stack([feature_turn(0), feature_turn(1)])
HSPLIT = hidden_split()
HTURN = np.stack([hidden_turn(0), hidden_turn(1)])
HJOIN = hidden_join()
WSWAP = np.stack([wire_swap(x) for x in range(NX)])


def mm(a, b):
    return jnp.dot(a, b, preferred_element_type=F32)


def mm_nt(a, b):
    return lax.dot_general(a, b, (((1,), (1,)), ((), ())), preferred_element_type=F32)


def low_half(shape):
    return lax.broadcasted_iota(jnp.int32, shape, 1) < 64


def vm(n):
    return [pl.BlockSpec(memory_space=pltpu.VMEM)] * n


def smem(n):
    return [pl.BlockSpec(memory_space=pltpu.SMEM)] * n


def params(mib):
    return pltpu.CompilerParams(vmem_limit_bytes=mib << 20)


def cost(us):
    return pl.CostEstimate(flops=us * 100_000_000, bytes_accessed=us * 100_000, transcendentals=0)


def shape(*dims, dtype=BF):
    return jax.ShapeDtypeStruct(dims, dtype)


def prep_kernel(idx, g_ref, u_ref, d_ref, swap, pg, pu, pd, scr):
    j = pl.program_id(0)
    pd[...] = jnp.zeros_like(pd)

    @pl.when(j < COLS)
    def _():
        pg[...] = jnp.zeros_like(pg)
        pu[...] = jnp.zeros_like(pu)
        for m, src in enumerate((g_ref, u_ref, d_ref)):
            for qh in range(2):
                rows = slice(qh * 16, qh * 16 + 16)
                halves = [
                    jnp.concatenate([src[rows, k * 128:k * 128 + 128] for k in TILE_ROWS[c]], axis=0)
                    for c in range(2)
                ]
                tiles = scr.at[2 * m + qh]
                tiles[...] = mm(swap[...], jnp.concatenate(halves, axis=1)).astype(BF)
                for q in range(16):
                    i = idx[m, j * KEEP + qh * 16 + q]
                    for c in range(2):
                        tile = tiles[q * 16:q * 16 + 16, c * 128:c * 128 + 128]
                        if m == 2:
                            pd[c * 16:c * 16 + 16, pl.ds(pl.multiple_of(i * 128, 128), 128)] = tile
                        else:
                            dst = pg if m == 0 else pu
                            dst[pl.ds(pl.multiple_of(i * 32 + c * 16, 16), 16), :] = tile


def prep(idx, gate, up, down):
    blocks = pl.BlockSpec((KEEP, D), lambda j, s: (jnp.minimum(j, COLS - 1), 0))
    panel = pl.BlockSpec((FEAT, 128), lambda j, s: (0, jnp.minimum(j, COLS - 1)))
    return pl.pallas_call(
        prep_kernel,
        grid_spec=pltpu.PrefetchScalarGridSpec(
            num_scalar_prefetch=1,
            grid=(COLS + 1,),
            in_specs=[blocks, blocks, blocks, pl.BlockSpec((256, 256), lambda j, s: (0, 0))],
            out_specs=[panel, panel, pl.BlockSpec((KEEP, 2 * D), lambda j, s: (j, 0))],
            scratch_shapes=[pltpu.VMEM((6, 256, 256), BF)],
        ),
        out_shape=[shape(FEAT, WIDE), shape(FEAT, WIDE), shape(256, 2 * D)],
        compiler_params=params(12),
        cost_estimate=cost(2),
        name="prep",
    )(idx, gate, up, down, jnp.asarray(SWAP, BF))


def forward_kernel(t0, t1, t2, t3, pg, pu, pd, fsplit, fturn, hsplit, hturn,
                   xt_own, xt_sib, ht_own, ht_sib, gl2, ul2, o0, o1, o2, o3, tok, xx, hid, hh):
    for n, piece in enumerate((t0, t1, t2, t3)):
        tok[n * 32:n * 32 + 32, :] = piece[...]
    for c in range(16):
        chunk = tok[:, c * 256:c * 256 + 256]
        split = mm(chunk, fsplit[...]).astype(BF)
        turned = mm_nt(fturn[...], chunk).astype(BF)
        for p in range(2):
            xx[p * 128:p * 128 + 128, c * 128:c * 128 + 128] = split[:, p * 128:p * 128 + 128]
            at = p * 1024 + c * 64
            xt_own[at:at + 64, :] = turned[p * 64:p * 64 + 64, :]
            xt_sib[at:at + 64, :] = turned[128 + p * 64:128 + p * 64 + 64, :]
    low = low_half((TOK, 128))
    hid[:, WIDE:] = jnp.zeros((TOK, 128), BF)
    for n in range(0, WIDE, 256):
        width = min(256, WIDE - n)
        gate = mm(xx[...], pg[:, n:n + width])
        up = mm(xx[...], pu[:, n:n + width])
        for s in range(0, width, 128):
            cols = slice(n + s, n + s + 128)
            gl = jnp.where(low, gate[:TOK, s:s + 128], gate[TOK:, s:s + 128])
            gl = gl + pltpu.roll(gl, 64, 1)
            ul = jnp.where(low, up[:TOK, s:s + 128], up[TOK:, s:s + 128])
            ul = ul + pltpu.roll(ul, 64, 1)
            gl2[:, cols] = gl
            ul2[:, cols] = ul
            hid[:, cols] = (gl * (1.0 / (1.0 + jnp.exp(-gl))) * ul).astype(BF)
    for g in range(2):
        group = hid[:, g * 512:g * 512 + 512]
        split = mm(group, hsplit[...]).astype(BF)
        turned = mm_nt(hturn[...], group).astype(BF)
        for p in range(2):
            hh[p * 128:p * 128 + 128, g * 128:g * 128 + 128] = split[:, p * 128:p * 128 + 128]
            at = p * 128 + g * 64
            ht_own[at:at + 64, :] = turned[p * 64:p * 64 + 64, :]
            ht_sib[at:at + 64, :] = turned[128 + p * 64:128 + p * 64 + 64, :]

    def step(n, carry):
        out = mm(hh[...], pd[:, pl.ds(pl.multiple_of(n * 1024, 1024), 1024)])
        parts = []
        for m in range(4):
            a0, a1 = out[:TOK, m * 256:m * 256 + 128], out[TOK:, m * 256:m * 256 + 128]
            b0, b1 = out[:TOK, m * 256 + 128:m * 256 + 256], out[TOK:, m * 256 + 128:m * 256 + 256]
            parts.append(jnp.where(low, a0, b1) + pltpu.roll(jnp.where(low, b0, a1), 64, 1))
        whole = jnp.concatenate(parts, axis=1).astype(BF)
        for r, dst in enumerate((o0, o1, o2, o3)):
            dst[:, pl.ds(pl.multiple_of(n * 512, 512), 512)] = whole[r * 32:r * 32 + 32, :]
        return carry

    lax.fori_loop(0, 8, step, 0)


def forward(pieces, pg, pu, pd, fturn, hturn):
    lin = shape(TOK, WIDE, dtype=F32)
    return pl.pallas_call(
        forward_kernel,
        in_specs=vm(11),
        out_specs=vm(10),
        out_shape=[shape(FEAT, TOK)] * 2 + [shape(256, TOK)] * 2 + [lin, lin] + [shape(32, D)] * 4,
        scratch_shapes=[
            pltpu.VMEM((TOK, D), BF),
            pltpu.VMEM((256, FEAT), BF),
            pltpu.VMEM((TOK, 1024), BF),
            pltpu.VMEM((256, 256), BF),
        ],
        compiler_params=params(24),
        cost_estimate=cost(3),
        name="forward",
    )(*pieces, pg, pu, pd, jnp.asarray(FSPLIT, BF), fturn, jnp.asarray(HSPLIT, BF), hturn)


def emit(wswap, tiles, parts, j):
    turned = mm(wswap[...], tiles[...]).astype(BF)
    for rel, dst in enumerate(parts):
        for k in range(4):
            top = (rel * 4 + k) * 16
            for half in range(2):
                dst[j * KEEP + half * 16:j * KEEP + half * 16 + 16, k * 128:k * 128 + 128] = turned[
                    top:top + 16, half * 128:half * 128 + 128
                ]


def down_kernel(idx, c0, c1, c2, c3, d0, d1, d2, d3, ht_own, ht_oth, wswap, w0, w1, w2, w3, both, part, tiles):
    for n, piece in enumerate((c0, c1, c2, c3, d0, d1, d2, d3)):
        both[n * 32:n * 32 + 32, :] = piece[...]

    def product(n, carry):
        lanes = pl.ds(pl.multiple_of(n * 512, 512), 512)
        hidden = jnp.concatenate([ht_own[...], ht_oth[...]], axis=1)
        part[:, lanes] = mm(hidden, both[:, lanes]).astype(BF)
        return carry

    lax.fori_loop(0, 8, product, 0)
    side = lax.broadcasted_iota(jnp.int32, (16, 128), 1) // 64
    for j in range(COLS):
        for q in range(KEEP):
            i = idx[2, j * KEEP + q]
            odd = lax.rem(i, 2)
            lanes = pl.ds(pl.multiple_of((i // 2) * 128, 128), 128)
            near = part[pl.ds(pl.multiple_of(odd * 128 + j * 16, 16), 16), lanes].astype(F32)
            far = part[pl.ds(pl.multiple_of((1 - odd) * 128 + j * 16, 16), 16), lanes].astype(F32)
            tile = jnp.where(side == odd, near, pltpu.roll(far, 64, 1)).astype(BF)
            tiles[(q % 16) * 16:(q % 16) * 16 + 16, (q // 16) * 128:(q // 16) * 128 + 128] = tile
        emit(wswap, tiles, (w0, w1, w2, w3), j)


def down_grads(idx, pieces, others, ht_own, ht_oth, wswap):
    return pl.pallas_call(
        down_kernel,
        in_specs=smem(1) + vm(11),
        out_specs=vm(4),
        out_shape=[shape(SLOT, 512)] * 4,
        scratch_shapes=[pltpu.VMEM((256, D), BF), pltpu.VMEM((256, D), BF), pltpu.VMEM((256, 256), BF)],
        compiler_params=params(14),
        cost_estimate=cost(2),
        name="down_grads",
    )(idx, *pieces, *others, ht_own, ht_oth, wswap)


def delta_kernel(c0, c1, c2, c3, pd, gl2, ul2, hjoin, gd_own, ud_own, gdx, udx, cx):
    low = low_half((32, 128))
    for n, piece in enumerate((c0, c1, c2, c3)):
        top = slice(n * 32, n * 32 + 32)
        bottom = slice(TOK + n * 32, TOK + n * 32 + 32)
        for m in range(32):
            c = piece[:, m * 128:m * 128 + 128].astype(F32)
            rolled = pltpu.roll(c, 64, 1)
            zero = jnp.zeros_like(c)
            first = slice(2 * m * 128, 2 * m * 128 + 128)
            second = slice(2 * m * 128 + 128, 2 * m * 128 + 256)
            cx[top, first] = jnp.where(low, c, zero).astype(BF)
            cx[bottom, first] = jnp.where(low, zero, rolled).astype(BF)
            cx[top, second] = jnp.where(low, rolled, zero).astype(BF)
            cx[bottom, second] = jnp.where(low, zero, c).astype(BF)

    def product(n, acc):
        lanes = pl.ds(pl.multiple_of(n * 1024, 1024), 1024)
        return acc + mm_nt(cx[:, lanes], pd[:, lanes])

    hd = lax.fori_loop(0, 8, product, jnp.zeros((256, 256), F32))
    high = hd.astype(BF)
    rest = (hd - high.astype(F32)).astype(BF)
    low = low_half((TOK, 128))
    gd_own[:, 384:] = jnp.zeros((TOK, 128), BF)
    ud_own[:, 384:] = jnp.zeros((TOK, 128), BF)
    for g in range(2):
        cols = slice(g * 128, g * 128 + 128)
        joined = sum(
            mm(jnp.concatenate([part[:TOK, cols], part[TOK:, cols]], axis=1), hjoin[...]) for part in (high, rest)
        )
        before = None
        for jl in range(4):
            j = g * 4 + jl
            if j == COLS:
                break
            lanes = slice(j * 128, j * 128 + 128)
            delta = joined[:, jl * 128:jl * 128 + 128]
            gl, ul = gl2[:, lanes], ul2[:, lanes]
            sig = 1.0 / (1.0 + jnp.exp(-gl))
            gd = delta * ul * sig * (1.0 + gl * (1.0 - sig))
            ud = delta * gl * sig
            for dst, val in ((gdx, gd), (udx, ud)):
                dst[:TOK, lanes] = jnp.where(low, val, 0.0).astype(BF)
                dst[TOK:, lanes] = jnp.where(low, 0.0, val).astype(BF)
            pair = slice((j // 2) * 128, (j // 2) * 128 + 128)
            if j % 2:
                gd_own[:, pair] = jnp.where(low, before[0], gd).astype(BF)
                ud_own[:, pair] = jnp.where(low, before[1], ud).astype(BF)
            elif j == COLS - 1:
                gd_own[:, pair] = jnp.where(low, gd, 0.0).astype(BF)
                ud_own[:, pair] = jnp.where(low, ud, 0.0).astype(BF)
            before = (gd, ud)


def deltas(pieces, pd, gl2, ul2):
    return pl.pallas_call(
        delta_kernel,
        in_specs=vm(8),
        out_specs=vm(4),
        out_shape=[shape(TOK, 512)] * 2 + [shape(256, WIDE)] * 2,
        scratch_shapes=[pltpu.VMEM((256, 2 * D), BF)],
        compiler_params=params(18),
        cost_estimate=cost(2),
        name="deltas",
    )(*pieces, pd, gl2, ul2, jnp.asarray(HJOIN, BF))


def back_kernel(gdx, udx, pg, pu, fjoin, i0, i1, i2, i3):
    def back(n, carry):
        rows = pl.ds(pl.multiple_of(n * 256, 256), 256)
        acc = (mm_nt(gdx[...], pg[rows, :]) + mm_nt(udx[...], pu[rows, :])).astype(BF)
        for c in range(2):
            cols = slice(c * 128, c * 128 + 128)
            pair = jnp.concatenate([acc[:TOK, cols], acc[TOK:, cols]], axis=1)
            whole = mm(pair, fjoin[...]).astype(BF)
            lanes = pl.ds(pl.multiple_of(n * 512 + c * 256, 256), 256)
            for r, dst in enumerate((i0, i1, i2, i3)):
                dst[:, lanes] = whole[r * 32:r * 32 + 32, :]
        return carry

    lax.fori_loop(0, 8, back, 0)


def input_parts(gdx, udx, pg, pu):
    return pl.pallas_call(
        back_kernel,
        in_specs=vm(5),
        out_specs=vm(4),
        out_shape=[shape(32, D)] * 4,
        compiler_params=params(18),
        cost_estimate=cost(2),
        name="input_parts",
    )(gdx, udx, pg, pu, jnp.asarray(FSPLIT.T, BF))


def inward_kernel(m, idx, xt_own, xt_oth, d_own, d_oth, wswap, w0, w1, w2, w3, part, tiles):
    delta = jnp.concatenate([d_own[...], d_oth[...]], axis=0)

    def product(n, carry):
        rows = pl.ds(pl.multiple_of(n * 256, 256), 256)
        part[rows, :] = mm(jnp.concatenate([xt_own[rows, :], xt_oth[rows, :]], axis=1), delta).astype(BF)
        return carry

    lax.fori_loop(0, 8, product, 0)
    low = low_half((16, 128))
    for j in range(COLS):
        odd = j % 2
        lanes = slice((j // 2) * 128, (j // 2) * 128 + 128)
        for q in range(KEEP):
            i = idx[m, j * KEEP + q]
            first = part[pl.ds(pl.multiple_of(i * 16, 16), 16), lanes].astype(F32)
            second = part[pl.ds(pl.multiple_of(1024 + i * 16, 16), 16), lanes].astype(F32)
            if odd:
                first = pltpu.roll(first, 64, 1)
            else:
                second = pltpu.roll(second, 64, 1)
            tile = jnp.where(low, first, second).astype(BF)
            tiles[(q % 16) * 16:(q % 16) * 16 + 16, (q // 16) * 128:(q // 16) * 128 + 128] = tile
        emit(wswap, tiles, (w0, w1, w2, w3), j)


def inward_grads(m, idx, xt_own, xt_oth, d_own, d_oth, wswap):
    return pl.pallas_call(
        functools.partial(inward_kernel, m),
        in_specs=smem(1) + vm(5),
        out_specs=vm(4),
        out_shape=[shape(SLOT, 512)] * 4,
        scratch_shapes=[pltpu.VMEM((FEAT, 512), BF), pltpu.VMEM((256, 256), BF)],
        compiler_params=params(14),
        cost_estimate=cost(2),
        name=("gate_grads", "up_grads")[m],
    )(idx, xt_own, xt_oth, d_own, d_oth, wswap)


def from_y(value, step):
    pairs = [((y + step) % NY * NZ + z, y * NZ + z) for y in range(NY) for z in range(NZ)]
    return lax.ppermute(value, "fsdp", pairs)


def from_x(value, other):
    pairs = [((x ^ other) * NC + c, x * NC + c) for x in range(NX) for c in range(NC)]
    return lax.ppermute(value, "dp", pairs)


def from_core(value):
    pairs = [(x * NC + 1 - c, x * NC + c) for x in range(NX) for c in range(NC)]
    return lax.ppermute(value, "dp", pairs)


def over_z(value):
    groups = [[y * NZ + z for z in range(NZ)] for y in range(NY)]
    return lax.all_to_all(value, "fsdp", 0, 0, axis_index_groups=groups, tiled=True)


def total_of(first, others):
    return sum((o.astype(F32) for o in others), first.astype(F32))


def reduce_x(parts):
    total = total_of(parts[0], [from_x(parts[d], d) for d in range(1, NX)])
    return (total * (1.0 / (NX * NC))).astype(BF)


def reduce_yz(pieces):
    rows = pieces[0].shape[0] // NZ
    total = total_of(pieces[0], [from_y(pieces[d], -d) for d in range(1, NY)])
    return over_z(total.astype(BF).reshape(NZ, rows, D)).astype(F32).sum(axis=0).astype(BF)


def body(tokens, cotangent, gate_blocks, up_blocks, down_blocks, block_index):
    rows = tokens.shape[0]
    here = lax.axis_index("dp")
    core, x = here % NC, here // NC
    fturn = jnp.where(core == 0, jnp.asarray(FTURN[0], BF), jnp.asarray(FTURN[1], BF))
    hturn = jnp.where(core == 0, jnp.asarray(HTURN[0], BF), jnp.asarray(HTURN[1], BF))
    wswap = lax.dynamic_index_in_dim(jnp.asarray(WSWAP, BF), x, 0, keepdims=False)

    own = jnp.concatenate([tokens, cotangent], axis=0)
    ring = over_z(jnp.broadcast_to(own[None], (NZ,) + own.shape))
    pg, pu, pd = prep(block_index, gate_blocks, up_blocks, down_blocks)
    tok_z = ring[:, :rows].reshape(NZ * rows, D)
    cot_z = ring[:, rows:].reshape(NZ * rows, D)
    tok = [tok_z] + [from_y(tok_z, s) for s in range(1, NY)]
    cot = [cot_z] + [from_y(cot_z, s) for s in range(1, NY)]
    cot_oth = [from_core(c) for c in cot]

    xt_own, xt_sib, ht_own, ht_sib, gl2, ul2, *out_parts = forward(tok, pg, pu, pd, fturn, hturn)
    xt_oth, ht_oth = from_core(xt_sib), from_core(ht_sib)
    layer_out = reduce_yz(out_parts)
    down_grad = reduce_x(down_grads(block_index, cot, cot_oth, ht_own, ht_oth, wswap))
    gd, ud, gdx, udx = deltas(cot, pd, gl2, ul2)
    gd_oth, ud_oth = from_core(gd), from_core(ud)
    input_grad = reduce_yz(input_parts(gdx, udx, pg, pu))
    gate_grad = reduce_x(inward_grads(0, block_index, xt_own, xt_oth, gd, gd_oth, wswap))
    up_grad = reduce_x(inward_grads(1, block_index, xt_own, xt_oth, ud, ud_oth, wswap))
    return (layer_out, input_grad, gate_grad, up_grad, down_grad)


def solution(mesh):
    return jax.shard_map(
        body,
        mesh=mesh,
        in_specs=(
            P(("dp", "fsdp"), None),
            P(("dp", "fsdp"), None),
            P("fsdp", None),
            P("fsdp", None),
            P("fsdp", None),
            P(None, "fsdp"),
        ),
        out_specs=(
            P(("dp", "fsdp"), None),
            P(("dp", "fsdp"), None),
            P("fsdp", "dp"),
            P("fsdp", "dp"),
            P("fsdp", "dp"),
        ),
        check_vma=False,
    )
```

```python
import functools

import jax
import jax.numpy as jnp
from jax import lax
from jax.experimental import pallas as pl
from jax.experimental.pallas import tpu as pltpu
from jax.sharding import PartitionSpec as P

D = 4096
BLK = 64
KEEP = 32
COLS = 7
SLOT = COLS * KEEP
TOK = 128
FEAT = 2048
WIDE = COLS * 128
NX, NC, NY, NZ = 4, 2, 4, 8
BF = jnp.bfloat16
F32 = jnp.float32

TILE_ROWS = [[8 * x + 4 * c + k4 for x in range(NX) for k4 in range(4)] for c in range(NC)]


def rows_of(n):
    return lax.broadcasted_iota(jnp.int32, (n, 1), 0)


def cols_of(n):
    return lax.broadcasted_iota(jnp.int32, (1, n), 1)


def one_hot(left, right):
    return jnp.where(left == right, 1.0, 0.0).astype(BF)


def split_index(at, stride):
    k = 8 * ((at >> 2) & 3) + 4 * ((at >> 4) & 1) + (at & 3)
    return ((at >> 5) & 3) * stride + 2 * k + (at >> 7)


def turn_index(at, core, stride):
    k = 8 * ((at >> 2) & 3) + 4 * (core ^ (at >> 7)) + (at & 3)
    return ((at >> 4) & 3) * stride + 2 * k + ((at >> 6) & 1)


def swap_matrix():
    at = cols_of(256)
    return one_hot(rows_of(256), (at & 15) * 16 + (at >> 4))


def wire_swap(x):
    at = rows_of(256)
    return one_hot((at & 15) * 16 + ((at >> 6) ^ x) * 4 + ((at >> 4) & 3), cols_of(256))


def place():
    dp, fsdp = lax.axis_index("dp"), lax.axis_index("fsdp")
    return lax.rem(dp, NC), dp // NC, fsdp // NZ


def mm(a, b):
    return jnp.dot(a, b, preferred_element_type=F32)


def mm_nt(a, b):
    return lax.dot_general(a, b, (((1,), (1,)), ((), ())), preferred_element_type=F32)


def low_half(shape):
    return lax.broadcasted_iota(jnp.int32, shape, 1) < 64


def vm(n):
    return [pl.BlockSpec(memory_space=pltpu.VMEM)] * n


def smem(n):
    return [pl.BlockSpec(memory_space=pltpu.SMEM)] * n


def params(mib):
    return pltpu.CompilerParams(vmem_limit_bytes=mib << 20)


def cost(us):
    return pl.CostEstimate(flops=us * 100_000_000, bytes_accessed=us * 100_000, transcendentals=0)


def shape(*dims, dtype=BF):
    return jax.ShapeDtypeStruct(dims, dtype)


def prep_kernel(idx, g_ref, u_ref, d_ref, pg, pu, pd, scr):
    j = pl.program_id(0)
    pd[...] = jnp.zeros_like(pd)

    @pl.when(j < COLS)
    def _():
        pg[...] = jnp.zeros_like(pg)
        pu[...] = jnp.zeros_like(pu)
        swap = swap_matrix()
        for m, src in enumerate((g_ref, u_ref, d_ref)):
            for qh in range(2):
                rows = slice(qh * 16, qh * 16 + 16)
                halves = [
                    jnp.concatenate([src[rows, k * 128:k * 128 + 128] for k in TILE_ROWS[c]], axis=0)
                    for c in range(2)
                ]
                tiles = scr.at[2 * m + qh]
                tiles[...] = mm(swap, jnp.concatenate(halves, axis=1)).astype(BF)
                for q in range(16):
                    i = idx[m, j * KEEP + qh * 16 + q]
                    for c in range(2):
                        tile = tiles[q * 16:q * 16 + 16, c * 128:c * 128 + 128]
                        if m == 2:
                            pd[c * 16:c * 16 + 16, pl.ds(pl.multiple_of(i * 128, 128), 128)] = tile
                        else:
                            dst = pg if m == 0 else pu
                            dst[pl.ds(pl.multiple_of(i * 32 + c * 16, 16), 16), :] = tile


def prep(idx, gate, up, down):
    blocks = pl.BlockSpec((KEEP, D), lambda j, s: (jnp.minimum(j, COLS - 1), 0))
    panel = pl.BlockSpec((FEAT, 128), lambda j, s: (0, jnp.minimum(j, COLS - 1)))
    return pl.pallas_call(
        prep_kernel,
        grid_spec=pltpu.PrefetchScalarGridSpec(
            num_scalar_prefetch=1,
            grid=(COLS + 1,),
            in_specs=[blocks, blocks, blocks],
            out_specs=[panel, panel, pl.BlockSpec((KEEP, 2 * D), lambda j, s: (j, 0))],
            scratch_shapes=[pltpu.VMEM((6, 256, 256), BF)],
        ),
        out_shape=[pltpu.VMEM((FEAT, WIDE), BF), pltpu.VMEM((FEAT, WIDE), BF), pltpu.VMEM((256, 2 * D), BF)],
        compiler_params=params(12),
        cost_estimate=cost(2),
        name="prep",
    )(idx, *(pltpu.with_memory_space_constraint(b, pltpu.HBM) for b in (gate, up, down)))


def forward_kernel(t0, t1, t2, t3, pg, pu, pd, xt_own, xt_sib, ht_own, ht_sib, gl2, ul2, out_parts, tok, xx, hid, hh):
    core, _, y = place()
    fsplit = one_hot(rows_of(256), split_index(cols_of(256), 64))
    fturn = one_hot(turn_index(rows_of(256), core, 64), cols_of(256))
    hsplit = one_hot(rows_of(512), split_index(cols_of(256), 128))
    hturn = one_hot(turn_index(rows_of(256), core, 128), cols_of(512))
    for n, piece in enumerate((t0, t1, t2, t3)):
        tok[n * 32:n * 32 + 32, :] = piece[...]
    for c in range(16):
        chunk = tok[:, c * 256:c * 256 + 256]
        split = mm(chunk, fsplit).astype(BF)
        turned = mm_nt(fturn, chunk).astype(BF)
        for p in range(2):
            xx[p * 128:p * 128 + 128, c * 128:c * 128 + 128] = split[:, p * 128:p * 128 + 128]
            at = p * 1024 + c * 64
            xt_own[at:at + 64, :] = turned[p * 64:p * 64 + 64, :]
            xt_sib[at:at + 64, :] = turned[128 + p * 64:128 + p * 64 + 64, :]
    low = low_half((TOK, 128))
    hid[:, WIDE:] = jnp.zeros((TOK, 128), BF)
    for n in range(0, WIDE, 256):
        width = min(256, WIDE - n)
        gate = mm(xx[...], pg[:, n:n + width])
        up = mm(xx[...], pu[:, n:n + width])
        for s in range(0, width, 128):
            cols = slice(n + s, n + s + 128)
            gl = jnp.where(low, gate[:TOK, s:s + 128], gate[TOK:, s:s + 128])
            gl = gl + pltpu.roll(gl, 64, 1)
            ul = jnp.where(low, up[:TOK, s:s + 128], up[TOK:, s:s + 128])
            ul = ul + pltpu.roll(ul, 64, 1)
            gl2[:, cols] = gl
            ul2[:, cols] = ul
            hid[:, cols] = (gl * (1.0 / (1.0 + jnp.exp(-gl))) * ul).astype(BF)
    for g in range(2):
        group = hid[:, g * 512:g * 512 + 512]
        split = mm(group, hsplit).astype(BF)
        turned = mm_nt(hturn, group).astype(BF)
        for p in range(2):
            hh[p * 128:p * 128 + 128, g * 128:g * 128 + 128] = split[:, p * 128:p * 128 + 128]
            at = p * 128 + g * 64
            ht_own[at:at + 64, :] = turned[p * 64:p * 64 + 64, :]
            ht_sib[at:at + 64, :] = turned[128 + p * 64:128 + p * 64 + 64, :]

    def step(n, carry):
        out = mm(hh[...], pd[:, pl.ds(pl.multiple_of(n * 1024, 1024), 1024)])
        parts = []
        for m in range(4):
            a0, a1 = out[:TOK, m * 256:m * 256 + 128], out[TOK:, m * 256:m * 256 + 128]
            b0, b1 = out[:TOK, m * 256 + 128:m * 256 + 256], out[TOK:, m * 256 + 128:m * 256 + 256]
            parts.append(jnp.where(low, a0, b1) + pltpu.roll(jnp.where(low, b0, a1), 64, 1))
        whole = jnp.concatenate(parts, axis=1).astype(BF)
        for r in range(NY):
            out_parts[lax.rem(y + r, NY), :, pl.ds(pl.multiple_of(n * 512, 512), 512)] = whole[r * 32:r * 32 + 32, :]
        return carry

    lax.fori_loop(0, 8, step, 0)


def forward(pieces, pg, pu, pd):
    lin = pltpu.VMEM((TOK, WIDE), F32)
    return pl.pallas_call(
        forward_kernel,
        in_specs=vm(7),
        out_specs=vm(7),
        out_shape=[shape(FEAT, TOK)] * 2 + [shape(256, TOK)] * 2 + [lin, lin, shape(NY, 32, D)],
        scratch_shapes=[
            pltpu.VMEM((TOK, D), BF),
            pltpu.VMEM((256, FEAT), BF),
            pltpu.VMEM((TOK, 1024), BF),
            pltpu.VMEM((256, 256), BF),
        ],
        compiler_params=params(24),
        cost_estimate=cost(3),
        name="forward",
    )(*pieces, pg, pu, pd)


def emit(wswap, tiles, parts, j):
    turned = mm(wswap, tiles[...]).astype(BF)
    for rel, dst in enumerate(parts):
        for k in range(4):
            top = (rel * 4 + k) * 16
            for half in range(2):
                dst[j * KEEP + half * 16:j * KEEP + half * 16 + 16, k * 128:k * 128 + 128] = turned[
                    top:top + 16, half * 128:half * 128 + 128
                ]


def down_kernel(idx, c0, c1, c2, c3, d0, d1, d2, d3, ht_own, ht_oth, w0, w1, w2, w3, both, part, tiles):
    wswap = wire_swap(place()[1])
    for n, piece in enumerate((c0, c1, c2, c3, d0, d1, d2, d3)):
        both[n * 32:n * 32 + 32, :] = piece[...]

    def product(n, carry):
        lanes = pl.ds(pl.multiple_of(n * 512, 512), 512)
        hidden = jnp.concatenate([ht_own[...], ht_oth[...]], axis=1)
        part[:, lanes] = mm(hidden, both[:, lanes]).astype(BF)
        return carry

    lax.fori_loop(0, 8, product, 0)
    side = lax.broadcasted_iota(jnp.int32, (16, 128), 1) // 64
    for j in range(COLS):
        for q in range(KEEP):
            i = idx[2, j * KEEP + q]
            odd = lax.rem(i, 2)
            lanes = pl.ds(pl.multiple_of((i // 2) * 128, 128), 128)
            near = part[pl.ds(pl.multiple_of(odd * 128 + j * 16, 16), 16), lanes].astype(F32)
            far = part[pl.ds(pl.multiple_of((1 - odd) * 128 + j * 16, 16), 16), lanes].astype(F32)
            tile = jnp.where(side == odd, near, pltpu.roll(far, 64, 1)).astype(BF)
            tiles[(q % 16) * 16:(q % 16) * 16 + 16, (q // 16) * 128:(q // 16) * 128 + 128] = tile
        emit(wswap, tiles, (w0, w1, w2, w3), j)


def down_grads(idx, pieces, others, ht_own, ht_oth):
    return pl.pallas_call(
        down_kernel,
        in_specs=smem(1) + vm(10),
        out_specs=vm(4),
        out_shape=[shape(SLOT, 512)] * 4,
        scratch_shapes=[pltpu.VMEM((256, D), BF), pltpu.VMEM((256, D), BF), pltpu.VMEM((256, 256), BF)],
        compiler_params=params(14),
        cost_estimate=cost(2),
        name="down_grads",
    )(idx, *pieces, *others, ht_own, ht_oth)


def delta_kernel(c0, c1, c2, c3, pd, gl2, ul2, gd_own, ud_own, gdx, udx, cx):
    at = cols_of(512)
    hjoin = one_hot(split_index(rows_of(256), 128), (at >> 7) * 128 + (at & 63))
    low = low_half((32, 128))
    for n, piece in enumerate((c0, c1, c2, c3)):
        top = slice(n * 32, n * 32 + 32)
        bottom = slice(TOK + n * 32, TOK + n * 32 + 32)
        for m in range(32):
            c = piece[:, m * 128:m * 128 + 128].astype(F32)
            rolled = pltpu.roll(c, 64, 1)
            zero = jnp.zeros_like(c)
            first = slice(2 * m * 128, 2 * m * 128 + 128)
            second = slice(2 * m * 128 + 128, 2 * m * 128 + 256)
            cx[top, first] = jnp.where(low, c, zero).astype(BF)
            cx[bottom, first] = jnp.where(low, zero, rolled).astype(BF)
            cx[top, second] = jnp.where(low, rolled, zero).astype(BF)
            cx[bottom, second] = jnp.where(low, zero, c).astype(BF)

    def product(n, acc):
        lanes = pl.ds(pl.multiple_of(n * 1024, 1024), 1024)
        return acc + mm_nt(cx[:, lanes], pd[:, lanes])

    hd = lax.fori_loop(0, 8, product, jnp.zeros((256, 256), F32))
    high = hd.astype(BF)
    rest = (hd - high.astype(F32)).astype(BF)
    low = low_half((TOK, 128))
    gd_own[:, 384:] = jnp.zeros((TOK, 128), BF)
    ud_own[:, 384:] = jnp.zeros((TOK, 128), BF)
    for g in range(2):
        cols = slice(g * 128, g * 128 + 128)
        joined = sum(
            mm(jnp.concatenate([part[:TOK, cols], part[TOK:, cols]], axis=1), hjoin) for part in (high, rest)
        )
        before = None
        for jl in range(4):
            j = g * 4 + jl
            if j == COLS:
                break
            lanes = slice(j * 128, j * 128 + 128)
            delta = joined[:, jl * 128:jl * 128 + 128]
            gl, ul = gl2[:, lanes], ul2[:, lanes]
            sig = 1.0 / (1.0 + jnp.exp(-gl))
            gd = delta * ul * sig * (1.0 + gl * (1.0 - sig))
            ud = delta * gl * sig
            for dst, val in ((gdx, gd), (udx, ud)):
                dst[:TOK, lanes] = jnp.where(low, val, 0.0).astype(BF)
                dst[TOK:, lanes] = jnp.where(low, 0.0, val).astype(BF)
            pair = slice((j // 2) * 128, (j // 2) * 128 + 128)
            if j % 2:
                gd_own[:, pair] = jnp.where(low, before[0], gd).astype(BF)
                ud_own[:, pair] = jnp.where(low, before[1], ud).astype(BF)
            elif j == COLS - 1:
                gd_own[:, pair] = jnp.where(low, gd, 0.0).astype(BF)
                ud_own[:, pair] = jnp.where(low, ud, 0.0).astype(BF)
            before = (gd, ud)


def deltas(pieces, pd, gl2, ul2):
    return pl.pallas_call(
        delta_kernel,
        in_specs=vm(7),
        out_specs=vm(4),
        out_shape=[shape(TOK, 512)] * 2 + [pltpu.VMEM((256, WIDE), BF)] * 2,
        scratch_shapes=[pltpu.VMEM((256, 2 * D), BF)],
        compiler_params=params(18),
        cost_estimate=cost(2),
        name="deltas",
    )(*pieces, pd, gl2, ul2)


def back_kernel(gdx, udx, pg, pu, i0, i1, i2, i3):
    fjoin = one_hot(split_index(rows_of(256), 64), cols_of(256))

    def back(n, carry):
        rows = pl.ds(pl.multiple_of(n * 256, 256), 256)
        acc = (mm_nt(gdx[...], pg[rows, :]) + mm_nt(udx[...], pu[rows, :])).astype(BF)
        for c in range(2):
            cols = slice(c * 128, c * 128 + 128)
            pair = jnp.concatenate([acc[:TOK, cols], acc[TOK:, cols]], axis=1)
            whole = mm(pair, fjoin).astype(BF)
            lanes = pl.ds(pl.multiple_of(n * 512 + c * 256, 256), 256)
            for r, dst in enumerate((i0, i1, i2, i3)):
                dst[:, lanes] = whole[r * 32:r * 32 + 32, :]
        return carry

    lax.fori_loop(0, 8, back, 0)


def input_parts(gdx, udx, pg, pu):
    return pl.pallas_call(
        back_kernel,
        in_specs=vm(4),
        out_specs=vm(4),
        out_shape=[shape(32, D)] * 4,
        compiler_params=params(18),
        cost_estimate=cost(2),
        name="input_parts",
    )(gdx, udx, pg, pu)


def inward_kernel(m, idx, xt_own, xt_oth, d_own, d_oth, w0, w1, w2, w3, part, tiles):
    wswap = wire_swap(place()[1])
    delta = jnp.concatenate([d_own[...], d_oth[...]], axis=0)

    def product(n, carry):
        rows = pl.ds(pl.multiple_of(n * 256, 256), 256)
        part[rows, :] = mm(jnp.concatenate([xt_own[rows, :], xt_oth[rows, :]], axis=1), delta).astype(BF)
        return carry

    lax.fori_loop(0, 8, product, 0)
    low = low_half((16, 128))
    for j in range(COLS):
        odd = j % 2
        lanes = slice((j // 2) * 128, (j // 2) * 128 + 128)
        for q in range(KEEP):
            i = idx[m, j * KEEP + q]
            first = part[pl.ds(pl.multiple_of(i * 16, 16), 16), lanes].astype(F32)
            second = part[pl.ds(pl.multiple_of(1024 + i * 16, 16), 16), lanes].astype(F32)
            if odd:
                first = pltpu.roll(first, 64, 1)
            else:
                second = pltpu.roll(second, 64, 1)
            tile = jnp.where(low, first, second).astype(BF)
            tiles[(q % 16) * 16:(q % 16) * 16 + 16, (q // 16) * 128:(q // 16) * 128 + 128] = tile
        emit(wswap, tiles, (w0, w1, w2, w3), j)


def inward_grads(m, idx, xt_own, xt_oth, d_own, d_oth):
    return pl.pallas_call(
        functools.partial(inward_kernel, m),
        in_specs=smem(1) + vm(4),
        out_specs=vm(4),
        out_shape=[shape(SLOT, 512)] * 4,
        scratch_shapes=[pltpu.VMEM((FEAT, 512), BF), pltpu.VMEM((256, 256), BF)],
        compiler_params=params(14),
        cost_estimate=cost(2),
        name=("gate_grads", "up_grads")[m],
    )(idx, xt_own, xt_oth, d_own, d_oth)


def from_y(value, step):
    pairs = [((y + step) % NY * NZ + z, y * NZ + z) for y in range(NY) for z in range(NZ)]
    return lax.ppermute(value, "fsdp", pairs)


def from_x(value, other):
    pairs = [((x ^ other) * NC + c, x * NC + c) for x in range(NX) for c in range(NC)]
    return lax.ppermute(value, "dp", pairs)


def from_core(value):
    pairs = [(x * NC + 1 - c, x * NC + c) for x in range(NX) for c in range(NC)]
    return lax.ppermute(value, "dp", pairs)


def z_groups():
    return [[y * NZ + z for z in range(NZ)] for y in range(NY)]


def over_z(value):
    return lax.all_to_all(value, "fsdp", 0, 0, axis_index_groups=z_groups(), tiled=True)


def copies_over_z(value):
    return over_z(jnp.broadcast_to(value[None], (NZ,) + value.shape)).reshape(-1, D)


def after(value, *others):
    return lax.optimization_barrier((value,) + others)[0]


def total_of(first, others):
    return sum((o.astype(F32) for o in others), first.astype(F32))


def reduce_x(parts):
    total = total_of(parts[0], [from_x(parts[d], d) for d in range(1, NX)])
    return (total * (1.0 / (NX * NC))).astype(BF)


def reduce_yz(pieces):
    rows = pieces[0].shape[0] // NZ
    total = total_of(pieces[0], [from_y(pieces[d], -d) for d in range(1, NY)])
    return over_z(total.astype(BF).reshape(NZ, rows, D)).astype(F32).sum(axis=0).astype(BF)


def scatter_yz(parts):
    rows = parts.shape[1] // NZ
    columns = [[y * NZ + z for y in range(NY)] for z in range(NZ)]
    mine = lax.psum_scatter(parts, "fsdp", scatter_dimension=0, axis_index_groups=columns)
    mine = mine.reshape(NZ, 4 * rows, D // 4)
    return lax.psum_scatter(mine, "fsdp", scatter_dimension=0, axis_index_groups=z_groups()).reshape(rows, D)


def body(tokens, cotangent, gate_blocks, up_blocks, down_blocks, block_index):
    tok_z = copies_over_z(tokens)
    cot_z = copies_over_z(cotangent)
    tok = [tok_z] + [from_y(tok_z, s) for s in range(1, NY)]
    pg, pu, pd = prep(after(block_index, tok_z), gate_blocks, up_blocks, down_blocks)
    cot_z = after(cot_z, pd)
    cot = [cot_z] + [from_y(cot_z, s) for s in range(1, NY)]
    cot_oth = [from_core(c) for c in cot]

    xt_own, xt_sib, ht_own, ht_sib, gl2, ul2, out_parts = forward(tok, pg, pu, pd)
    xt_oth, ht_oth = from_core(xt_sib), from_core(ht_sib)
    layer_out = scatter_yz(out_parts)
    wire = down_grads(block_index, cot, cot_oth, ht_own, ht_oth)
    down_grad = reduce_x(wire)
    gd, ud, gdx, udx = deltas(cot, pd, after(gl2, wire[0]), ul2)
    gd_oth, ud_oth = from_core(gd), from_core(ud)
    in_parts = input_parts(gdx, udx, pg, pu)
    input_grad = reduce_yz(in_parts)
    wire = inward_grads(0, block_index, xt_own, xt_oth, after(gd, in_parts[0]), gd_oth)
    gate_grad = reduce_x(wire)
    wire = inward_grads(1, block_index, xt_own, xt_oth, after(ud, wire[0]), ud_oth)
    up_grad = reduce_x(wire)
    return (layer_out, input_grad, gate_grad, up_grad, down_grad)


def solution(mesh):
    return jax.shard_map(
        body,
        mesh=mesh,
        in_specs=(
            P(("dp", "fsdp"), None),
            P(("dp", "fsdp"), None),
            P("fsdp", None),
            P("fsdp", None),
            P("fsdp", None),
            P(None, "fsdp"),
        ),
        out_specs=(
            P(("dp", "fsdp"), None),
            P(("dp", "fsdp"), None),
            P("fsdp", "dp"),
            P("fsdp", "dp"),
            P("fsdp", "dp"),
        ),
        check_vma=False,
    )
```

```python
import functools

import jax
import jax.numpy as jnp
from jax import lax
from jax.experimental import pallas as pl
from jax.experimental.pallas import tpu as pltpu
from jax.sharding import PartitionSpec as P

D = 4096
BLK = 64
KEEP = 32
COLS = 7
SLOT = COLS * KEEP
TOK = 128
FEAT = 2048
WIDE = COLS * 128
NX, NC, NY, NZ = 4, 2, 4, 8
BF = jnp.bfloat16
F32 = jnp.float32

TILE_ROWS = [[8 * x + 4 * c + k4 for x in range(NX) for k4 in range(4)] for c in range(NC)]


def rows_of(n):
    return lax.broadcasted_iota(jnp.int32, (n, 1), 0)


def cols_of(n):
    return lax.broadcasted_iota(jnp.int32, (1, n), 1)


def one_hot(left, right):
    return jnp.where(left == right, 1.0, 0.0).astype(BF)


def split_index(at, stride):
    k = 8 * ((at >> 2) & 3) + 4 * ((at >> 4) & 1) + (at & 3)
    return ((at >> 5) & 3) * stride + 2 * k + (at >> 7)


def turn_index(at, core, stride):
    k = 8 * ((at >> 2) & 3) + 4 * (core ^ (at >> 7)) + (at & 3)
    return ((at >> 4) & 3) * stride + 2 * k + ((at >> 6) & 1)


def swap_matrix():
    at = cols_of(256)
    return one_hot(rows_of(256), (at & 15) * 16 + (at >> 4))


def wire_swap(x):
    at = rows_of(256)
    return one_hot((at & 15) * 16 + ((at >> 6) ^ x) * 4 + ((at >> 4) & 3), cols_of(256))


def place():
    dp, fsdp = lax.axis_index("dp"), lax.axis_index("fsdp")
    return lax.rem(dp, NC), dp // NC, fsdp // NZ


def mm(a, b):
    return jnp.dot(a, b, preferred_element_type=F32)


def mm_nt(a, b):
    return lax.dot_general(a, b, (((1,), (1,)), ((), ())), preferred_element_type=F32)


def low_half(shape):
    return lax.broadcasted_iota(jnp.int32, shape, 1) < 64


def vm(n):
    return [pl.BlockSpec(memory_space=pltpu.VMEM)] * n


def smem(n):
    return [pl.BlockSpec(memory_space=pltpu.SMEM)] * n


def params(mib):
    return pltpu.CompilerParams(vmem_limit_bytes=mib << 20)


def cost(us):
    return pl.CostEstimate(flops=int(us * 1_000_000_000), bytes_accessed=1000, transcendentals=0)


def shape(*dims, dtype=BF):
    return jax.ShapeDtypeStruct(dims, dtype)


def unfold(src, qh, swap):
    rows = slice(qh * 16, qh * 16 + 16)
    halves = [jnp.concatenate([src[rows, k * 128:k * 128 + 128] for k in TILE_ROWS[c]], axis=0) for c in range(2)]
    return mm(swap, jnp.concatenate(halves, axis=1)).astype(BF)


def inward_panels_kernel(idx, g_ref, u_ref, pg, pu, scr):
    j = pl.program_id(0)
    pg[...] = jnp.zeros_like(pg)
    pu[...] = jnp.zeros_like(pu)
    swap = swap_matrix()
    for m, (src, dst) in enumerate(((g_ref, pg), (u_ref, pu))):
        for qh in range(2):
            tiles = scr.at[2 * m + qh]
            tiles[...] = unfold(src, qh, swap)
            for q in range(16):
                i = idx[m, j * KEEP + qh * 16 + q]
                for c in range(2):
                    dst[pl.ds(pl.multiple_of(i * 32 + c * 16, 16), 16), :] = tiles[
                        q * 16:q * 16 + 16, c * 128:c * 128 + 128
                    ]


def outward_panel_kernel(idx, d_ref, pd, scr):
    j = pl.program_id(0)
    pd[...] = jnp.zeros_like(pd)

    @pl.when(j < COLS)
    def _():
        swap = swap_matrix()
        for qh in range(2):
            tiles = scr.at[qh]
            tiles[...] = unfold(d_ref, qh, swap)
            for q in range(16):
                i = idx[2, j * KEEP + qh * 16 + q]
                for c in range(2):
                    pd[c * 16:c * 16 + 16, pl.ds(pl.multiple_of(i * 128, 128), 128)] = tiles[
                        q * 16:q * 16 + 16, c * 128:c * 128 + 128
                    ]


def hbm(value):
    return pltpu.with_memory_space_constraint(value, pltpu.HBM)


def inward_panels(idx, gate, up):
    blocks = pl.BlockSpec((KEEP, D), lambda j, s: (j, 0))
    panel = pl.BlockSpec((FEAT, 128), lambda j, s: (0, j))
    return pl.pallas_call(
        inward_panels_kernel,
        grid_spec=pltpu.PrefetchScalarGridSpec(
            num_scalar_prefetch=1,
            grid=(COLS,),
            in_specs=[blocks, blocks],
            out_specs=[panel, panel],
            scratch_shapes=[pltpu.VMEM((4, 256, 256), BF)],
        ),
        out_shape=[pltpu.VMEM((FEAT, WIDE), BF), pltpu.VMEM((FEAT, WIDE), BF)],
        compiler_params=params(10),
        cost_estimate=cost(6),
        name="inward_panels",
    )(idx, hbm(gate), hbm(up))


def outward_panel(idx, down):
    return pl.pallas_call(
        outward_panel_kernel,
        grid_spec=pltpu.PrefetchScalarGridSpec(
            num_scalar_prefetch=1,
            grid=(COLS + 1,),
            in_specs=[pl.BlockSpec((KEEP, D), lambda j, s: (jnp.minimum(j, COLS - 1), 0))],
            out_specs=pl.BlockSpec((KEEP, 2 * D), lambda j, s: (j, 0)),
            scratch_shapes=[pltpu.VMEM((2, 256, 256), BF)],
        ),
        out_shape=pltpu.VMEM((256, 2 * D), BF),
        compiler_params=params(10),
        cost_estimate=cost(3),
        name="outward_panel",
    )(idx, hbm(down))


def forward_kernel(t0, t1, t2, t3, pg, pu, pd, xt_own, ht_own, sib, gl2, ul2, out_parts, tok, xx, hid, hh):
    core, _, y = place()
    fsplit = one_hot(rows_of(256), split_index(cols_of(256), 64))
    fturn = one_hot(turn_index(rows_of(256), core, 64), cols_of(256))
    hsplit = one_hot(rows_of(512), split_index(cols_of(256), 128))
    hturn = one_hot(turn_index(rows_of(256), core, 128), cols_of(512))
    for n, piece in enumerate((t0, t1, t2, t3)):
        tok[n * 32:n * 32 + 32, :] = piece[...]
    for c in range(16):
        chunk = tok[:, c * 256:c * 256 + 256]
        split = mm(chunk, fsplit).astype(BF)
        turned = mm_nt(fturn, chunk).astype(BF)
        for p in range(2):
            xx[p * 128:p * 128 + 128, c * 128:c * 128 + 128] = split[:, p * 128:p * 128 + 128]
            at = p * 1024 + c * 64
            xt_own[at:at + 64, :] = turned[p * 64:p * 64 + 64, :]
            sib[at:at + 64, :] = turned[128 + p * 64:128 + p * 64 + 64, :]
    low = low_half((TOK, 128))
    hid[:, WIDE:] = jnp.zeros((TOK, 128), BF)
    for n in range(0, WIDE, 256):
        width = min(256, WIDE - n)
        gate = mm(xx[...], pg[:, n:n + width])
        up = mm(xx[...], pu[:, n:n + width])
        for s in range(0, width, 128):
            cols = slice(n + s, n + s + 128)
            gl = jnp.where(low, gate[:TOK, s:s + 128], gate[TOK:, s:s + 128])
            gl = gl + pltpu.roll(gl, 64, 1)
            ul = jnp.where(low, up[:TOK, s:s + 128], up[TOK:, s:s + 128])
            ul = ul + pltpu.roll(ul, 64, 1)
            gl2[:, cols] = gl
            ul2[:, cols] = ul
            hid[:, cols] = (gl * (1.0 / (1.0 + jnp.exp(-gl))) * ul).astype(BF)
    for g in range(2):
        group = hid[:, g * 512:g * 512 + 512]
        split = mm(group, hsplit).astype(BF)
        turned = mm_nt(hturn, group).astype(BF)
        for p in range(2):
            hh[p * 128:p * 128 + 128, g * 128:g * 128 + 128] = split[:, p * 128:p * 128 + 128]
            at = p * 128 + g * 64
            ht_own[at:at + 64, :] = turned[p * 64:p * 64 + 64, :]
            sib[FEAT + at:FEAT + at + 64, :] = turned[128 + p * 64:128 + p * 64 + 64, :]

    def step(n, carry):
        out = mm(hh[...], pd[:, pl.ds(pl.multiple_of(n * 1024, 1024), 1024)])
        parts = []
        for m in range(4):
            a0, a1 = out[:TOK, m * 256:m * 256 + 128], out[TOK:, m * 256:m * 256 + 128]
            b0, b1 = out[:TOK, m * 256 + 128:m * 256 + 256], out[TOK:, m * 256 + 128:m * 256 + 256]
            parts.append(jnp.where(low, a0, b1) + pltpu.roll(jnp.where(low, b0, a1), 64, 1))
        whole = jnp.concatenate(parts, axis=1).astype(BF)
        for r in range(NY):
            out_parts[lax.rem(y + r, NY), :, pl.ds(pl.multiple_of(n * 512, 512), 512)] = whole[r * 32:r * 32 + 32, :]
        return carry

    lax.fori_loop(0, 8, step, 0)


def forward(pieces, pg, pu, pd):
    lin = pltpu.VMEM((TOK, WIDE), F32)
    return pl.pallas_call(
        forward_kernel,
        in_specs=vm(7),
        out_specs=vm(6),
        out_shape=[
            shape(FEAT, TOK), shape(256, TOK), shape(FEAT + 256, TOK), lin, lin, shape(NY, 32, D)
        ],
        scratch_shapes=[
            pltpu.VMEM((TOK, D), BF),
            pltpu.VMEM((256, FEAT), BF),
            pltpu.VMEM((TOK, 1024), BF),
            pltpu.VMEM((256, 256), BF),
        ],
        compiler_params=params(24),
        cost_estimate=cost(8),
        name="forward",
    )(*pieces, pg, pu, pd)


def emit(wswap, tiles, parts, row):
    turned = mm(wswap, tiles[...]).astype(BF)
    for rel, dst in enumerate(parts):
        for k in range(4):
            top = (rel * 4 + k) * 16
            for half in range(2):
                dst[row + half * 16:row + half * 16 + 16, k * 128:k * 128 + 128] = turned[
                    top:top + 16, half * 128:half * 128 + 128
                ]


def down_kernel(idx, cot_own, cot_oth, ht_own, sib_oth, w0, w1, w2, w3, both, part, tiles):
    wswap = wire_swap(place()[1])
    both[:TOK, :] = cot_own[...]
    both[TOK:, :] = cot_oth[...]

    def product(n, carry):
        lanes = pl.ds(pl.multiple_of(n * 512, 512), 512)
        hidden = jnp.concatenate([ht_own[...], sib_oth[FEAT:, :]], axis=1)
        part[:, lanes] = mm(hidden, both[:, lanes]).astype(BF)
        return carry

    lax.fori_loop(0, 8, product, 0)
    side = lax.broadcasted_iota(jnp.int32, (16, 128), 1) // 64
    for j in range(COLS):
        for q in range(KEEP):
            i = idx[2, j * KEEP + q]
            odd = lax.rem(i, 2)
            lanes = pl.ds(pl.multiple_of((i // 2) * 128, 128), 128)
            near = part[pl.ds(pl.multiple_of(odd * 128 + j * 16, 16), 16), lanes].astype(F32)
            far = part[pl.ds(pl.multiple_of((1 - odd) * 128 + j * 16, 16), 16), lanes].astype(F32)
            tile = jnp.where(side == odd, near, pltpu.roll(far, 64, 1)).astype(BF)
            tiles[(q % 16) * 16:(q % 16) * 16 + 16, (q // 16) * 128:(q // 16) * 128 + 128] = tile
        emit(wswap, tiles, (w0, w1, w2, w3), j * KEEP)


def down_grads(idx, cot_own, cot_oth, ht_own, sib_oth):
    return pl.pallas_call(
        down_kernel,
        in_specs=smem(1) + vm(4),
        out_specs=vm(4),
        out_shape=[shape(SLOT, 512)] * 4,
        scratch_shapes=[pltpu.VMEM((256, D), BF), pltpu.VMEM((256, D), BF), pltpu.VMEM((256, 256), BF)],
        compiler_params=params(14),
        cost_estimate=cost(0.2),
        name="down_grads",
    )(idx, cot_own, cot_oth, ht_own, sib_oth)


def delta_kernel(c0, c1, c2, c3, pd_far, gl2, ul2, own, cot, gdx, udx, cx, pd, sem):
    fetch = pltpu.make_async_copy(pd_far, pd, sem)
    fetch.start()
    at = cols_of(512)
    hjoin = one_hot(split_index(rows_of(256), 128), (at >> 7) * 128 + (at & 63))
    low = low_half((32, 128))
    for n, piece in enumerate((c0, c1, c2, c3)):
        top = slice(n * 32, n * 32 + 32)
        bottom = slice(TOK + n * 32, TOK + n * 32 + 32)
        cot[top, :] = piece[...]
        for m in range(32):
            c = piece[:, m * 128:m * 128 + 128].astype(F32)
            rolled = pltpu.roll(c, 64, 1)
            zero = jnp.zeros_like(c)
            first = slice(2 * m * 128, 2 * m * 128 + 128)
            second = slice(2 * m * 128 + 128, 2 * m * 128 + 256)
            cx[top, first] = jnp.where(low, c, zero).astype(BF)
            cx[bottom, first] = jnp.where(low, zero, rolled).astype(BF)
            cx[top, second] = jnp.where(low, rolled, zero).astype(BF)
            cx[bottom, second] = jnp.where(low, zero, c).astype(BF)

    fetch.wait()

    def product(n, acc):
        lanes = pl.ds(pl.multiple_of(n * 1024, 1024), 1024)
        return acc + mm_nt(cx[:, lanes], pd[:, lanes])

    hd = lax.fori_loop(0, 8, product, jnp.zeros((256, 256), F32))
    high = hd.astype(BF)
    rest = (hd - high.astype(F32)).astype(BF)
    low = low_half((TOK, 128))
    for g in range(2):
        cols = slice(g * 128, g * 128 + 128)
        joined = sum(
            mm(jnp.concatenate([part[:TOK, cols], part[TOK:, cols]], axis=1), hjoin) for part in (high, rest)
        )
        before = None
        for jl in range(4):
            j = g * 4 + jl
            if j == COLS:
                break
            lanes = slice(j * 128, j * 128 + 128)
            delta = joined[:, jl * 128:jl * 128 + 128]
            gl, ul = gl2[:, lanes], ul2[:, lanes]
            sig = 1.0 / (1.0 + jnp.exp(-gl))
            gd = delta * ul * sig * (1.0 + gl * (1.0 - sig))
            ud = delta * gl * sig
            for dst, val in ((gdx, gd), (udx, ud)):
                dst[:TOK, lanes] = jnp.where(low, val, 0.0).astype(BF)
                dst[TOK:, lanes] = jnp.where(low, 0.0, val).astype(BF)
            pair = slice((j // 2) * 128, (j // 2) * 128 + 128)
            if j % 2:
                own[:TOK, pair] = jnp.where(low, before[0], gd).astype(BF)
                own[TOK:, pair] = jnp.where(low, before[1], ud).astype(BF)
            elif j == COLS - 1:
                own[:TOK, pair] = jnp.where(low, gd, 0.0).astype(BF)
                own[TOK:, pair] = jnp.where(low, ud, 0.0).astype(BF)
            before = (gd, ud)


def deltas(pieces, pd, gl2, ul2):
    return pl.pallas_call(
        delta_kernel,
        in_specs=vm(4) + [pl.BlockSpec(memory_space=pl.ANY)] + vm(2),
        out_specs=vm(4),
        out_shape=[shape(256, 512), shape(TOK, D)] + [pltpu.VMEM((256, WIDE), BF)] * 2,
        scratch_shapes=[
            pltpu.VMEM((256, 2 * D), BF),
            pltpu.VMEM((256, 2 * D), BF),
            pltpu.SemaphoreType.DMA,
        ],
        compiler_params=params(18),
        cost_estimate=cost(0.2),
        name="deltas",
    )(*pieces, hbm(pd), gl2, ul2)


def back_kernel(gdx, udx, pg, pu, parts):
    y = place()[2]
    fjoin = one_hot(split_index(rows_of(256), 64), cols_of(256))
    n = pl.program_id(0)
    acc = (mm_nt(gdx[...], pg[...]) + mm_nt(udx[...], pu[...])).astype(BF)
    for c in range(2):
        cols = slice(c * 128, c * 128 + 128)
        pair = jnp.concatenate([acc[:TOK, cols], acc[TOK:, cols]], axis=1)
        whole = mm(pair, fjoin).astype(BF)
        lanes = pl.ds(pl.multiple_of(n * 512 + c * 256, 256), 256)
        for r in range(NY):
            parts[lax.rem(y + r, NY), :, lanes] = whole[r * 32:r * 32 + 32, :]


def input_parts(gdx, udx, pg, pu):
    whole = pl.BlockSpec((256, WIDE), lambda n: (0, 0))
    panel = pl.BlockSpec((256, WIDE), lambda n: (n, 0))
    return pl.pallas_call(
        back_kernel,
        grid=(FEAT // 256,),
        in_specs=[whole, whole, panel, panel],
        out_specs=pl.BlockSpec((NY, 32, D), lambda n: (0, 0, 0)),
        out_shape=shape(NY, 32, D),
        compiler_params=params(10),
        cost_estimate=cost(0.2),
        name="input_parts",
    )(gdx, udx, hbm(pg), hbm(pu))


def inward_kernel(m, idx, xt_own, sib_oth, d_own, d_oth, w0, w1, w2, w3, part, tiles):
    wswap = wire_swap(place()[1])
    low = low_half((16, 128))
    delta = jnp.concatenate([d[m * TOK:m * TOK + TOK, :] for d in (d_own, d_oth)], axis=0)

    def product(n, carry):
        rows = pl.ds(pl.multiple_of(n * 256, 256), 256)
        tokens = jnp.concatenate([xt_own[rows, :], sib_oth[rows, :]], axis=1)
        part[rows, :] = mm(tokens, delta).astype(BF)
        return carry

    lax.fori_loop(0, 8, product, 0)
    for j in range(COLS):
        odd = j % 2
        lanes = slice((j // 2) * 128, (j // 2) * 128 + 128)
        for q in range(KEEP):
            i = idx[m, j * KEEP + q]
            first = part[pl.ds(pl.multiple_of(i * 16, 16), 16), lanes].astype(F32)
            second = part[pl.ds(pl.multiple_of(1024 + i * 16, 16), 16), lanes].astype(F32)
            if odd:
                first = pltpu.roll(first, 64, 1)
            else:
                second = pltpu.roll(second, 64, 1)
            tile = jnp.where(low, first, second).astype(BF)
            tiles[(q % 16) * 16:(q % 16) * 16 + 16, (q // 16) * 128:(q // 16) * 128 + 128] = tile
        emit(wswap, tiles, (w0, w1, w2, w3), j * KEEP)


def inward_grads(m, idx, xt_own, sib_oth, d_own, d_oth):
    return pl.pallas_call(
        functools.partial(inward_kernel, m),
        in_specs=smem(1) + vm(4),
        out_specs=vm(4),
        out_shape=[shape(SLOT, 512)] * 4,
        scratch_shapes=[pltpu.VMEM((FEAT, 512), BF), pltpu.VMEM((256, 256), BF)],
        compiler_params=params(14),
        cost_estimate=cost(0.2),
        name=("gate_grads", "up_grads")[m],
    )(idx, xt_own, sib_oth, d_own, d_oth)


def from_y(value, step):
    pairs = [((y + step) % NY * NZ + z, y * NZ + z) for y in range(NY) for z in range(NZ)]
    return lax.ppermute(value, "fsdp", pairs)


def from_x(value, other):
    pairs = [((x ^ other) * NC + c, x * NC + c) for x in range(NX) for c in range(NC)]
    return lax.ppermute(value, "dp", pairs)


def from_core(value):
    pairs = [(x * NC + 1 - c, x * NC + c) for x in range(NX) for c in range(NC)]
    return lax.ppermute(value, "dp", pairs)


def z_groups():
    return [[y * NZ + z for z in range(NZ)] for y in range(NY)]


def y_groups():
    return [[y * NZ + z for y in range(NY)] for z in range(NZ)]


def over_z(value):
    return lax.all_to_all(value, "fsdp", 0, 0, axis_index_groups=z_groups(), tiled=True)


def over_y(value):
    return lax.all_to_all(value, "fsdp", 0, 0, axis_index_groups=y_groups(), tiled=True)


def copies_over_z(value):
    return over_z(jnp.broadcast_to(value[None], (NZ,) + value.shape))


def after(value, *others):
    return lax.optimization_barrier((value,) + others)[0]


def exchange_x(parts):
    return [parts[0]] + [from_x(parts[d], d) for d in range(1, NX)]


def mean_of(parts):
    total = sum((p.astype(F32) for p in parts[1:]), parts[0].astype(F32))
    return (total * (1.0 / (NX * NC))).astype(BF)


def body(tokens, cotangent, gate_blocks, up_blocks, down_blocks, block_index):
    rows = tokens.shape[0]
    ring = copies_over_z(jnp.concatenate([tokens, cotangent], axis=0))
    tok_z = ring[:, :rows].reshape(NZ * rows, D)
    cot_z = ring[:, rows:].reshape(NZ * rows, D)
    tok = [tok_z] + [from_y(tok_z, s) for s in range(1, NY)]
    idx = after(block_index, tok_z)
    pg, pu = inward_panels(idx, gate_blocks, up_blocks)
    cot_z = after(cot_z, pg)
    pd = outward_panel(idx, down_blocks)
    cot = [cot_z] + [from_y(cot_z, s) for s in range(1, NY)]

    xt_own, ht_own, sib, gl2, ul2, out_parts = forward(tok, pg, pu, pd)
    sib_oth = from_core(sib)
    out_y = lax.psum_scatter(
        after(out_parts, *cot), "fsdp", scatter_dimension=0, axis_index_groups=y_groups()
    )
    own, cot_own, gdx, udx = deltas(cot, pd, gl2, ul2)
    oth, cot_oth = from_core(own), from_core(cot_own)
    gate_wire = inward_grads(0, block_index, xt_own, sib_oth, own, oth)
    gate_got = exchange_x(gate_wire)
    in_parts = input_parts(after(gdx, gate_wire[0]), udx, pg, pu)
    in_got = over_y(in_parts)
    down_wire = down_grads(block_index, cot_own, cot_oth, after(ht_own, in_parts), sib_oth)
    down_got = exchange_x(down_wire)
    up_wire = inward_grads(1, block_index, xt_own, sib_oth, after(own, down_wire[0], *gate_got[1:]), oth)
    up_got = exchange_x(up_wire)
    in_y = after(in_got, up_wire[0], *down_got[1:]).astype(F32).sum(axis=0).astype(BF)
    gate_grad, up_grad, down_grad = (mean_of(g) for g in (gate_got, up_got, down_got))

    both = jnp.concatenate([part.reshape(NZ, rows, D) for part in (out_y, in_y)], axis=1)
    total = over_z(both).astype(F32).sum(axis=0).astype(BF)
    return (total[:rows], total[rows:], gate_grad, up_grad, down_grad)


def solution(mesh):
    return jax.shard_map(
        body,
        mesh=mesh,
        in_specs=(
            P(("dp", "fsdp"), None),
            P(("dp", "fsdp"), None),
            P("fsdp", None),
            P("fsdp", None),
            P("fsdp", None),
            P(None, "fsdp"),
        ),
        out_specs=(
            P(("dp", "fsdp"), None),
            P(("dp", "fsdp"), None),
            P("fsdp", "dp"),
            P("fsdp", "dp"),
            P("fsdp", "dp"),
        ),
        check_vma=False,
    )
```

```python
import functools

import jax
import jax.numpy as jnp
from jax import lax
from jax.experimental import pallas as pl
from jax.experimental.pallas import tpu as pltpu
from jax.sharding import PartitionSpec as P

D = 4096
BLK = 64
KEEP = 32
COLS = 7
SLOT = COLS * KEEP
TOK = 128
FEAT = 2048
WIDE = COLS * 128
NX, NC, NY, NZ = 4, 2, 4, 8
BF = jnp.bfloat16
F32 = jnp.float32

TILE_ROWS = [[8 * x + 4 * c + k4 for x in range(NX) for k4 in range(4)] for c in range(NC)]


def rows_of(n):
    return lax.broadcasted_iota(jnp.int32, (n, 1), 0)


def cols_of(n):
    return lax.broadcasted_iota(jnp.int32, (1, n), 1)


def one_hot(left, right):
    return jnp.where(left == right, 1.0, 0.0).astype(BF)


def split_index(at, stride):
    k = 8 * ((at >> 2) & 3) + 4 * ((at >> 4) & 1) + (at & 3)
    return ((at >> 5) & 3) * stride + 2 * k + (at >> 7)


def turn_index(at, core, stride):
    k = 8 * ((at >> 2) & 3) + 4 * (core ^ (at >> 7)) + (at & 3)
    return ((at >> 4) & 3) * stride + 2 * k + ((at >> 6) & 1)


def swap_matrix():
    at = cols_of(256)
    return one_hot(rows_of(256), (at & 15) * 16 + (at >> 4))


def wire_swap(x):
    at = rows_of(256)
    return one_hot((at & 15) * 16 + ((at >> 6) ^ x) * 4 + ((at >> 4) & 3), cols_of(256))


def place():
    dp, fsdp = lax.axis_index("dp"), lax.axis_index("fsdp")
    return lax.rem(dp, NC), dp // NC, fsdp // NZ


def mm(a, b):
    return jnp.dot(a, b, preferred_element_type=F32)


def mm_nt(a, b):
    return lax.dot_general(a, b, (((1,), (1,)), ((), ())), preferred_element_type=F32)


def low_half(shape):
    return lax.broadcasted_iota(jnp.int32, shape, 1) < 64


def vm(n):
    return [pl.BlockSpec(memory_space=pltpu.VMEM)] * n


def smem(n):
    return [pl.BlockSpec(memory_space=pltpu.SMEM)] * n


def params(mib):
    return pltpu.CompilerParams(vmem_limit_bytes=mib << 20)


def cost(us):
    return pl.CostEstimate(flops=int(us * 1_000_000_000), bytes_accessed=1000, transcendentals=0)


def shape(*dims, dtype=BF):
    return jax.ShapeDtypeStruct(dims, dtype)


def unfold(src, row, swap):
    rows = pl.ds(pl.multiple_of(row, 16), 16)
    halves = [jnp.concatenate([src[rows, k * 128:k * 128 + 128] for k in TILE_ROWS[c]], axis=0) for c in range(2)]
    return mm(swap, jnp.concatenate(halves, axis=1)).astype(BF)


def inward_panels_kernel(idx, gate, up, pg, pu, held, tiles, sems):
    fetches = [pltpu.make_async_copy(src, held.at[m], sems.at[m]) for m, src in enumerate((gate, up))]
    for fetch in fetches:
        fetch.start()
    swap = swap_matrix()
    for m, dst in enumerate((pg, pu)):
        dst[...] = jnp.zeros_like(dst)
        fetches[m].wait()

        def column(j, carry):
            lanes = pl.ds(pl.multiple_of(j * 128, 128), 128)
            for half in range(2):
                tiles[half, :, :] = unfold(held.at[m], j * KEEP + half * 16, swap)
                for q in range(16):
                    i = idx[m, j * KEEP + half * 16 + q]
                    for c in range(2):
                        dst[pl.ds(pl.multiple_of(i * 32 + c * 16, 16), 16), lanes] = tiles[
                            half, q * 16:q * 16 + 16, c * 128:c * 128 + 128
                        ]
            return carry

        lax.fori_loop(0, COLS, column, 0)


def outward_panel_kernel(idx, down, pd, held, tiles, sem):
    fetch = pltpu.make_async_copy(down, held, sem)
    fetch.start()
    swap = swap_matrix()
    pd[...] = jnp.zeros_like(pd)
    fetch.wait()

    def column(j, carry):
        for half in range(2):
            tiles[half, :, :] = unfold(held, j * KEEP + half * 16, swap)
            for q in range(16):
                i = idx[2, j * KEEP + half * 16 + q]
                for c in range(2):
                    rows = pl.ds(pl.multiple_of(j * 32 + c * 16, 16), 16)
                    pd[rows, pl.ds(pl.multiple_of(i * 128, 128), 128)] = tiles[
                        half, q * 16:q * 16 + 16, c * 128:c * 128 + 128
                    ]
        return carry

    lax.fori_loop(0, COLS, column, 0)


def hbm(value):
    return pltpu.with_memory_space_constraint(value, pltpu.HBM)


def far(n):
    return [pl.BlockSpec(memory_space=pl.ANY)] * n


def inward_panels(idx, gate, up):
    return pl.pallas_call(
        inward_panels_kernel,
        in_specs=smem(1) + far(2),
        out_specs=vm(2),
        out_shape=[pltpu.VMEM((FEAT, WIDE), BF), pltpu.VMEM((FEAT, WIDE), BF)],
        scratch_shapes=[
            pltpu.VMEM((2, SLOT, D), BF),
            pltpu.VMEM((2, 256, 256), BF),
            pltpu.SemaphoreType.DMA((2,)),
        ],
        compiler_params=params(14),
        cost_estimate=cost(6),
        name="inward_panels",
    )(idx, hbm(gate), hbm(up))


def outward_panel(idx, down):
    return pl.pallas_call(
        outward_panel_kernel,
        in_specs=smem(1) + far(1),
        out_specs=vm(1)[0],
        out_shape=pltpu.VMEM((256, 2 * D), BF),
        scratch_shapes=[pltpu.VMEM((SLOT, D), BF), pltpu.VMEM((2, 256, 256), BF), pltpu.SemaphoreType.DMA],
        compiler_params=params(10),
        cost_estimate=cost(3),
        name="outward_panel",
    )(idx, hbm(down))


def forward_kernel(t0, t1, t2, t3, pg, pu, pd, xt_own, ht_own, sib, gl2, ul2, out_parts, tok, xx, hid, hh):
    core, _, y = place()
    fsplit = one_hot(rows_of(256), split_index(cols_of(256), 64))
    fturn = one_hot(turn_index(rows_of(256), core, 64), cols_of(256))
    hsplit = one_hot(rows_of(512), split_index(cols_of(256), 128))
    hturn = one_hot(turn_index(rows_of(256), core, 128), cols_of(512))
    for n, piece in enumerate((t0, t1, t2, t3)):
        tok[n * 32:n * 32 + 32, :] = piece[...]
    for c in range(16):
        chunk = tok[:, c * 256:c * 256 + 256]
        split = mm(chunk, fsplit).astype(BF)
        turned = mm_nt(fturn, chunk).astype(BF)
        for p in range(2):
            xx[p * 128:p * 128 + 128, c * 128:c * 128 + 128] = split[:, p * 128:p * 128 + 128]
            at = p * 1024 + c * 64
            xt_own[at:at + 64, :] = turned[p * 64:p * 64 + 64, :]
            sib[at:at + 64, :] = turned[128 + p * 64:128 + p * 64 + 64, :]
    low = low_half((TOK, 128))
    hid[:, WIDE:] = jnp.zeros((TOK, 128), BF)
    for n in range(0, WIDE, 256):
        width = min(256, WIDE - n)
        gate = mm(xx[...], pg[:, n:n + width])
        up = mm(xx[...], pu[:, n:n + width])
        for s in range(0, width, 128):
            cols = slice(n + s, n + s + 128)
            gl = jnp.where(low, gate[:TOK, s:s + 128], gate[TOK:, s:s + 128])
            gl = gl + pltpu.roll(gl, 64, 1)
            ul = jnp.where(low, up[:TOK, s:s + 128], up[TOK:, s:s + 128])
            ul = ul + pltpu.roll(ul, 64, 1)
            gl2[:, cols] = gl
            ul2[:, cols] = ul
            hid[:, cols] = (gl * (1.0 / (1.0 + jnp.exp(-gl))) * ul).astype(BF)
    for g in range(2):
        group = hid[:, g * 512:g * 512 + 512]
        split = mm(group, hsplit).astype(BF)
        turned = mm_nt(hturn, group).astype(BF)
        for p in range(2):
            hh[p * 128:p * 128 + 128, g * 128:g * 128 + 128] = split[:, p * 128:p * 128 + 128]
            at = p * 128 + g * 64
            ht_own[at:at + 64, :] = turned[p * 64:p * 64 + 64, :]
            sib[FEAT + at:FEAT + at + 64, :] = turned[128 + p * 64:128 + p * 64 + 64, :]

    def step(n, carry):
        out = mm(hh[...], pd[:, pl.ds(pl.multiple_of(n * 1024, 1024), 1024)])
        parts = []
        for m in range(4):
            a0, a1 = out[:TOK, m * 256:m * 256 + 128], out[TOK:, m * 256:m * 256 + 128]
            b0, b1 = out[:TOK, m * 256 + 128:m * 256 + 256], out[TOK:, m * 256 + 128:m * 256 + 256]
            parts.append(jnp.where(low, a0, b1) + pltpu.roll(jnp.where(low, b0, a1), 64, 1))
        whole = jnp.concatenate(parts, axis=1).astype(BF)
        for r in range(NY):
            out_parts[lax.rem(y + r, NY), :, pl.ds(pl.multiple_of(n * 512, 512), 512)] = whole[r * 32:r * 32 + 32, :]
        return carry

    lax.fori_loop(0, 8, step, 0)


def forward(pieces, pg, pu, pd):
    lin = pltpu.VMEM((TOK, WIDE), F32)
    return pl.pallas_call(
        forward_kernel,
        in_specs=vm(7),
        out_specs=vm(6),
        out_shape=[
            shape(FEAT, TOK), shape(256, TOK), shape(FEAT + 256, TOK), lin, lin, shape(NY, 32, D)
        ],
        scratch_shapes=[
            pltpu.VMEM((TOK, D), BF),
            pltpu.VMEM((256, FEAT), BF),
            pltpu.VMEM((TOK, 1024), BF),
            pltpu.VMEM((256, 256), BF),
        ],
        compiler_params=params(24),
        cost_estimate=cost(8),
        name="forward",
    )(*pieces, pg, pu, pd)


def emit(wswap, tiles, parts, row):
    turned = mm(wswap, tiles[...]).astype(BF)
    for rel, dst in enumerate(parts):
        for k in range(4):
            top = (rel * 4 + k) * 16
            for half in range(2):
                dst[row + half * 16:row + half * 16 + 16, k * 128:k * 128 + 128] = turned[
                    top:top + 16, half * 128:half * 128 + 128
                ]


def down_kernel(idx, cot_own, cot_oth, ht_own, sib_oth, w0, w1, w2, w3, both, part, tiles):
    wswap = wire_swap(place()[1])
    both[:TOK, :] = cot_own[...]
    both[TOK:, :] = cot_oth[...]

    def product(n, carry):
        lanes = pl.ds(pl.multiple_of(n * 512, 512), 512)
        hidden = jnp.concatenate([ht_own[...], sib_oth[FEAT:, :]], axis=1)
        part[:, lanes] = mm(hidden, both[:, lanes]).astype(BF)
        return carry

    lax.fori_loop(0, 8, product, 0)
    side = lax.broadcasted_iota(jnp.int32, (16, 128), 1) // 64
    for j in range(COLS):
        for q in range(KEEP):
            i = idx[2, j * KEEP + q]
            odd = lax.rem(i, 2)
            lanes = pl.ds(pl.multiple_of((i // 2) * 128, 128), 128)
            near = part[pl.ds(pl.multiple_of(odd * 128 + j * 16, 16), 16), lanes].astype(F32)
            far = part[pl.ds(pl.multiple_of((1 - odd) * 128 + j * 16, 16), 16), lanes].astype(F32)
            tile = jnp.where(side == odd, near, pltpu.roll(far, 64, 1)).astype(BF)
            tiles[(q % 16) * 16:(q % 16) * 16 + 16, (q // 16) * 128:(q // 16) * 128 + 128] = tile
        emit(wswap, tiles, (w0, w1, w2, w3), j * KEEP)


def down_grads(idx, cot_own, cot_oth, ht_own, sib_oth):
    return pl.pallas_call(
        down_kernel,
        in_specs=smem(1) + vm(4),
        out_specs=vm(4),
        out_shape=[shape(SLOT, 512)] * 4,
        scratch_shapes=[pltpu.VMEM((256, D), BF), pltpu.VMEM((256, D), BF), pltpu.VMEM((256, 256), BF)],
        compiler_params=params(14),
        cost_estimate=cost(0.2),
        name="down_grads",
    )(idx, cot_own, cot_oth, ht_own, sib_oth)


def delta_kernel(c0, c1, c2, c3, pd_far, gl2, ul2, own, cot, gdx, udx, cx, pd, sem):
    def fetch(n):
        lanes = pl.ds(n * 1024, 1024)
        return pltpu.make_async_copy(pd_far.at[:, lanes], pd.at[:, lanes], sem.at[n])

    for n in range(8):
        fetch(n).start()
    at = cols_of(512)
    hjoin = one_hot(split_index(rows_of(256), 128), (at >> 7) * 128 + (at & 63))
    low = low_half((32, 128))
    for n, piece in enumerate((c0, c1, c2, c3)):
        top = slice(n * 32, n * 32 + 32)
        bottom = slice(TOK + n * 32, TOK + n * 32 + 32)
        cot[top, :] = piece[...]
        for m in range(32):
            c = piece[:, m * 128:m * 128 + 128].astype(F32)
            rolled = pltpu.roll(c, 64, 1)
            zero = jnp.zeros_like(c)
            first = slice(2 * m * 128, 2 * m * 128 + 128)
            second = slice(2 * m * 128 + 128, 2 * m * 128 + 256)
            cx[top, first] = jnp.where(low, c, zero).astype(BF)
            cx[bottom, first] = jnp.where(low, zero, rolled).astype(BF)
            cx[top, second] = jnp.where(low, rolled, zero).astype(BF)
            cx[bottom, second] = jnp.where(low, zero, c).astype(BF)

    hd = jnp.zeros((256, 256), F32)
    for n in range(8):
        lanes = slice(n * 1024, n * 1024 + 1024)
        fetch(n).wait()
        hd = hd + mm_nt(cx[:, lanes], pd[:, lanes])
    high = hd.astype(BF)
    rest = (hd - high.astype(F32)).astype(BF)
    low = low_half((TOK, 128))
    for g in range(2):
        cols = slice(g * 128, g * 128 + 128)
        joined = sum(
            mm(jnp.concatenate([part[:TOK, cols], part[TOK:, cols]], axis=1), hjoin) for part in (high, rest)
        )
        before = None
        for jl in range(4):
            j = g * 4 + jl
            if j == COLS:
                break
            lanes = slice(j * 128, j * 128 + 128)
            delta = joined[:, jl * 128:jl * 128 + 128]
            gl, ul = gl2[:, lanes], ul2[:, lanes]
            sig = 1.0 / (1.0 + jnp.exp(-gl))
            gd = delta * ul * sig * (1.0 + gl * (1.0 - sig))
            ud = delta * gl * sig
            for dst, val in ((gdx, gd), (udx, ud)):
                dst[:TOK, lanes] = jnp.where(low, val, 0.0).astype(BF)
                dst[TOK:, lanes] = jnp.where(low, 0.0, val).astype(BF)
            pair = slice((j // 2) * 128, (j // 2) * 128 + 128)
            if j % 2:
                own[:TOK, pair] = jnp.where(low, before[0], gd).astype(BF)
                own[TOK:, pair] = jnp.where(low, before[1], ud).astype(BF)
            elif j == COLS - 1:
                own[:TOK, pair] = jnp.where(low, gd, 0.0).astype(BF)
                own[TOK:, pair] = jnp.where(low, ud, 0.0).astype(BF)
            before = (gd, ud)


def deltas(pieces, pd, gl2, ul2):
    return pl.pallas_call(
        delta_kernel,
        in_specs=vm(4) + [pl.BlockSpec(memory_space=pl.ANY)] + vm(2),
        out_specs=vm(4),
        out_shape=[shape(256, 512), shape(TOK, D)] + [pltpu.VMEM((256, WIDE), BF)] * 2,
        scratch_shapes=[
            pltpu.VMEM((256, 2 * D), BF),
            pltpu.VMEM((256, 2 * D), BF),
            pltpu.SemaphoreType.DMA((8,)),
        ],
        compiler_params=params(18),
        cost_estimate=cost(0.2),
        name="deltas",
    )(*pieces, hbm(pd), gl2, ul2)


def back_kernel(gdx, udx, pg, pu, out_parts, parts, fjoin):
    y = place()[2]
    n = pl.program_id(0)

    @pl.when(n == 0)
    def _():
        fjoin[...] = one_hot(split_index(rows_of(256), 64), cols_of(256))

    parts[:, :32, :] = out_parts[...]
    acc = (mm_nt(gdx[...], pg[...]) + mm_nt(udx[...], pu[...])).astype(BF)
    for c in range(4):
        cols = slice(c * 128, c * 128 + 128)
        pair = jnp.concatenate([acc[:TOK, cols], acc[TOK:, cols]], axis=1)
        whole = mm(pair, fjoin[...]).astype(BF)
        for r in range(NY):
            parts[lax.rem(y + r, NY), 32:, c * 256:c * 256 + 256] = whole[r * 32:r * 32 + 32, :]


def input_parts(gdx, udx, pg, pu, out_parts):
    whole = pl.BlockSpec((256, WIDE), lambda n: (0, 0))
    panel = pl.BlockSpec((512, WIDE), lambda n: (n, 0))
    return pl.pallas_call(
        back_kernel,
        grid=(FEAT // 512,),
        in_specs=[whole, whole, panel, panel, pl.BlockSpec((NY, 32, 1024), lambda n: (0, 0, n))],
        out_specs=pl.BlockSpec((NY, 64, 1024), lambda n: (0, 0, n)),
        out_shape=shape(NY, 64, D),
        scratch_shapes=[pltpu.VMEM((256, 256), BF)],
        compiler_params=params(14),
        cost_estimate=cost(0.2),
        name="input_parts",
    )(gdx, udx, hbm(pg), hbm(pu), out_parts)


def merge_kernel(got, both):
    for n in range(0, D, 512):
        lanes = slice(n, n + 512)
        total = sum(got[r, :, lanes].astype(F32) for r in range(1, NY)) + got[0, :, lanes].astype(F32)
        for z in range(NZ):
            both[z, :, lanes] = jnp.concatenate(
                [total[z * 4:z * 4 + 4], total[32 + z * 4:36 + z * 4]], axis=0
            ).astype(BF)


def merge_y(got):
    return pl.pallas_call(
        merge_kernel,
        in_specs=vm(1),
        out_specs=vm(1)[0],
        out_shape=shape(NZ, 8, D),
        compiler_params=params(10),
        cost_estimate=cost(0.2),
        name="merge_y",
    )(got)


def inward_kernel(m, idx, xt_own, sib_oth, d_own, d_oth, w0, w1, w2, w3, part, tiles):
    wswap = wire_swap(place()[1])
    low = low_half((16, 128))
    delta = jnp.concatenate([d[m * TOK:m * TOK + TOK, :] for d in (d_own, d_oth)], axis=0)

    def product(n, carry):
        rows = pl.ds(pl.multiple_of(n * 256, 256), 256)
        tokens = jnp.concatenate([xt_own[rows, :], sib_oth[rows, :]], axis=1)
        part[rows, :] = mm(tokens, delta).astype(BF)
        return carry

    lax.fori_loop(0, 8, product, 0)
    for j in range(COLS):
        odd = j % 2
        lanes = slice((j // 2) * 128, (j // 2) * 128 + 128)
        for q in range(KEEP):
            i = idx[m, j * KEEP + q]
            first = part[pl.ds(pl.multiple_of(i * 16, 16), 16), lanes].astype(F32)
            second = part[pl.ds(pl.multiple_of(1024 + i * 16, 16), 16), lanes].astype(F32)
            if odd:
                first = pltpu.roll(first, 64, 1)
            else:
                second = pltpu.roll(second, 64, 1)
            tile = jnp.where(low, first, second).astype(BF)
            tiles[(q % 16) * 16:(q % 16) * 16 + 16, (q // 16) * 128:(q // 16) * 128 + 128] = tile
        emit(wswap, tiles, (w0, w1, w2, w3), j * KEEP)


def inward_grads(m, idx, xt_own, sib_oth, d_own, d_oth):
    return pl.pallas_call(
        functools.partial(inward_kernel, m),
        in_specs=smem(1) + vm(4),
        out_specs=vm(4),
        out_shape=[shape(SLOT, 512)] * 4,
        scratch_shapes=[pltpu.VMEM((FEAT, 512), BF), pltpu.VMEM((256, 256), BF)],
        compiler_params=params(14),
        cost_estimate=cost(0.2),
        name=("gate_grads", "up_grads")[m],
    )(idx, xt_own, sib_oth, d_own, d_oth)


def from_y(value, step):
    pairs = [((y + step) % NY * NZ + z, y * NZ + z) for y in range(NY) for z in range(NZ)]
    return lax.ppermute(value, "fsdp", pairs)


def from_x(value, other):
    pairs = [((x ^ other) * NC + c, x * NC + c) for x in range(NX) for c in range(NC)]
    return lax.ppermute(value, "dp", pairs)


def from_core(value):
    pairs = [(x * NC + 1 - c, x * NC + c) for x in range(NX) for c in range(NC)]
    return lax.ppermute(value, "dp", pairs)


def z_groups():
    return [[y * NZ + z for z in range(NZ)] for y in range(NY)]


def y_groups():
    return [[y * NZ + z for y in range(NY)] for z in range(NZ)]


def over_z(value):
    return lax.all_to_all(value, "fsdp", 0, 0, axis_index_groups=z_groups(), tiled=True)


def over_y(value):
    return lax.all_to_all(value, "fsdp", 0, 0, axis_index_groups=y_groups(), tiled=True)


def copies_over_z(value):
    return over_z(jnp.broadcast_to(value[None], (NZ,) + value.shape))


def after(value, *others):
    return lax.optimization_barrier((value,) + others)[0]


def exchange_x(parts):
    return [parts[0]] + [from_x(parts[d], d) for d in range(1, NX)]


def mean_of(parts):
    total = sum((p.astype(F32) for p in parts[1:]), parts[0].astype(F32))
    return (total * (1.0 / (NX * NC))).astype(BF)


def body(tokens, cotangent, gate_blocks, up_blocks, down_blocks, block_index):
    rows = tokens.shape[0]
    ring = copies_over_z(jnp.concatenate([tokens, cotangent], axis=0))
    tok_z = ring[:, :rows].reshape(NZ * rows, D)
    cot_z = ring[:, rows:].reshape(NZ * rows, D)
    tok = [tok_z] + [from_y(tok_z, s) for s in range(1, NY)]
    idx = after(block_index, tok_z)
    pg, pu = inward_panels(idx, gate_blocks, up_blocks)
    cot_z = after(cot_z, pg)
    pd = outward_panel(idx, down_blocks)
    cot = [cot_z] + [from_y(cot_z, s) for s in range(1, NY)]

    xt_own, ht_own, sib, gl2, ul2, out_parts = forward(tok, pg, pu, pd)
    sib_oth = from_core(after(sib, *cot))
    own, cot_own, gdx, udx = deltas(cot, pd, gl2, ul2)
    oth, cot_oth = from_core(own), from_core(cot_own)
    gate_wire = inward_grads(0, block_index, xt_own, sib_oth, own, oth)
    gate_got = exchange_x(gate_wire)
    parts = input_parts(after(gdx, gate_wire[0]), udx, pg, pu, out_parts)
    parts_got = over_y(parts)
    down_wire = down_grads(block_index, cot_own, cot_oth, after(ht_own, parts), sib_oth)
    down_got = exchange_x(down_wire)
    up_wire = inward_grads(1, block_index, xt_own, sib_oth, after(own, down_wire[0], *gate_got[1:]), oth)
    up_got = exchange_x(up_wire)
    both = merge_y(after(parts_got, up_wire[0], *down_got[1:]))
    gate_grad, up_grad, down_grad = (mean_of(g) for g in (gate_got, up_got, down_got))
    total = over_z(both).astype(F32).sum(axis=0).astype(BF)
    return (total[:rows], total[rows:], gate_grad, up_grad, down_grad)


def solution(mesh):
    return jax.shard_map(
        body,
        mesh=mesh,
        in_specs=(
            P(("dp", "fsdp"), None),
            P(("dp", "fsdp"), None),
            P("fsdp", None),
            P("fsdp", None),
            P("fsdp", None),
            P(None, "fsdp"),
        ),
        out_specs=(
            P(("dp", "fsdp"), None),
            P(("dp", "fsdp"), None),
            P("fsdp", "dp"),
            P("fsdp", "dp"),
            P("fsdp", "dp"),
        ),
        check_vma=False,
    )
```

```python
import jax
import jax.numpy as jnp
from jax import lax
from jax.experimental import pallas as pl
from jax.experimental.pallas import tpu as pltpu
from jax.sharding import PartitionSpec as P

D = 4096
BLK = 64
KEEP = 32
COLS = 7
SLOT = COLS * KEEP
TOK = 128
FEAT = 2048
WIDE = COLS * 128
NX, NC, NY, NZ = 4, 2, 4, 8
BF = jnp.bfloat16
F32 = jnp.float32

TILE_ROWS = [[8 * x + 4 * c + k4 for x in range(NX) for k4 in range(4)] for c in range(NC)]


def rows_of(n):
    return lax.broadcasted_iota(jnp.int32, (n, 1), 0)


def cols_of(n):
    return lax.broadcasted_iota(jnp.int32, (1, n), 1)


def one_hot(left, right):
    return jnp.where(left == right, 1.0, 0.0).astype(BF)


def split_index(at, stride):
    k = 8 * ((at >> 2) & 3) + 4 * ((at >> 4) & 1) + (at & 3)
    return ((at >> 5) & 3) * stride + 2 * k + (at >> 7)


def turn_index(at, core, stride):
    k = 8 * ((at >> 2) & 3) + 4 * (core ^ (at >> 7)) + (at & 3)
    return ((at >> 4) & 3) * stride + 2 * k + ((at >> 6) & 1)


def swap_matrix():
    at = cols_of(256)
    return one_hot(rows_of(256), (at & 15) * 16 + (at >> 4))


def wire_swap(x):
    at = rows_of(256)
    return one_hot((at & 15) * 16 + ((at >> 6) ^ x) * 4 + ((at >> 4) & 3), cols_of(256))


def place():
    dp, fsdp = lax.axis_index("dp"), lax.axis_index("fsdp")
    return lax.rem(dp, NC), dp // NC, fsdp // NZ


def mm(a, b):
    return jnp.dot(a, b, preferred_element_type=F32)


def mm_nt(a, b):
    return lax.dot_general(a, b, (((1,), (1,)), ((), ())), preferred_element_type=F32)


def low_half(shape):
    return lax.broadcasted_iota(jnp.int32, shape, 1) < 64


def vm(n):
    return [pl.BlockSpec(memory_space=pltpu.VMEM)] * n


def smem(n):
    return [pl.BlockSpec(memory_space=pltpu.SMEM)] * n


def params(mib):
    return pltpu.CompilerParams(vmem_limit_bytes=mib << 20)


def cost(us):
    return pl.CostEstimate(flops=int(us * 1_000_000_000), bytes_accessed=1000, transcendentals=0)


def shape(*dims, dtype=BF):
    return jax.ShapeDtypeStruct(dims, dtype)


def unfold(src, row, swap):
    rows = pl.ds(pl.multiple_of(row, 16), 16)
    halves = [jnp.concatenate([src[rows, k * 128:k * 128 + 128] for k in TILE_ROWS[c]], axis=0) for c in range(2)]
    return mm(swap, jnp.concatenate(halves, axis=1)).astype(BF)


def inward_panels_kernel(idx, gate, up, pg, pu, held, tiles, sems):
    fetches = [pltpu.make_async_copy(src, held.at[m], sems.at[m]) for m, src in enumerate((gate, up))]
    for fetch in fetches:
        fetch.start()
    swap = swap_matrix()
    for m, dst in enumerate((pg, pu)):
        dst[...] = jnp.zeros_like(dst)
        fetches[m].wait()

        def column(j, carry):
            lanes = pl.ds(pl.multiple_of(j * 128, 128), 128)
            for half in range(2):
                tiles[half, :, :] = unfold(held.at[m], j * KEEP + half * 16, swap)
                for q in range(16):
                    i = idx[m, j * KEEP + half * 16 + q]
                    for c in range(2):
                        dst[pl.ds(pl.multiple_of(i * 32 + c * 16, 16), 16), lanes] = tiles[
                            half, q * 16:q * 16 + 16, c * 128:c * 128 + 128
                        ]
            return carry

        lax.fori_loop(0, COLS, column, 0)


def outward_panel_kernel(idx, down, pd, held, tiles, sem):
    fetch = pltpu.make_async_copy(down, held, sem)
    fetch.start()
    swap = swap_matrix()
    pd[...] = jnp.zeros_like(pd)
    fetch.wait()

    def column(j, carry):
        for half in range(2):
            tiles[half, :, :] = unfold(held, j * KEEP + half * 16, swap)
            for q in range(16):
                i = idx[2, j * KEEP + half * 16 + q]
                for c in range(2):
                    rows = pl.ds(pl.multiple_of(j * 32 + c * 16, 16), 16)
                    pd[rows, pl.ds(pl.multiple_of(i * 128, 128), 128)] = tiles[
                        half, q * 16:q * 16 + 16, c * 128:c * 128 + 128
                    ]
        return carry

    lax.fori_loop(0, COLS, column, 0)


def hbm(value):
    return pltpu.with_memory_space_constraint(value, pltpu.HBM)


def far(n):
    return [pl.BlockSpec(memory_space=pl.ANY)] * n


def inward_panels(idx, gate, up):
    return pl.pallas_call(
        inward_panels_kernel,
        in_specs=smem(1) + far(2),
        out_specs=vm(2),
        out_shape=[pltpu.VMEM((FEAT, WIDE), BF), pltpu.VMEM((FEAT, WIDE), BF)],
        scratch_shapes=[
            pltpu.VMEM((2, SLOT, D), BF),
            pltpu.VMEM((2, 256, 256), BF),
            pltpu.SemaphoreType.DMA((2,)),
        ],
        compiler_params=params(14),
        cost_estimate=cost(6),
        name="inward_panels",
    )(idx, hbm(gate), hbm(up))


def outward_panel(idx, down):
    return pl.pallas_call(
        outward_panel_kernel,
        in_specs=smem(1) + far(1),
        out_specs=vm(1)[0],
        out_shape=pltpu.VMEM((256, 2 * D), BF),
        scratch_shapes=[pltpu.VMEM((SLOT, D), BF), pltpu.VMEM((2, 256, 256), BF), pltpu.SemaphoreType.DMA],
        compiler_params=params(10),
        cost_estimate=cost(3),
        name="outward_panel",
    )(idx, hbm(down))


def forward_kernel(t0, t1, t2, t3, pg, pu, pd, xt_own, ht_own, sib, gl2, ul2, out_parts, tok, xx, hid, hh):
    core, _, y = place()
    fsplit = one_hot(rows_of(256), split_index(cols_of(256), 64))
    fturn = one_hot(turn_index(rows_of(256), core, 64), cols_of(256))
    hsplit = one_hot(rows_of(512), split_index(cols_of(256), 128))
    hturn = one_hot(turn_index(rows_of(256), core, 128), cols_of(512))
    for n, piece in enumerate((t0, t1, t2, t3)):
        tok[n * 32:n * 32 + 32, :] = piece[...]
    for c in range(16):
        chunk = tok[:, c * 256:c * 256 + 256]
        split = mm(chunk, fsplit).astype(BF)
        turned = mm_nt(fturn, chunk).astype(BF)
        for p in range(2):
            xx[p * 128:p * 128 + 128, c * 128:c * 128 + 128] = split[:, p * 128:p * 128 + 128]
            at = p * 1024 + c * 64
            xt_own[at:at + 64, :] = turned[p * 64:p * 64 + 64, :]
            sib[at:at + 64, :] = turned[128 + p * 64:128 + p * 64 + 64, :]
    low = low_half((TOK, 128))
    hid[:, WIDE:] = jnp.zeros((TOK, 128), BF)
    for n in range(0, WIDE, 256):
        width = min(256, WIDE - n)
        gate = mm(xx[...], pg[:, n:n + width])
        up = mm(xx[...], pu[:, n:n + width])
        for s in range(0, width, 128):
            cols = slice(n + s, n + s + 128)
            gl = jnp.where(low, gate[:TOK, s:s + 128], gate[TOK:, s:s + 128])
            gl = gl + pltpu.roll(gl, 64, 1)
            ul = jnp.where(low, up[:TOK, s:s + 128], up[TOK:, s:s + 128])
            ul = ul + pltpu.roll(ul, 64, 1)
            gl2[:, cols] = gl
            ul2[:, cols] = ul
            hid[:, cols] = (gl * (1.0 / (1.0 + jnp.exp(-gl))) * ul).astype(BF)
    for g in range(2):
        group = hid[:, g * 512:g * 512 + 512]
        split = mm(group, hsplit).astype(BF)
        turned = mm_nt(hturn, group).astype(BF)
        for p in range(2):
            hh[p * 128:p * 128 + 128, g * 128:g * 128 + 128] = split[:, p * 128:p * 128 + 128]
            at = p * 128 + g * 64
            ht_own[at:at + 64, :] = turned[p * 64:p * 64 + 64, :]
            sib[FEAT + at:FEAT + at + 64, :] = turned[128 + p * 64:128 + p * 64 + 64, :]

    def step(n, carry):
        out = mm(hh[...], pd[:, pl.ds(pl.multiple_of(n * 1024, 1024), 1024)])
        parts = []
        for m in range(4):
            a0, a1 = out[:TOK, m * 256:m * 256 + 128], out[TOK:, m * 256:m * 256 + 128]
            b0, b1 = out[:TOK, m * 256 + 128:m * 256 + 256], out[TOK:, m * 256 + 128:m * 256 + 256]
            parts.append(jnp.where(low, a0, b1) + pltpu.roll(jnp.where(low, b0, a1), 64, 1))
        whole = jnp.concatenate(parts, axis=1).astype(BF)
        for r in range(NY):
            out_parts[lax.rem(y + r, NY), :, pl.ds(pl.multiple_of(n * 512, 512), 512)] = whole[r * 32:r * 32 + 32, :]
        return carry

    lax.fori_loop(0, 8, step, 0)


def forward(pieces, pg, pu, pd):
    lin = pltpu.VMEM((TOK, WIDE), F32)
    return pl.pallas_call(
        forward_kernel,
        in_specs=vm(7),
        out_specs=vm(6),
        out_shape=[
            shape(FEAT, TOK), shape(256, TOK), shape(FEAT + 256, TOK), lin, lin, shape(NY, 32, D)
        ],
        scratch_shapes=[
            pltpu.VMEM((TOK, D), BF),
            pltpu.VMEM((256, FEAT), BF),
            pltpu.VMEM((TOK, 1024), BF),
            pltpu.VMEM((256, 256), BF),
        ],
        compiler_params=params(24),
        cost_estimate=cost(8),
        name="forward",
    )(*pieces, pg, pu, pd)


def emit(wswap, tiles, parts, row):
    turned = mm(wswap, tiles[...]).astype(BF)
    for rel, dst in enumerate(parts):
        for k in range(4):
            top = (rel * 4 + k) * 16
            for half in range(2):
                dst[row + half * 16:row + half * 16 + 16, k * 128:k * 128 + 128] = turned[
                    top:top + 16, half * 128:half * 128 + 128
                ]


def down_kernel(idx, cot_own, cot_oth, ht_own, sib_oth, w0, w1, w2, w3, both, part, tiles):
    wswap = wire_swap(place()[1])
    both[:TOK, :] = cot_own[...]
    both[TOK:, :] = cot_oth[...]

    def product(n, carry):
        lanes = pl.ds(pl.multiple_of(n * 512, 512), 512)
        hidden = jnp.concatenate([ht_own[...], sib_oth[FEAT:, :]], axis=1)
        part[:, lanes] = mm(hidden, both[:, lanes]).astype(BF)
        return carry

    lax.fori_loop(0, 8, product, 0)
    side = lax.broadcasted_iota(jnp.int32, (16, 128), 1) // 64
    for j in range(COLS):
        for q in range(KEEP):
            i = idx[2, j * KEEP + q]
            odd = lax.rem(i, 2)
            lanes = pl.ds(pl.multiple_of((i // 2) * 128, 128), 128)
            near = part[pl.ds(pl.multiple_of(odd * 128 + j * 16, 16), 16), lanes].astype(F32)
            far = part[pl.ds(pl.multiple_of((1 - odd) * 128 + j * 16, 16), 16), lanes].astype(F32)
            tile = jnp.where(side == odd, near, pltpu.roll(far, 64, 1)).astype(BF)
            tiles[(q % 16) * 16:(q % 16) * 16 + 16, (q // 16) * 128:(q // 16) * 128 + 128] = tile
        emit(wswap, tiles, (w0, w1, w2, w3), j * KEEP)


def down_grads(idx, cot_own, cot_oth, ht_own, sib_oth):
    return pl.pallas_call(
        down_kernel,
        in_specs=smem(1) + vm(4),
        out_specs=vm(4),
        out_shape=[pltpu.HBM((SLOT, 512), BF)] * 4,
        scratch_shapes=[pltpu.VMEM((256, D), BF), pltpu.VMEM((256, D), BF), pltpu.VMEM((256, 256), BF)],
        compiler_params=params(14),
        cost_estimate=cost(0.2),
        name="down_grads",
    )(idx, cot_own, cot_oth, ht_own, sib_oth)


def delta_kernel(c0, c1, c2, c3, pd_far, gl2, ul2, own, cot, gdx, udx, cx, pd, sem):
    def fetch(n):
        lanes = pl.ds(n * 1024, 1024)
        return pltpu.make_async_copy(pd_far.at[:, lanes], pd.at[:, lanes], sem.at[n])

    for n in range(8):
        fetch(n).start()
    at = cols_of(512)
    hjoin = one_hot(split_index(rows_of(256), 128), (at >> 7) * 128 + (at & 63))
    low = low_half((32, 128))
    for n, piece in enumerate((c0, c1, c2, c3)):
        top = slice(n * 32, n * 32 + 32)
        bottom = slice(TOK + n * 32, TOK + n * 32 + 32)
        cot[top, :] = piece[...]
        for m in range(32):
            c = piece[:, m * 128:m * 128 + 128].astype(F32)
            rolled = pltpu.roll(c, 64, 1)
            zero = jnp.zeros_like(c)
            first = slice(2 * m * 128, 2 * m * 128 + 128)
            second = slice(2 * m * 128 + 128, 2 * m * 128 + 256)
            cx[top, first] = jnp.where(low, c, zero).astype(BF)
            cx[bottom, first] = jnp.where(low, zero, rolled).astype(BF)
            cx[top, second] = jnp.where(low, rolled, zero).astype(BF)
            cx[bottom, second] = jnp.where(low, zero, c).astype(BF)

    hd = jnp.zeros((256, 256), F32)
    for n in range(8):
        lanes = slice(n * 1024, n * 1024 + 1024)
        fetch(n).wait()
        hd = hd + mm_nt(cx[:, lanes], pd[:, lanes])
    high = hd.astype(BF)
    rest = (hd - high.astype(F32)).astype(BF)
    low = low_half((TOK, 128))
    for g in range(2):
        cols = slice(g * 128, g * 128 + 128)
        joined = sum(
            mm(jnp.concatenate([part[:TOK, cols], part[TOK:, cols]], axis=1), hjoin) for part in (high, rest)
        )
        before = None
        for jl in range(4):
            j = g * 4 + jl
            if j == COLS:
                break
            lanes = slice(j * 128, j * 128 + 128)
            delta = joined[:, jl * 128:jl * 128 + 128]
            gl, ul = gl2[:, lanes], ul2[:, lanes]
            sig = 1.0 / (1.0 + jnp.exp(-gl))
            gd = delta * ul * sig * (1.0 + gl * (1.0 - sig))
            ud = delta * gl * sig
            for dst, val in ((gdx, gd), (udx, ud)):
                dst[:TOK, lanes] = jnp.where(low, val, 0.0).astype(BF)
                dst[TOK:, lanes] = jnp.where(low, 0.0, val).astype(BF)
            pair = slice((j // 2) * 128, (j // 2) * 128 + 128)
            if j % 2:
                own[:TOK, pair] = jnp.where(low, before[0], gd).astype(BF)
                own[TOK:, pair] = jnp.where(low, before[1], ud).astype(BF)
            elif j == COLS - 1:
                own[:TOK, pair] = jnp.where(low, gd, 0.0).astype(BF)
                own[TOK:, pair] = jnp.where(low, ud, 0.0).astype(BF)
            before = (gd, ud)


def deltas(pieces, pd, gl2, ul2):
    return pl.pallas_call(
        delta_kernel,
        in_specs=vm(4) + [pl.BlockSpec(memory_space=pl.ANY)] + vm(2),
        out_specs=vm(4),
        out_shape=[shape(256, 512), pltpu.HBM((TOK, D), BF)] + [pltpu.VMEM((256, WIDE), BF)] * 2,
        scratch_shapes=[
            pltpu.VMEM((256, 2 * D), BF),
            pltpu.VMEM((256, 2 * D), BF),
            pltpu.SemaphoreType.DMA((8,)),
        ],
        compiler_params=params(18),
        cost_estimate=cost(0.2),
        name="deltas",
    )(*pieces, hbm(pd), gl2, ul2)


def back_kernel(gdx, udx, pg, pu, out_parts, parts, fjoin):
    y = place()[2]
    n = pl.program_id(0)

    @pl.when(n == 0)
    def _():
        fjoin[...] = one_hot(split_index(rows_of(256), 64), cols_of(256))

    parts[:, :32, :] = out_parts[...]
    acc = (mm_nt(gdx[...], pg[...]) + mm_nt(udx[...], pu[...])).astype(BF)
    for c in range(4):
        cols = slice(c * 128, c * 128 + 128)
        pair = jnp.concatenate([acc[:TOK, cols], acc[TOK:, cols]], axis=1)
        whole = mm(pair, fjoin[...]).astype(BF)
        for r in range(NY):
            parts[lax.rem(y + r, NY), 32:, c * 256:c * 256 + 256] = whole[r * 32:r * 32 + 32, :]


def input_parts(gdx, udx, pg, pu, out_parts):
    whole = pl.BlockSpec((256, WIDE), lambda n: (0, 0))
    panel = pl.BlockSpec((512, WIDE), lambda n: (n, 0))
    return pl.pallas_call(
        back_kernel,
        grid=(FEAT // 512,),
        in_specs=[whole, whole, panel, panel, pl.BlockSpec((NY, 32, 1024), lambda n: (0, 0, n))],
        out_specs=pl.BlockSpec((NY, 64, 1024), lambda n: (0, 0, n)),
        out_shape=pltpu.HBM((NY, 64, D), BF),
        scratch_shapes=[pltpu.VMEM((256, 256), BF)],
        compiler_params=params(14),
        cost_estimate=cost(0.2),
        name="input_parts",
    )(gdx, udx, hbm(pg), hbm(pu), out_parts)


def merge_kernel(got, both):
    for n in range(0, D, 512):
        lanes = slice(n, n + 512)
        total = sum(got[r, :, lanes].astype(F32) for r in range(1, NY)) + got[0, :, lanes].astype(F32)
        for z in range(NZ):
            both[z, :, lanes] = jnp.concatenate(
                [total[z * 4:z * 4 + 4], total[32 + z * 4:36 + z * 4]], axis=0
            ).astype(BF)


def merge_y(got):
    return pl.pallas_call(
        merge_kernel,
        in_specs=vm(1),
        out_specs=vm(1)[0],
        out_shape=shape(NZ, 8, D),
        compiler_params=params(10),
        cost_estimate=cost(0.2),
        name="merge_y",
    )(got)


def inward_kernel(idx, xt_own, sib_oth, d_own, d_oth, w0, w1, w2, w3, part, tiles):
    wswap = wire_swap(place()[1])
    low = low_half((16, 128))
    for m in range(2):
        delta = jnp.concatenate([d[m * TOK:m * TOK + TOK, :] for d in (d_own, d_oth)], axis=0)

        def product(n, carry):
            rows = pl.ds(pl.multiple_of(n * 256, 256), 256)
            tokens = jnp.concatenate([xt_own[rows, :], sib_oth[rows, :]], axis=1)
            part[rows, :] = mm(tokens, delta).astype(BF)
            return carry

        lax.fori_loop(0, 8, product, 0)
        for j in range(COLS):
            odd = j % 2
            lanes = slice((j // 2) * 128, (j // 2) * 128 + 128)
            for q in range(KEEP):
                i = idx[m, j * KEEP + q]
                first = part[pl.ds(pl.multiple_of(i * 16, 16), 16), lanes].astype(F32)
                second = part[pl.ds(pl.multiple_of(1024 + i * 16, 16), 16), lanes].astype(F32)
                if odd:
                    first = pltpu.roll(first, 64, 1)
                else:
                    second = pltpu.roll(second, 64, 1)
                tile = jnp.where(low, first, second).astype(BF)
                tiles[(q % 16) * 16:(q % 16) * 16 + 16, (q // 16) * 128:(q // 16) * 128 + 128] = tile
            emit(wswap, tiles, (w0, w1, w2, w3), m * SLOT + j * KEEP)


def inward_grads(idx, xt_own, sib_oth, d_own, d_oth):
    return pl.pallas_call(
        inward_kernel,
        in_specs=smem(1) + vm(4),
        out_specs=vm(4),
        out_shape=[pltpu.HBM((2 * SLOT, 512), BF)] * 4,
        scratch_shapes=[pltpu.VMEM((FEAT, 512), BF), pltpu.VMEM((256, 256), BF)],
        compiler_params=params(14),
        cost_estimate=cost(0.2),
        name="inward_grads",
    )(idx, xt_own, sib_oth, d_own, d_oth)


def from_y(value, step):
    pairs = [((y + step) % NY * NZ + z, y * NZ + z) for y in range(NY) for z in range(NZ)]
    return lax.ppermute(value, "fsdp", pairs)


def from_x(value, other):
    pairs = [((x ^ other) * NC + c, x * NC + c) for x in range(NX) for c in range(NC)]
    return lax.ppermute(value, "dp", pairs)


def from_core(value):
    pairs = [(x * NC + 1 - c, x * NC + c) for x in range(NX) for c in range(NC)]
    return lax.ppermute(value, "dp", pairs)


def z_groups():
    return [[y * NZ + z for z in range(NZ)] for y in range(NY)]


def y_groups():
    return [[y * NZ + z for y in range(NY)] for z in range(NZ)]


def over_z(value):
    return lax.all_to_all(value, "fsdp", 0, 0, axis_index_groups=z_groups(), tiled=True)


def over_y(value):
    return lax.all_to_all(value, "fsdp", 0, 0, axis_index_groups=y_groups(), tiled=True)


def copies_over_z(value):
    return over_z(jnp.broadcast_to(value[None], (NZ,) + value.shape))


def after(value, *others):
    return lax.optimization_barrier((value,) + others)[0]


def exchange_x(parts):
    return [parts[0]] + [from_x(parts[d], d) for d in range(1, NX)]


def mean_of(*parts):
    total = sum((p.astype(F32) for p in parts[1:]), parts[0].astype(F32))
    return (total * (1.0 / (NX * NC))).astype(BF)


def inward_mean_kernel(a, b, c, d, gate, up):
    for n, dst in enumerate((gate, up)):
        rows = slice(n * SLOT, n * SLOT + SLOT)
        dst[...] = mean_of(*(p[rows, :] for p in (a, b, c, d)))


def inward_mean(*parts):
    return pl.pallas_call(
        inward_mean_kernel,
        in_specs=vm(4),
        out_specs=vm(2),
        out_shape=[shape(SLOT, 512)] * 2,
        compiler_params=params(10),
        cost_estimate=cost(20),
        name="inward_mean",
    )(*parts)


def body(tokens, cotangent, gate_blocks, up_blocks, down_blocks, block_index):
    rows = tokens.shape[0]
    ring = copies_over_z(jnp.concatenate([tokens, cotangent], axis=0))
    tok_z = ring[:, :rows].reshape(NZ * rows, D)
    cot_z = ring[:, rows:].reshape(NZ * rows, D)
    tok = [tok_z] + [from_y(tok_z, s) for s in range(1, NY)]
    idx = after(block_index, tok_z)
    pg, pu = inward_panels(idx, gate_blocks, up_blocks)
    cot_z = after(cot_z, pg)
    pd = outward_panel(idx, down_blocks)
    cot = [cot_z] + [from_y(cot_z, s) for s in range(1, NY)]

    xt_own, ht_own, sib, gl2, ul2, out_parts = forward(tok, pg, pu, pd)
    sib_oth = from_core(after(sib, *cot))
    own, cot_own, gdx, udx = deltas(cot, pd, gl2, ul2)
    oth, cot_oth = from_core(own), from_core(cot_own)
    parts = input_parts(gdx, udx, pg, pu, out_parts)
    parts_got = over_y(after(parts, cot_oth, sib_oth))
    down_wire = down_grads(block_index, cot_own, cot_oth, after(ht_own, parts), sib_oth)
    down_got = exchange_x(down_wire)
    wire = inward_grads(block_index, xt_own, sib_oth, after(own, down_wire[0]), oth)
    got = exchange_x(wire)
    down_grad = mean_of(*down_got)
    both = merge_y(after(parts_got, wire[0], down_grad))
    gate_grad, up_grad = inward_mean(*got)
    total = after(over_z(both), gate_grad).astype(F32).sum(axis=0).astype(BF)
    return (total[:rows], total[rows:], gate_grad, up_grad, down_grad)


def solution(mesh):
    return jax.shard_map(
        body,
        mesh=mesh,
        in_specs=(
            P(("dp", "fsdp"), None),
            P(("dp", "fsdp"), None),
            P("fsdp", None),
            P("fsdp", None),
            P("fsdp", None),
            P(None, "fsdp"),
        ),
        out_specs=(
            P(("dp", "fsdp"), None),
            P(("dp", "fsdp"), None),
            P("fsdp", "dp"),
            P("fsdp", "dp"),
            P("fsdp", "dp"),
        ),
        check_vma=False,
    )
```

```python
import jax
import jax.numpy as jnp
from jax import lax
from jax.experimental import pallas as pl
from jax.experimental.pallas import tpu as pltpu
from jax.sharding import PartitionSpec as P

D = 4096
BLK = 64
KEEP = 32
COLS = 7
SLOT = COLS * KEEP
TOK = 128
FEAT = 2048
WIDE = COLS * 128
NX, NC, NY, NZ = 4, 2, 4, 8
BF = jnp.bfloat16
F32 = jnp.float32

TILE_ROWS = [[8 * x + 4 * c + k4 for x in range(NX) for k4 in range(4)] for c in range(NC)]


def rows_of(n):
    return lax.broadcasted_iota(jnp.int32, (n, 1), 0)


def cols_of(n):
    return lax.broadcasted_iota(jnp.int32, (1, n), 1)


def one_hot(left, right):
    return jnp.where(left == right, 1.0, 0.0).astype(BF)


def split_index(at, stride):
    k = 8 * ((at >> 2) & 3) + 4 * ((at >> 4) & 1) + (at & 3)
    return ((at >> 5) & 3) * stride + 2 * k + (at >> 7)


def turn_index(at, core, stride):
    k = 8 * ((at >> 2) & 3) + 4 * (core ^ (at >> 7)) + (at & 3)
    return ((at >> 4) & 3) * stride + 2 * k + ((at >> 6) & 1)


def swap_matrix():
    at = cols_of(256)
    return one_hot(rows_of(256), (at & 15) * 16 + (at >> 4))


def wire_swap(x):
    at = rows_of(256)
    return one_hot((at & 15) * 16 + ((at >> 6) ^ x) * 4 + ((at >> 4) & 3), cols_of(256))


def place():
    dp, fsdp = lax.axis_index("dp"), lax.axis_index("fsdp")
    return lax.rem(dp, NC), dp // NC, fsdp // NZ


def mm(a, b):
    return jnp.dot(a, b, preferred_element_type=F32)


def mm_nt(a, b):
    return lax.dot_general(a, b, (((1,), (1,)), ((), ())), preferred_element_type=F32)


def low_half(shape):
    return lax.broadcasted_iota(jnp.int32, shape, 1) < 64


def vm(n):
    return [pl.BlockSpec(memory_space=pltpu.VMEM)] * n


def smem(n):
    return [pl.BlockSpec(memory_space=pltpu.SMEM)] * n


def params(mib):
    return pltpu.CompilerParams(vmem_limit_bytes=mib << 20)


def cost(us):
    return pl.CostEstimate(flops=int(us * 1_000_000_000), bytes_accessed=1000, transcendentals=0)


def shape(*dims, dtype=BF):
    return jax.ShapeDtypeStruct(dims, dtype)


def unfold(src, row, swap):
    rows = pl.ds(pl.multiple_of(row, 16), 16)
    halves = [jnp.concatenate([src[rows, k * 128:k * 128 + 128] for k in TILE_ROWS[c]], axis=0) for c in range(2)]
    return mm(swap, jnp.concatenate(halves, axis=1)).astype(BF)


def inward_panels_kernel(idx, gate, up, pg, pu, held, tiles, sems):
    fetches = [pltpu.make_async_copy(src, held.at[m], sems.at[m]) for m, src in enumerate((gate, up))]
    for fetch in fetches:
        fetch.start()
    swap = swap_matrix()
    for m, dst in enumerate((pg, pu)):
        dst[...] = jnp.zeros_like(dst)
        fetches[m].wait()

        def column(j, carry):
            lanes = pl.ds(pl.multiple_of(j * 128, 128), 128)
            for half in range(2):
                tiles[half, :, :] = unfold(held.at[m], j * KEEP + half * 16, swap)
                for q in range(16):
                    i = idx[m, j * KEEP + half * 16 + q]
                    for c in range(2):
                        dst[pl.ds(pl.multiple_of(i * 32 + c * 16, 16), 16), lanes] = tiles[
                            half, q * 16:q * 16 + 16, c * 128:c * 128 + 128
                        ]
            return carry

        lax.fori_loop(0, COLS, column, 0)


def outward_panel_kernel(idx, down, pd, held, tiles, sem):
    fetch = pltpu.make_async_copy(down, held, sem)
    fetch.start()
    swap = swap_matrix()
    pd[...] = jnp.zeros_like(pd)
    fetch.wait()

    def column(j, carry):
        for half in range(2):
            tiles[half, :, :] = unfold(held, j * KEEP + half * 16, swap)
            for q in range(16):
                i = idx[2, j * KEEP + half * 16 + q]
                for c in range(2):
                    rows = pl.ds(pl.multiple_of(j * 32 + c * 16, 16), 16)
                    pd[rows, pl.ds(pl.multiple_of(i * 128, 128), 128)] = tiles[
                        half, q * 16:q * 16 + 16, c * 128:c * 128 + 128
                    ]
        return carry

    lax.fori_loop(0, COLS, column, 0)


def hbm(value):
    return pltpu.with_memory_space_constraint(value, pltpu.HBM)


def far(n):
    return [pl.BlockSpec(memory_space=pl.ANY)] * n


def inward_panels(idx, gate, up):
    return pl.pallas_call(
        inward_panels_kernel,
        in_specs=smem(1) + far(2),
        out_specs=vm(2),
        out_shape=[pltpu.VMEM((FEAT, WIDE), BF), pltpu.VMEM((FEAT, WIDE), BF)],
        scratch_shapes=[
            pltpu.VMEM((2, SLOT, D), BF),
            pltpu.VMEM((2, 256, 256), BF),
            pltpu.SemaphoreType.DMA((2,)),
        ],
        compiler_params=params(14),
        cost_estimate=cost(6),
        name="inward_panels",
    )(idx, hbm(gate), hbm(up))


def outward_panel(idx, down):
    return pl.pallas_call(
        outward_panel_kernel,
        in_specs=smem(1) + far(1),
        out_specs=vm(1)[0],
        out_shape=pltpu.VMEM((256, 2 * D), BF),
        scratch_shapes=[pltpu.VMEM((SLOT, D), BF), pltpu.VMEM((2, 256, 256), BF), pltpu.SemaphoreType.DMA],
        compiler_params=params(10),
        cost_estimate=cost(3),
        name="outward_panel",
    )(idx, hbm(down))


def forward_kernel(t0, t1, t2, t3, pg, pu, pd, xt_own, ht_own, sib, gl2, ul2, out_parts, tok, xx, hid, hh):
    core, _, y = place()
    fsplit = one_hot(rows_of(256), split_index(cols_of(256), 64))
    fturn = one_hot(turn_index(rows_of(256), core, 64), cols_of(256))
    hsplit = one_hot(rows_of(512), split_index(cols_of(256), 128))
    hturn = one_hot(turn_index(rows_of(256), core, 128), cols_of(512))
    for n, piece in enumerate((t0, t1, t2, t3)):
        tok[n * 32:n * 32 + 32, :] = piece[...]
    for c in range(16):
        chunk = tok[:, c * 256:c * 256 + 256]
        split = mm(chunk, fsplit).astype(BF)
        turned = mm_nt(fturn, chunk).astype(BF)
        for p in range(2):
            xx[p * 128:p * 128 + 128, c * 128:c * 128 + 128] = split[:, p * 128:p * 128 + 128]
            at = p * 1024 + c * 64
            xt_own[at:at + 64, :] = turned[p * 64:p * 64 + 64, :]
            sib[at:at + 64, :] = turned[128 + p * 64:128 + p * 64 + 64, :]
    low = low_half((TOK, 128))
    hid[:, WIDE:] = jnp.zeros((TOK, 128), BF)
    for n in range(0, WIDE, 256):
        width = min(256, WIDE - n)
        gate = mm(xx[...], pg[:, n:n + width])
        up = mm(xx[...], pu[:, n:n + width])
        for s in range(0, width, 128):
            cols = slice(n + s, n + s + 128)
            gl = jnp.where(low, gate[:TOK, s:s + 128], gate[TOK:, s:s + 128])
            gl = gl + pltpu.roll(gl, 64, 1)
            ul = jnp.where(low, up[:TOK, s:s + 128], up[TOK:, s:s + 128])
            ul = ul + pltpu.roll(ul, 64, 1)
            gl2[:, cols] = gl
            ul2[:, cols] = ul
            hid[:, cols] = (gl * (1.0 / (1.0 + jnp.exp(-gl))) * ul).astype(BF)
    for g in range(2):
        group = hid[:, g * 512:g * 512 + 512]
        split = mm(group, hsplit).astype(BF)
        turned = mm_nt(hturn, group).astype(BF)
        for p in range(2):
            hh[p * 128:p * 128 + 128, g * 128:g * 128 + 128] = split[:, p * 128:p * 128 + 128]
            at = p * 128 + g * 64
            ht_own[at:at + 64, :] = turned[p * 64:p * 64 + 64, :]
            sib[FEAT + at:FEAT + at + 64, :] = turned[128 + p * 64:128 + p * 64 + 64, :]

    def step(n, carry):
        out = mm(hh[...], pd[:, pl.ds(pl.multiple_of(n * 1024, 1024), 1024)])
        parts = []
        for m in range(4):
            a0, a1 = out[:TOK, m * 256:m * 256 + 128], out[TOK:, m * 256:m * 256 + 128]
            b0, b1 = out[:TOK, m * 256 + 128:m * 256 + 256], out[TOK:, m * 256 + 128:m * 256 + 256]
            parts.append(jnp.where(low, a0, b1) + pltpu.roll(jnp.where(low, b0, a1), 64, 1))
        whole = jnp.concatenate(parts, axis=1).astype(BF)
        for r in range(NY):
            out_parts[lax.rem(y + r, NY), :, pl.ds(pl.multiple_of(n * 512, 512), 512)] = whole[r * 32:r * 32 + 32, :]
        return carry

    lax.fori_loop(0, 8, step, 0)


def forward(pieces, pg, pu, pd):
    lin = pltpu.VMEM((TOK, WIDE), F32)
    return pl.pallas_call(
        forward_kernel,
        in_specs=vm(7),
        out_specs=vm(6),
        out_shape=[
            shape(FEAT, TOK), shape(256, TOK), shape(FEAT + 256, TOK), lin, lin, shape(NY, 32, D)
        ],
        scratch_shapes=[
            pltpu.VMEM((TOK, D), BF),
            pltpu.VMEM((256, FEAT), BF),
            pltpu.VMEM((TOK, 1024), BF),
            pltpu.VMEM((256, 256), BF),
        ],
        compiler_params=params(24),
        cost_estimate=cost(8),
        name="forward",
    )(*pieces, pg, pu, pd)


def emit(wswap, tiles, parts, row):
    turned = mm(wswap, tiles[...]).astype(BF)
    for rel, dst in enumerate(parts):
        for k in range(4):
            top = (rel * 4 + k) * 16
            for half in range(2):
                dst[row + half * 16:row + half * 16 + 16, k * 128:k * 128 + 128] = turned[
                    top:top + 16, half * 128:half * 128 + 128
                ]


def down_kernel(idx, cots, ht_own, sib_oth, w0, w1, w2, w3, both, part, tiles, sems):
    wswap = wire_swap(place()[1])
    def fetch(n):
        lanes = pl.ds(n * 1024, 1024)
        return pltpu.make_async_copy(cots.at[:, lanes], both.at[:, lanes], sems.at[n])

    for n in range(4):
        fetch(n).start()
    hidden = jnp.concatenate([ht_own[...], sib_oth[FEAT:, :]], axis=1)
    for n in range(8):
        if n % 2 == 0:
            fetch(n // 2).wait()
        lanes = slice(n * 512, n * 512 + 512)
        part[:, lanes] = mm(hidden, both[:, lanes]).astype(BF)
    side = lax.broadcasted_iota(jnp.int32, (16, 128), 1) // 64
    for j in range(COLS):
        for q in range(KEEP):
            i = idx[2, j * KEEP + q]
            odd = lax.rem(i, 2)
            lanes = pl.ds(pl.multiple_of((i // 2) * 128, 128), 128)
            near = part[pl.ds(pl.multiple_of(odd * 128 + j * 16, 16), 16), lanes].astype(F32)
            far = part[pl.ds(pl.multiple_of((1 - odd) * 128 + j * 16, 16), 16), lanes].astype(F32)
            tile = jnp.where(side == odd, near, pltpu.roll(far, 64, 1)).astype(BF)
            tiles[j, (q % 16) * 16:(q % 16) * 16 + 16, (q // 16) * 128:(q // 16) * 128 + 128] = tile
        emit(wswap, tiles.at[j], (w0, w1, w2, w3), j * KEEP)


def down_grads(idx, cots, ht_own, sib_oth):
    return pl.pallas_call(
        down_kernel,
        in_specs=smem(1) + far(1) + vm(2),
        out_specs=vm(4),
        out_shape=[pltpu.HBM((SLOT, 512), BF)] * 4,
        scratch_shapes=[
            pltpu.VMEM((256, D), BF),
            pltpu.VMEM((256, D), BF),
            pltpu.VMEM((COLS, 256, 256), BF),
            pltpu.SemaphoreType.DMA((4,)),
        ],
        compiler_params=params(14),
        cost_estimate=cost(0.2),
        name="down_grads",
    )(idx, cots, ht_own, sib_oth)


def back_kernel(c0, c1, c2, c3, d0, d1, d2, d3, pd_far, gl2, ul2, pg_far, pu_far, out_parts,
                own, parts, cots, cx, pd, pg, pu, gdx, udx, ins, sem, panel_sems, part_sems, cot_sems):
    y = place()[2]
    share = pltpu.make_async_copy(out_parts, parts.at[:, :32, :], part_sems.at[4])
    share.start()
    bundle = [
        pltpu.make_async_copy(piece, cots.at[pl.ds(n * 32, 32), :], cot_sems.at[n])
        for n, piece in enumerate((c0, c1, c2, c3, d0, d1, d2, d3))
    ]

    def fetch_panel(n):
        rows = pl.ds(n * 512, 512)
        return [
            pltpu.make_async_copy(far_ref.at[rows, :], near.at[rows, :], panel_sems.at[m, n])
            for m, (far_ref, near) in enumerate(((pg_far, pg), (pu_far, pu)))
        ]

    def fetch(n):
        lanes = pl.ds(n * 1024, 1024)
        return pltpu.make_async_copy(pd_far.at[:, lanes], pd.at[:, lanes], sem.at[n])

    for n in range(8):
        fetch(n).start()
    for n in range(4):
        for copy in fetch_panel(n):
            copy.start()
    for copy in bundle:
        copy.start()
    at = cols_of(512)
    hjoin = one_hot(split_index(rows_of(256), 128), (at >> 7) * 128 + (at & 63))
    low = low_half((32, 128))
    for n, piece in enumerate((c0, c1, c2, c3)):
        top = slice(n * 32, n * 32 + 32)
        bottom = slice(TOK + n * 32, TOK + n * 32 + 32)
        for m in range(32):
            c = piece[:, m * 128:m * 128 + 128].astype(F32)
            rolled = pltpu.roll(c, 64, 1)
            zero = jnp.zeros_like(c)
            first = slice(2 * m * 128, 2 * m * 128 + 128)
            second = slice(2 * m * 128 + 128, 2 * m * 128 + 256)
            cx[top, first] = jnp.where(low, c, zero).astype(BF)
            cx[bottom, first] = jnp.where(low, zero, rolled).astype(BF)
            cx[top, second] = jnp.where(low, rolled, zero).astype(BF)
            cx[bottom, second] = jnp.where(low, zero, c).astype(BF)

    hd = jnp.zeros((256, 256), F32)
    for n in range(8):
        lanes = slice(n * 1024, n * 1024 + 1024)
        fetch(n).wait()
        hd = hd + mm_nt(cx[:, lanes], pd[:, lanes])
    high = hd.astype(BF)
    rest = (hd - high.astype(F32)).astype(BF)
    low = low_half((TOK, 128))
    for g in range(2):
        cols = slice(g * 128, g * 128 + 128)
        joined = sum(
            mm(jnp.concatenate([part[:TOK, cols], part[TOK:, cols]], axis=1), hjoin) for part in (high, rest)
        )
        before = None
        for jl in range(4):
            j = g * 4 + jl
            if j == COLS:
                break
            lanes = slice(j * 128, j * 128 + 128)
            delta = joined[:, jl * 128:jl * 128 + 128]
            gl, ul = gl2[:, lanes], ul2[:, lanes]
            sig = 1.0 / (1.0 + jnp.exp(-gl))
            gd = delta * ul * sig * (1.0 + gl * (1.0 - sig))
            ud = delta * gl * sig
            for dst, val in ((gdx, gd), (udx, ud)):
                dst[:TOK, lanes] = jnp.where(low, val, 0.0).astype(BF)
                dst[TOK:, lanes] = jnp.where(low, 0.0, val).astype(BF)
            pair = slice((j // 2) * 128, (j // 2) * 128 + 128)
            if j % 2:
                own[:TOK, pair] = jnp.where(low, before[0], gd).astype(BF)
                own[TOK:, pair] = jnp.where(low, before[1], ud).astype(BF)
            elif j == COLS - 1:
                own[:TOK, pair] = jnp.where(low, gd, 0.0).astype(BF)
                own[TOK:, pair] = jnp.where(low, ud, 0.0).astype(BF)
            before = (gd, ud)


    fjoin = one_hot(split_index(rows_of(256), 64), cols_of(256))
    sends = []
    for n in range(4):
        for copy in fetch_panel(n):
            copy.wait()
        rows = slice(n * 512, n * 512 + 512)
        acc = (mm_nt(gdx[...], pg[rows, :]) + mm_nt(udx[...], pu[rows, :])).astype(BF)
        for c in range(4):
            cols = slice(c * 128, c * 128 + 128)
            pair = jnp.concatenate([acc[:TOK, cols], acc[TOK:, cols]], axis=1)
            whole = mm(pair, fjoin).astype(BF)
            lanes = slice(n * 1024 + c * 256, n * 1024 + c * 256 + 256)
            for r in range(NY):
                ins[lax.rem(y + r, NY), :, lanes] = whole[r * 32:r * 32 + 32, :]
        lanes = pl.ds(n * 1024, 1024)
        sends.append(pltpu.make_async_copy(ins.at[:, :, lanes], parts.at[:, 32:, lanes], part_sems.at[n]))
        sends[-1].start()
    for copy in sends + bundle + [share]:
        copy.wait()


def backward(pieces, others, pd, gl2, ul2, pg, pu, out_parts):
    return pl.pallas_call(
        back_kernel,
        in_specs=vm(4) + far(5) + vm(2) + far(3),
        out_specs=vm(1) + far(2),
        out_shape=[shape(256, 512), pltpu.HBM((NY, 64, D), BF), pltpu.HBM((256, D), BF)],
        scratch_shapes=[
            pltpu.VMEM((256, 2 * D), BF),
            pltpu.VMEM((256, 2 * D), BF),
            pltpu.VMEM((FEAT, WIDE), BF),
            pltpu.VMEM((FEAT, WIDE), BF),
            pltpu.VMEM((256, WIDE), BF),
            pltpu.VMEM((256, WIDE), BF),
            pltpu.VMEM((NY, 32, D), BF),
            pltpu.SemaphoreType.DMA((8,)),
            pltpu.SemaphoreType.DMA((2, 4)),
            pltpu.SemaphoreType.DMA((5,)),
            pltpu.SemaphoreType.DMA((8,)),
        ],
        compiler_params=params(26),
        cost_estimate=cost(9),
        name="backward",
    )(*pieces, *others, hbm(pd), gl2, ul2, hbm(pg), hbm(pu), out_parts)


def merge_kernel(got, both):
    for n in range(0, D, 512):
        lanes = slice(n, n + 512)
        total = sum(got[r, :, lanes].astype(F32) for r in range(1, NY)) + got[0, :, lanes].astype(F32)
        for z in range(NZ):
            both[z, :, lanes] = jnp.concatenate(
                [total[z * 4:z * 4 + 4], total[32 + z * 4:36 + z * 4]], axis=0
            ).astype(BF)


def merge_y(got):
    return pl.pallas_call(
        merge_kernel,
        in_specs=vm(1),
        out_specs=vm(1)[0],
        out_shape=shape(NZ, 8, D),
        compiler_params=params(10),
        cost_estimate=cost(0.2),
        name="merge_y",
    )(got)


def inward_kernel(idx, xt_own, sib_oth, d_own, d_oth, w0, w1, w2, w3, part, tiles):
    wswap = wire_swap(place()[1])
    low = low_half((16, 128))
    for m in range(2):
        delta = jnp.concatenate([d[m * TOK:m * TOK + TOK, :] for d in (d_own, d_oth)], axis=0)

        def product(n, carry):
            rows = pl.ds(pl.multiple_of(n * 256, 256), 256)
            tokens = jnp.concatenate([xt_own[rows, :], sib_oth[rows, :]], axis=1)
            part[rows, :] = mm(tokens, delta).astype(BF)
            return carry

        lax.fori_loop(0, 8, product, 0)
        for j in range(COLS):
            odd = j % 2
            lanes = slice((j // 2) * 128, (j // 2) * 128 + 128)
            for q in range(KEEP):
                i = idx[m, j * KEEP + q]
                first = part[pl.ds(pl.multiple_of(i * 16, 16), 16), lanes].astype(F32)
                second = part[pl.ds(pl.multiple_of(1024 + i * 16, 16), 16), lanes].astype(F32)
                if odd:
                    first = pltpu.roll(first, 64, 1)
                else:
                    second = pltpu.roll(second, 64, 1)
                tile = jnp.where(low, first, second).astype(BF)
                tiles[j, (q % 16) * 16:(q % 16) * 16 + 16, (q // 16) * 128:(q // 16) * 128 + 128] = tile
            emit(wswap, tiles.at[j], (w0, w1, w2, w3), m * SLOT + j * KEEP)


def inward_grads(idx, xt_own, sib_oth, d_own, d_oth):
    return pl.pallas_call(
        inward_kernel,
        in_specs=smem(1) + vm(4),
        out_specs=vm(4),
        out_shape=[pltpu.HBM((2 * SLOT, 512), BF)] * 4,
        scratch_shapes=[pltpu.VMEM((FEAT, 512), BF), pltpu.VMEM((COLS, 256, 256), BF)],
        compiler_params=params(14),
        cost_estimate=cost(0.2),
        name="inward_grads",
    )(idx, xt_own, sib_oth, d_own, d_oth)


def from_y(value, step):
    pairs = [((y + step) % NY * NZ + z, y * NZ + z) for y in range(NY) for z in range(NZ)]
    return lax.ppermute(value, "fsdp", pairs)


def from_x(value, other):
    pairs = [((x ^ other) * NC + c, x * NC + c) for x in range(NX) for c in range(NC)]
    return lax.ppermute(value, "dp", pairs)


def from_core(value):
    pairs = [(x * NC + 1 - c, x * NC + c) for x in range(NX) for c in range(NC)]
    return lax.ppermute(value, "dp", pairs)


def z_groups():
    return [[y * NZ + z for z in range(NZ)] for y in range(NY)]


def y_groups():
    return [[y * NZ + z for y in range(NY)] for z in range(NZ)]


def over_z(value):
    return lax.all_to_all(value, "fsdp", 0, 0, axis_index_groups=z_groups(), tiled=True)


def over_y(value):
    return lax.all_to_all(value, "fsdp", 0, 0, axis_index_groups=y_groups(), tiled=True)


def copies_over_z(value):
    return over_z(jnp.broadcast_to(value[None], (NZ,) + value.shape))


def after(value, *others):
    return lax.optimization_barrier((value,) + others)[0]


def exchange_x(parts):
    return [parts[0]] + [from_x(parts[d], d) for d in range(1, NX)]


def mean_of(*parts):
    total = sum((p.astype(F32) for p in parts[1:]), parts[0].astype(F32))
    return (total * (1.0 / (NX * NC))).astype(BF)


def inward_mean_kernel(a, b, c, d, gate, up):
    for n, dst in enumerate((gate, up)):
        rows = slice(n * SLOT, n * SLOT + SLOT)
        dst[...] = mean_of(*(p[rows, :] for p in (a, b, c, d)))


def inward_mean(*parts):
    return pl.pallas_call(
        inward_mean_kernel,
        in_specs=vm(4),
        out_specs=vm(2),
        out_shape=[shape(SLOT, 512)] * 2,
        compiler_params=params(10),
        cost_estimate=cost(20),
        name="inward_mean",
    )(*parts)


def body(tokens, cotangent, gate_blocks, up_blocks, down_blocks, block_index):
    rows = tokens.shape[0]
    ring = copies_over_z(jnp.concatenate([tokens, cotangent], axis=0))
    tok_z = ring[:, :rows].reshape(NZ * rows, D)
    cot_z = ring[:, rows:].reshape(NZ * rows, D)
    tok = [tok_z] + [from_y(tok_z, s) for s in range(1, NY)]
    idx = after(block_index, tok_z, cot_z)
    pg, pu = inward_panels(idx, gate_blocks, up_blocks)
    cot_z = after(cot_z, pg)
    pd = outward_panel(idx, down_blocks)
    cot = [cot_z] + [from_y(cot_z, s) for s in range(1, NY)]

    xt_own, ht_own, sib, gl2, ul2, out_parts = forward(tok, pg, pu, pd)
    sib_oth = from_core(after(sib, *cot))
    cot_oth = [from_core(after(c, ht_own)) for c in cot]
    own, parts, cots = backward(cot, cot_oth, pd, after(gl2, sib_oth), ul2, pg, pu, out_parts)
    oth = from_core(own)
    parts_got = over_y(parts)
    down_wire = down_grads(block_index, hbm(cots), after(ht_own, parts), sib_oth)
    down_got = exchange_x(down_wire)
    wire = inward_grads(block_index, xt_own, sib_oth, after(own, down_wire[0]), oth)
    got = exchange_x(wire)
    down_grad = mean_of(*down_got)
    both = merge_y(after(parts_got, wire[0], down_grad))
    gate_grad, up_grad = inward_mean(*got)
    total = after(over_z(both), gate_grad).astype(F32).sum(axis=0).astype(BF)
    return (total[:rows], total[rows:], gate_grad, up_grad, down_grad)


def solution(mesh):
    return jax.shard_map(
        body,
        mesh=mesh,
        in_specs=(
            P(("dp", "fsdp"), None),
            P(("dp", "fsdp"), None),
            P("fsdp", None),
            P("fsdp", None),
            P("fsdp", None),
            P(None, "fsdp"),
        ),
        out_specs=(
            P(("dp", "fsdp"), None),
            P(("dp", "fsdp"), None),
            P("fsdp", "dp"),
            P("fsdp", "dp"),
            P("fsdp", "dp"),
        ),
        check_vma=False,
    )
```

```python
import jax
import jax.numpy as jnp
from jax import lax
from jax.experimental import pallas as pl
from jax.experimental.pallas import tpu as pltpu
from jax.sharding import PartitionSpec as P

D = 4096
BLK = 64
KEEP = 32
COLS = 7
SLOT = COLS * KEEP
TOK = 128
FEAT = 2048
WIDE = COLS * 128
NX, NC, NY, NZ = 4, 2, 4, 8
BF = jnp.bfloat16
F32 = jnp.float32

TILE_ROWS = [[8 * x + 4 * c + k4 for x in range(NX) for k4 in range(4)] for c in range(NC)]


def rows_of(n):
    return lax.broadcasted_iota(jnp.int32, (n, 1), 0)


def cols_of(n):
    return lax.broadcasted_iota(jnp.int32, (1, n), 1)


def one_hot(left, right):
    return jnp.where(left == right, 1.0, 0.0).astype(BF)


def split_index(at, stride):
    k = 8 * ((at >> 2) & 3) + 4 * ((at >> 4) & 1) + (at & 3)
    return ((at >> 5) & 3) * stride + 2 * k + (at >> 7)


def turn_index(at, core, stride):
    k = 8 * ((at >> 2) & 3) + 4 * (core ^ (at >> 7)) + (at & 3)
    return ((at >> 4) & 3) * stride + 2 * k + ((at >> 6) & 1)


def swap_matrix():
    at = cols_of(256)
    return one_hot(rows_of(256), (at & 15) * 16 + (at >> 4))


def wire_swap(x):
    at = rows_of(256)
    return one_hot((at & 15) * 16 + ((at >> 6) ^ x) * 4 + ((at >> 4) & 3), cols_of(256))


def place():
    dp, fsdp = lax.axis_index("dp"), lax.axis_index("fsdp")
    return lax.rem(dp, NC), dp // NC, fsdp // NZ


def mm(a, b):
    return jnp.dot(a, b, preferred_element_type=F32)


def mm_nt(a, b):
    return lax.dot_general(a, b, (((1,), (1,)), ((), ())), preferred_element_type=F32)


def mm_tn(a, b):
    return lax.dot_general(a, b, (((0,), (0,)), ((), ())), preferred_element_type=F32)


def low_half(shape):
    return lax.broadcasted_iota(jnp.int32, shape, 1) < 64


def vm(n):
    return [pl.BlockSpec(memory_space=pltpu.VMEM)] * n


def smem(n):
    return [pl.BlockSpec(memory_space=pltpu.SMEM)] * n


def params(mib):
    return pltpu.CompilerParams(vmem_limit_bytes=mib << 20)


def cost(us):
    return pl.CostEstimate(flops=int(us * 1_000_000_000), bytes_accessed=1000, transcendentals=0)


def shape(*dims, dtype=BF):
    return jax.ShapeDtypeStruct(dims, dtype)


def unfold(src, row, swap):
    rows = pl.ds(pl.multiple_of(row, 16), 16)
    halves = [jnp.concatenate([src[rows, k * 128:k * 128 + 128] for k in TILE_ROWS[c]], axis=0) for c in range(2)]
    return mm(swap, jnp.concatenate(halves, axis=1)).astype(BF)


def inward_panels_kernel(idx, gate, up, pg, pu, held, tiles, sems):
    fetches = [pltpu.make_async_copy(src, held.at[m], sems.at[m]) for m, src in enumerate((gate, up))]
    for fetch in fetches:
        fetch.start()
    swap = swap_matrix()
    for m, dst in enumerate((pg, pu)):
        dst[...] = jnp.zeros_like(dst)
        fetches[m].wait()

        def column(j, carry):
            lanes = pl.ds(pl.multiple_of(j * 128, 128), 128)
            for half in range(2):
                tiles[half, :, :] = unfold(held.at[m], j * KEEP + half * 16, swap)
                for q in range(16):
                    i = idx[m, j * KEEP + half * 16 + q]
                    for c in range(2):
                        dst[pl.ds(pl.multiple_of(i * 32 + c * 16, 16), 16), lanes] = tiles[
                            half, q * 16:q * 16 + 16, c * 128:c * 128 + 128
                        ]
            return carry

        lax.fori_loop(0, COLS, column, 0)


def outward_panel_kernel(idx, down, pd, held, tiles, sem):
    fetch = pltpu.make_async_copy(down, held, sem)
    fetch.start()
    swap = swap_matrix()
    pd[...] = jnp.zeros_like(pd)
    fetch.wait()

    def column(j, carry):
        for half in range(2):
            tiles[half, :, :] = unfold(held, j * KEEP + half * 16, swap)
            for q in range(16):
                i = idx[2, j * KEEP + half * 16 + q]
                for c in range(2):
                    rows = pl.ds(pl.multiple_of(j * 32 + c * 16, 16), 16)
                    pd[rows, pl.ds(pl.multiple_of(i * 128, 128), 128)] = tiles[
                        half, q * 16:q * 16 + 16, c * 128:c * 128 + 128
                    ]
        return carry

    lax.fori_loop(0, COLS, column, 0)


def hbm(value):
    return pltpu.with_memory_space_constraint(value, pltpu.HBM)


def far(n):
    return [pl.BlockSpec(memory_space=pl.ANY)] * n


def inward_panels(idx, gate, up):
    return pl.pallas_call(
        inward_panels_kernel,
        in_specs=smem(1) + far(2),
        out_specs=vm(2),
        out_shape=[pltpu.VMEM((FEAT, WIDE), BF), pltpu.VMEM((FEAT, WIDE), BF)],
        scratch_shapes=[
            pltpu.VMEM((2, SLOT, D), BF),
            pltpu.VMEM((2, 256, 256), BF),
            pltpu.SemaphoreType.DMA((2,)),
        ],
        compiler_params=params(14),
        cost_estimate=cost(6),
        name="inward_panels",
    )(idx, hbm(gate), hbm(up))


def outward_panel(idx, down):
    return pl.pallas_call(
        outward_panel_kernel,
        in_specs=smem(1) + far(1),
        out_specs=vm(1)[0],
        out_shape=pltpu.VMEM((256, 2 * D), BF),
        scratch_shapes=[pltpu.VMEM((SLOT, D), BF), pltpu.VMEM((2, 256, 256), BF), pltpu.SemaphoreType.DMA],
        compiler_params=params(10),
        cost_estimate=cost(3),
        name="outward_panel",
    )(idx, hbm(down))


def forward_kernel(t0, t1, t2, t3, pg, pu, pd, xt_own, ht_own, sib, gl2, ul2, out_parts, tok, xx, hid, hh):
    core, _, y = place()
    fsplit = one_hot(rows_of(256), split_index(cols_of(256), 64))
    fturn = one_hot(turn_index(rows_of(256), core, 64), cols_of(256))
    hsplit = one_hot(rows_of(512), split_index(cols_of(256), 128))
    hturn = one_hot(turn_index(rows_of(256), core, 128), cols_of(512))
    for n, piece in enumerate((t0, t1, t2, t3)):
        tok[n * 32:n * 32 + 32, :] = piece[...]
    for c in range(16):
        chunk = tok[:, c * 256:c * 256 + 256]
        split = mm(chunk, fsplit).astype(BF)
        turned = mm_nt(fturn, chunk).astype(BF)
        for p in range(2):
            xx[p * 128:p * 128 + 128, c * 128:c * 128 + 128] = split[:, p * 128:p * 128 + 128]
            at = p * 1024 + c * 64
            xt_own[at:at + 64, :] = turned[p * 64:p * 64 + 64, :]
            sib[at:at + 64, :] = turned[128 + p * 64:128 + p * 64 + 64, :]
    low = low_half((TOK, 128))
    hid[:, WIDE:] = jnp.zeros((TOK, 128), BF)
    for n in range(0, WIDE, 256):
        width = min(256, WIDE - n)
        gate = mm(xx[...], pg[:, n:n + width])
        up = mm(xx[...], pu[:, n:n + width])
        for s in range(0, width, 128):
            cols = slice(n + s, n + s + 128)
            gl = jnp.where(low, gate[:TOK, s:s + 128], gate[TOK:, s:s + 128])
            gl = gl + pltpu.roll(gl, 64, 1)
            ul = jnp.where(low, up[:TOK, s:s + 128], up[TOK:, s:s + 128])
            ul = ul + pltpu.roll(ul, 64, 1)
            gl2[:, cols] = gl
            ul2[:, cols] = ul
            hid[:, cols] = (gl * (1.0 / (1.0 + jnp.exp(-gl))) * ul).astype(BF)
    for g in range(2):
        group = hid[:, g * 512:g * 512 + 512]
        split = mm(group, hsplit).astype(BF)
        turned = mm_nt(hturn, group).astype(BF)
        for p in range(2):
            hh[p * 128:p * 128 + 128, g * 128:g * 128 + 128] = split[:, p * 128:p * 128 + 128]
            at = p * 128 + g * 64
            ht_own[at:at + 64, :] = turned[p * 64:p * 64 + 64, :]
            sib[FEAT + at:FEAT + at + 64, :] = turned[128 + p * 64:128 + p * 64 + 64, :]

    def step(n, carry):
        out = mm(hh[...], pd[:, pl.ds(pl.multiple_of(n * 1024, 1024), 1024)])
        parts = []
        for m in range(4):
            a0, a1 = out[:TOK, m * 256:m * 256 + 128], out[TOK:, m * 256:m * 256 + 128]
            b0, b1 = out[:TOK, m * 256 + 128:m * 256 + 256], out[TOK:, m * 256 + 128:m * 256 + 256]
            parts.append(jnp.where(low, a0, b1) + pltpu.roll(jnp.where(low, b0, a1), 64, 1))
        whole = jnp.concatenate(parts, axis=1).astype(BF)
        for r in range(NY):
            out_parts[lax.rem(y + r, NY), :, pl.ds(pl.multiple_of(n * 512, 512), 512)] = whole[r * 32:r * 32 + 32, :]
        return carry

    lax.fori_loop(0, 8, step, 0)


def forward(pieces, pg, pu, pd):
    lin = pltpu.VMEM((TOK, WIDE), F32)
    return pl.pallas_call(
        forward_kernel,
        in_specs=vm(7),
        out_specs=vm(6),
        out_shape=[
            shape(FEAT, TOK), shape(256, TOK), shape(FEAT + 256, TOK), lin, lin, shape(NY, 32, D)
        ],
        scratch_shapes=[
            pltpu.VMEM((TOK, D), BF),
            pltpu.VMEM((256, FEAT), BF),
            pltpu.VMEM((TOK, 1024), BF),
            pltpu.VMEM((256, 256), BF),
        ],
        compiler_params=params(24),
        cost_estimate=cost(8),
        name="forward",
    )(*pieces, pg, pu, pd)


def emit(wswap, tiles, parts, row):
    turned = mm(wswap, tiles[...]).astype(BF)
    for rel, dst in enumerate(parts):
        for k in range(4):
            top = (rel * 4 + k) * 16
            for half in range(2):
                dst[row + half * 16:row + half * 16 + 16, k * 128:k * 128 + 128] = turned[
                    top:top + 16, half * 128:half * 128 + 128
                ]


def down_kernel(idx, cots, ht_own, sib_oth, w0, w1, w2, w3, both, part, tiles, sems):
    wswap = wire_swap(place()[1])
    def fetch(n):
        lanes = pl.ds(n * 1024, 1024)
        return pltpu.make_async_copy(cots.at[:, lanes], both.at[:, lanes], sems.at[n])

    for n in range(4):
        fetch(n).start()
    hidden = jnp.concatenate([ht_own[...], sib_oth[FEAT:, :]], axis=1)
    for n in range(8):
        if n % 2 == 0:
            fetch(n // 2).wait()
        lanes = slice(n * 512, n * 512 + 512)
        part[:, lanes] = mm(hidden, both[:, lanes]).astype(BF)
    side = lax.broadcasted_iota(jnp.int32, (16, 128), 1) // 64
    for j in range(COLS):
        for q in range(KEEP):
            i = idx[2, j * KEEP + q]
            odd = lax.rem(i, 2)
            lanes = pl.ds(pl.multiple_of((i // 2) * 128, 128), 128)
            near = part[pl.ds(pl.multiple_of(odd * 128 + j * 16, 16), 16), lanes].astype(F32)
            far = part[pl.ds(pl.multiple_of((1 - odd) * 128 + j * 16, 16), 16), lanes].astype(F32)
            tile = jnp.where(side == odd, near, pltpu.roll(far, 64, 1)).astype(BF)
            tiles[j, (q % 16) * 16:(q % 16) * 16 + 16, (q // 16) * 128:(q // 16) * 128 + 128] = tile
        emit(wswap, tiles.at[j], (w0, w1, w2, w3), j * KEEP)


def down_grads(idx, cots, ht_own, sib_oth):
    return pl.pallas_call(
        down_kernel,
        in_specs=smem(1) + far(1) + vm(2),
        out_specs=vm(4),
        out_shape=[pltpu.HBM((SLOT, 512), BF)] * 4,
        scratch_shapes=[
            pltpu.VMEM((256, D), BF),
            pltpu.VMEM((256, D), BF),
            pltpu.VMEM((COLS, 256, 256), BF),
            pltpu.SemaphoreType.DMA((4,)),
        ],
        compiler_params=params(14),
        cost_estimate=cost(0.2),
        name="down_grads",
    )(idx, cots, ht_own, sib_oth)


def back_kernel(c0, c1, c2, c3, d0, d1, d2, d3, pd, gl2, ul2, pg, pu, out_parts,
                own, parts, cots, cxt, gdt, udt, ins, part_sems, cot_sems):
    y = place()[2]
    at = cols_of(512)
    hjoin = one_hot(split_index(rows_of(256), 128), (at >> 7) * 128 + (at & 63))
    fjoin = one_hot(split_index(rows_of(256), 64), cols_of(256))
    share = pltpu.make_async_copy(out_parts, parts.at[:, :32, :], part_sems.at[4])
    share.start()
    bundle = [
        pltpu.make_async_copy(piece, cots.at[pl.ds(n * 32, 32), :], cot_sems.at[n])
        for n, piece in enumerate((c0, c1, c2, c3, d0, d1, d2, d3))
    ]
    for copy in bundle:
        copy.start()
    zero = jnp.zeros((64, TOK), BF)
    for m in range(32):
        lanes = slice(m * 128, m * 128 + 128)
        turned = jnp.concatenate([c[:, lanes] for c in (c0, c1, c2, c3)], axis=0).T
        for e in range(2):
            row = (2 * m + e) * 128
            half = turned[e * 64:e * 64 + 64, :]
            cxt[row:row + 64, :TOK] = half
            cxt[row:row + 64, TOK:] = zero
            cxt[row + 64:row + 128, :TOK] = zero
            cxt[row + 64:row + 128, TOK:] = half
    hd = mm(pd[...], cxt[...])
    high = hd.astype(BF)
    rest = (hd - high.astype(F32)).astype(BF)
    low = low_half((TOK, 128))
    for g in range(2):
        rows = slice(g * 128, g * 128 + 128)
        joined = sum(
            mm_tn(jnp.concatenate([part[rows, :TOK], part[rows, TOK:]], axis=0), hjoin) for part in (high, rest)
        )
        before = None
        for jl in range(4):
            j = g * 4 + jl
            if j == COLS:
                break
            lanes = slice(j * 128, j * 128 + 128)
            delta = joined[:, jl * 128:jl * 128 + 128]
            gl, ul = gl2[:, lanes], ul2[:, lanes]
            sig = 1.0 / (1.0 + jnp.exp(-gl))
            gd = delta * ul * sig * (1.0 + gl * (1.0 - sig))
            ud = delta * gl * sig
            for dst, val in ((gdt, gd), (udt, ud)):
                turned = val.astype(BF).T
                row = j * 128
                dst[row:row + 64, :TOK] = turned[:64, :]
                dst[row:row + 64, TOK:] = zero
                dst[row + 64:row + 128, :TOK] = zero
                dst[row + 64:row + 128, TOK:] = turned[64:, :]
            pair = slice((j // 2) * 128, (j // 2) * 128 + 128)
            if j % 2:
                own[:TOK, pair] = jnp.where(low, before[0], gd).astype(BF)
                own[TOK:, pair] = jnp.where(low, before[1], ud).astype(BF)
            elif j == COLS - 1:
                own[:TOK, pair] = jnp.where(low, gd, 0.0).astype(BF)
                own[TOK:, pair] = jnp.where(low, ud, 0.0).astype(BF)
            before = (gd, ud)
    sends = []
    for n in range(4):
        rows = slice(n * 512, n * 512 + 512)
        acc = (mm(pg[rows, :], gdt[...]) + mm(pu[rows, :], udt[...])).astype(BF)
        for c in range(4):
            rows = slice(c * 128, c * 128 + 128)
            pair = jnp.concatenate([acc[rows, :TOK], acc[rows, TOK:]], axis=0)
            whole = mm_tn(pair, fjoin).astype(BF)
            lanes = slice(n * 1024 + c * 256, n * 1024 + c * 256 + 256)
            for r in range(NY):
                ins[lax.rem(y + r, NY), :, lanes] = whole[r * 32:r * 32 + 32, :]
        lanes = pl.ds(n * 1024, 1024)
        sends.append(pltpu.make_async_copy(ins.at[:, :, lanes], parts.at[:, 32:, lanes], part_sems.at[n]))
        sends[-1].start()
    for copy in sends + bundle + [share]:
        copy.wait()


def backward(pieces, others, pd, gl2, ul2, pg, pu, out_parts):
    return pl.pallas_call(
        back_kernel,
        in_specs=vm(4) + far(4) + vm(5) + far(1),
        out_specs=vm(1) + far(2),
        out_shape=[shape(256, 512), pltpu.HBM((NY, 64, D), BF), pltpu.HBM((256, D), BF)],
        scratch_shapes=[
            pltpu.VMEM((2 * D, 256), BF),
            pltpu.VMEM((WIDE, 256), BF),
            pltpu.VMEM((WIDE, 256), BF),
            pltpu.VMEM((NY, 32, D), BF),
            pltpu.SemaphoreType.DMA((5,)),
            pltpu.SemaphoreType.DMA((8,)),
        ],
        compiler_params=params(26),
        cost_estimate=cost(9),
        name="backward",
    )(*pieces, *others, pd, gl2, ul2, pg, pu, out_parts)


def merge_kernel(got, both):
    for n in range(0, D, 512):
        lanes = slice(n, n + 512)
        total = sum(got[r, :, lanes].astype(F32) for r in range(1, NY)) + got[0, :, lanes].astype(F32)
        for z in range(NZ):
            both[z, :, lanes] = jnp.concatenate(
                [total[z * 4:z * 4 + 4], total[32 + z * 4:36 + z * 4]], axis=0
            ).astype(BF)


def merge_y(got):
    return pl.pallas_call(
        merge_kernel,
        in_specs=vm(1),
        out_specs=vm(1)[0],
        out_shape=shape(NZ, 8, D),
        compiler_params=params(10),
        cost_estimate=cost(0.2),
        name="merge_y",
    )(got)


def inward_kernel(idx, xt_own, sib_oth, d_own, d_oth, w0, w1, w2, w3, part, tiles):
    wswap = wire_swap(place()[1])
    low = low_half((16, 128))
    for m in range(2):
        delta = jnp.concatenate([d[m * TOK:m * TOK + TOK, :] for d in (d_own, d_oth)], axis=0)

        for n in range(8):
            rows = slice(n * 256, n * 256 + 256)
            tokens = jnp.concatenate([xt_own[rows, :], sib_oth[rows, :]], axis=1)
            part[rows, :] = mm(tokens, delta).astype(BF)
        for j in range(COLS):
            odd = j % 2
            lanes = slice((j // 2) * 128, (j // 2) * 128 + 128)
            for q in range(KEEP):
                i = idx[m, j * KEEP + q]
                first = part[pl.ds(pl.multiple_of(i * 16, 16), 16), lanes].astype(F32)
                second = part[pl.ds(pl.multiple_of(1024 + i * 16, 16), 16), lanes].astype(F32)
                if odd:
                    first = pltpu.roll(first, 64, 1)
                else:
                    second = pltpu.roll(second, 64, 1)
                tile = jnp.where(low, first, second).astype(BF)
                tiles[j, (q % 16) * 16:(q % 16) * 16 + 16, (q // 16) * 128:(q // 16) * 128 + 128] = tile
            emit(wswap, tiles.at[j], (w0, w1, w2, w3), m * SLOT + j * KEEP)


def inward_grads(idx, xt_own, sib_oth, d_own, d_oth):
    return pl.pallas_call(
        inward_kernel,
        in_specs=smem(1) + vm(4),
        out_specs=vm(4),
        out_shape=[pltpu.HBM((2 * SLOT, 512), BF)] * 4,
        scratch_shapes=[pltpu.VMEM((FEAT, 512), BF), pltpu.VMEM((COLS, 256, 256), BF)],
        compiler_params=params(14),
        cost_estimate=cost(0.2),
        name="inward_grads",
    )(idx, xt_own, sib_oth, d_own, d_oth)


def from_y(value, step):
    pairs = [((y + step) % NY * NZ + z, y * NZ + z) for y in range(NY) for z in range(NZ)]
    return lax.ppermute(value, "fsdp", pairs)


def from_x(value, other):
    pairs = [((x ^ other) * NC + c, x * NC + c) for x in range(NX) for c in range(NC)]
    return lax.ppermute(value, "dp", pairs)


def from_core(value):
    pairs = [(x * NC + 1 - c, x * NC + c) for x in range(NX) for c in range(NC)]
    return lax.ppermute(value, "dp", pairs)


def z_groups():
    return [[y * NZ + z for z in range(NZ)] for y in range(NY)]


def y_groups():
    return [[y * NZ + z for y in range(NY)] for z in range(NZ)]


def over_z(value):
    return lax.all_to_all(value, "fsdp", 0, 0, axis_index_groups=z_groups(), tiled=True)


def over_y(value):
    return lax.all_to_all(value, "fsdp", 0, 0, axis_index_groups=y_groups(), tiled=True)


def copies_over_z(value):
    return over_z(jnp.broadcast_to(value[None], (NZ,) + value.shape))


def after(value, *others):
    return lax.optimization_barrier((value,) + others)[0]


def exchange_x(parts):
    return [parts[0]] + [from_x(parts[d], d) for d in range(1, NX)]


def mean_of(*parts):
    total = sum((p.astype(F32) for p in parts[1:]), parts[0].astype(F32))
    return (total * (1.0 / (NX * NC))).astype(BF)


def inward_mean_kernel(a, b, c, d, gate, up):
    for n, dst in enumerate((gate, up)):
        rows = slice(n * SLOT, n * SLOT + SLOT)
        dst[...] = mean_of(*(p[rows, :] for p in (a, b, c, d)))


def inward_mean(*parts):
    return pl.pallas_call(
        inward_mean_kernel,
        in_specs=vm(4),
        out_specs=vm(2),
        out_shape=[shape(SLOT, 512)] * 2,
        compiler_params=params(10),
        cost_estimate=cost(20),
        name="inward_mean",
    )(*parts)


def body(tokens, cotangent, gate_blocks, up_blocks, down_blocks, block_index):
    rows = tokens.shape[0]
    ring = copies_over_z(jnp.concatenate([tokens, cotangent], axis=0))
    tok_z = ring[:, :rows].reshape(NZ * rows, D)
    cot_z = ring[:, rows:].reshape(NZ * rows, D)
    tok = [tok_z] + [from_y(tok_z, s) for s in range(1, NY)]
    idx = after(block_index, tok_z, cot_z)
    pg, pu = inward_panels(idx, gate_blocks, up_blocks)
    cot_z = after(cot_z, pg)
    pd = outward_panel(idx, down_blocks)
    cot = [cot_z] + [from_y(cot_z, s) for s in range(1, NY)]

    xt_own, ht_own, sib, gl2, ul2, out_parts = forward(tok, pg, pu, pd)
    sib_oth = from_core(after(sib, *cot))
    cot_oth = [from_core(after(c, ht_own)) for c in cot]
    own, parts, cots = backward(cot, cot_oth, pd, after(gl2, sib_oth), ul2, pg, pu, out_parts)
    oth = from_core(own)
    parts_got = over_y(parts)
    down_wire = down_grads(block_index, hbm(cots), after(ht_own, parts), sib_oth)
    down_got = exchange_x(down_wire)
    wire = inward_grads(block_index, xt_own, sib_oth, after(own, down_wire[0]), oth)
    got = exchange_x(wire)
    down_grad = mean_of(*down_got)
    both = merge_y(after(parts_got, wire[0], down_grad))
    gate_grad, up_grad = inward_mean(*got)
    total = after(over_z(both), gate_grad).astype(F32).sum(axis=0).astype(BF)
    return (total[:rows], total[rows:], gate_grad, up_grad, down_grad)


def solution(mesh):
    return jax.shard_map(
        body,
        mesh=mesh,
        in_specs=(
            P(("dp", "fsdp"), None),
            P(("dp", "fsdp"), None),
            P("fsdp", None),
            P("fsdp", None),
            P("fsdp", None),
            P(None, "fsdp"),
        ),
        out_specs=(
            P(("dp", "fsdp"), None),
            P(("dp", "fsdp"), None),
            P("fsdp", "dp"),
            P("fsdp", "dp"),
            P("fsdp", "dp"),
        ),
        check_vma=False,
    )
```

```python
import jax
import jax.numpy as jnp
from jax import lax
from jax.experimental import pallas as pl
from jax.experimental.pallas import tpu as pltpu
from jax.sharding import PartitionSpec as P

D = 4096
BLK = 64
KEEP = 32
COLS = 7
SLOT = COLS * KEEP
TOK = 128
FEAT = 2048
WIDE = COLS * 128
NX, NC, NY, NZ = 4, 2, 4, 8
BF = jnp.bfloat16
F32 = jnp.float32

TILE_ROWS = [[8 * x + 4 * c + k4 for x in range(NX) for k4 in range(4)] for c in range(NC)]


def rows_of(n):
    return lax.broadcasted_iota(jnp.int32, (n, 1), 0)


def cols_of(n):
    return lax.broadcasted_iota(jnp.int32, (1, n), 1)


def one_hot(left, right):
    return jnp.where(left == right, 1.0, 0.0).astype(BF)


def split_index(at, stride):
    k = 8 * ((at >> 2) & 3) + 4 * ((at >> 4) & 1) + (at & 3)
    return ((at >> 5) & 3) * stride + 2 * k + (at >> 7)


def turn_index(at, core, stride):
    k = 8 * ((at >> 2) & 3) + 4 * (core ^ (at >> 7)) + (at & 3)
    return ((at >> 4) & 3) * stride + 2 * k + ((at >> 6) & 1)


def swap_matrix():
    at = cols_of(256)
    return one_hot(rows_of(256), (at & 15) * 16 + (at >> 4))


def wire_swap(x):
    at = rows_of(256)
    return one_hot((at & 15) * 16 + ((at >> 6) ^ x) * 4 + ((at >> 4) & 3), cols_of(256))


def place():
    dp, fsdp = lax.axis_index("dp"), lax.axis_index("fsdp")
    return lax.rem(dp, NC), dp // NC, fsdp // NZ


def mm(a, b):
    return jnp.dot(a, b, preferred_element_type=F32)


def mm_nt(a, b):
    return lax.dot_general(a, b, (((1,), (1,)), ((), ())), preferred_element_type=F32)


def mm_tn(a, b):
    return lax.dot_general(a, b, (((0,), (0,)), ((), ())), preferred_element_type=F32)


def low_half(shape):
    return lax.broadcasted_iota(jnp.int32, shape, 1) < 64


def vm(n):
    return [pl.BlockSpec(memory_space=pltpu.VMEM)] * n


def smem(n):
    return [pl.BlockSpec(memory_space=pltpu.SMEM)] * n


def params(mib):
    return pltpu.CompilerParams(vmem_limit_bytes=mib << 20)


def cost(us):
    return pl.CostEstimate(flops=int(us * 1_000_000_000), bytes_accessed=1000, transcendentals=0)


def shape(*dims, dtype=BF):
    return jax.ShapeDtypeStruct(dims, dtype)


def unfold(src, row, swap):
    rows = pl.ds(pl.multiple_of(row, 16), 16)
    halves = [jnp.concatenate([src[rows, k * 128:k * 128 + 128] for k in TILE_ROWS[c]], axis=0) for c in range(2)]
    return mm(swap, jnp.concatenate(halves, axis=1)).astype(BF)


def inward_panels_kernel(idx, gate, up, pg, pu, held, tiles, sems):
    fetches = [pltpu.make_async_copy(src, held.at[m], sems.at[m]) for m, src in enumerate((gate, up))]
    for fetch in fetches:
        fetch.start()
    swap = swap_matrix()
    for m, dst in enumerate((pg, pu)):
        dst[...] = jnp.zeros_like(dst)
        fetches[m].wait()

        def column(j, carry):
            lanes = pl.ds(pl.multiple_of(j * 128, 128), 128)
            for half in range(2):
                tiles[half, :, :] = unfold(held.at[m], j * KEEP + half * 16, swap)
                for q in range(16):
                    i = idx[m, j * KEEP + half * 16 + q]
                    for c in range(2):
                        dst[pl.ds(pl.multiple_of(i * 32 + c * 16, 16), 16), lanes] = tiles[
                            half, q * 16:q * 16 + 16, c * 128:c * 128 + 128
                        ]
            return carry

        lax.fori_loop(0, COLS, column, 0)


def outward_panel_kernel(idx, down, pd, held, tiles, sem):
    fetch = pltpu.make_async_copy(down, held, sem)
    fetch.start()
    swap = swap_matrix()
    pd[...] = jnp.zeros_like(pd)
    fetch.wait()

    def column(j, carry):
        for half in range(2):
            tiles[half, :, :] = unfold(held, j * KEEP + half * 16, swap)
            for q in range(16):
                i = idx[2, j * KEEP + half * 16 + q]
                for c in range(2):
                    rows = pl.ds(pl.multiple_of(j * 32 + c * 16, 16), 16)
                    pd[rows, pl.ds(pl.multiple_of(i * 128, 128), 128)] = tiles[
                        half, q * 16:q * 16 + 16, c * 128:c * 128 + 128
                    ]
        return carry

    lax.fori_loop(0, COLS, column, 0)


def hbm(value):
    return pltpu.with_memory_space_constraint(value, pltpu.HBM)


def far(n):
    return [pl.BlockSpec(memory_space=pl.ANY)] * n


def inward_panels(idx, gate, up):
    return pl.pallas_call(
        inward_panels_kernel,
        in_specs=smem(1) + far(2),
        out_specs=vm(2),
        out_shape=[pltpu.VMEM((FEAT, WIDE), BF), pltpu.VMEM((FEAT, WIDE), BF)],
        scratch_shapes=[
            pltpu.VMEM((2, SLOT, D), BF),
            pltpu.VMEM((2, 256, 256), BF),
            pltpu.SemaphoreType.DMA((2,)),
        ],
        compiler_params=params(14),
        cost_estimate=cost(6),
        name="inward_panels",
    )(idx, hbm(gate), hbm(up))


def outward_panel(idx, down):
    return pl.pallas_call(
        outward_panel_kernel,
        in_specs=smem(1) + far(1),
        out_specs=vm(1)[0],
        out_shape=pltpu.VMEM((256, 2 * D), BF),
        scratch_shapes=[pltpu.VMEM((SLOT, D), BF), pltpu.VMEM((2, 256, 256), BF), pltpu.SemaphoreType.DMA],
        compiler_params=params(10),
        cost_estimate=cost(3),
        name="outward_panel",
    )(idx, hbm(down))


def forward_kernel(t0, t1, t2, t3, pg, pu, pd, xt_own, ht_own, sib, gl2, ul2, out_parts, tok, xx, hid, hh):
    core, _, y = place()
    fsplit = one_hot(rows_of(256), split_index(cols_of(256), 64))
    fturn = one_hot(turn_index(rows_of(256), core, 64), cols_of(256))
    hsplit = one_hot(rows_of(512), split_index(cols_of(256), 128))
    hturn = one_hot(turn_index(rows_of(256), core, 128), cols_of(512))
    for n, piece in enumerate((t0, t1, t2, t3)):
        tok[n * 32:n * 32 + 32, :] = piece[...]
    for c in range(16):
        chunk = tok[:, c * 256:c * 256 + 256]
        split = mm(chunk, fsplit).astype(BF)
        turned = mm_nt(fturn, chunk).astype(BF)
        for p in range(2):
            xx[p * 128:p * 128 + 128, c * 128:c * 128 + 128] = split[:, p * 128:p * 128 + 128]
            at = p * 1024 + c * 64
            xt_own[at:at + 64, :] = turned[p * 64:p * 64 + 64, :]
            sib[at:at + 64, :] = turned[128 + p * 64:128 + p * 64 + 64, :]
    low = low_half((TOK, 128))
    hid[:, WIDE:] = jnp.zeros((TOK, 128), BF)
    for n in range(0, WIDE, 256):
        width = min(256, WIDE - n)
        gate = mm(xx[...], pg[:, n:n + width])
        up = mm(xx[...], pu[:, n:n + width])
        for s in range(0, width, 128):
            cols = slice(n + s, n + s + 128)
            gl = jnp.where(low, gate[:TOK, s:s + 128], gate[TOK:, s:s + 128])
            gl = gl + pltpu.roll(gl, 64, 1)
            ul = jnp.where(low, up[:TOK, s:s + 128], up[TOK:, s:s + 128])
            ul = ul + pltpu.roll(ul, 64, 1)
            gl2[:, cols] = gl
            ul2[:, cols] = ul
            hid[:, cols] = (gl * (1.0 / (1.0 + jnp.exp(-gl))) * ul).astype(BF)
    for g in range(2):
        group = hid[:, g * 512:g * 512 + 512]
        split = mm(group, hsplit).astype(BF)
        turned = mm_nt(hturn, group).astype(BF)
        for p in range(2):
            hh[p * 128:p * 128 + 128, g * 128:g * 128 + 128] = split[:, p * 128:p * 128 + 128]
            at = p * 128 + g * 64
            ht_own[at:at + 64, :] = turned[p * 64:p * 64 + 64, :]
            sib[FEAT + at:FEAT + at + 64, :] = turned[128 + p * 64:128 + p * 64 + 64, :]

    def step(n, carry):
        out = mm(hh[...], pd[:, pl.ds(pl.multiple_of(n * 1024, 1024), 1024)])
        parts = []
        for m in range(4):
            a0, a1 = out[:TOK, m * 256:m * 256 + 128], out[TOK:, m * 256:m * 256 + 128]
            b0, b1 = out[:TOK, m * 256 + 128:m * 256 + 256], out[TOK:, m * 256 + 128:m * 256 + 256]
            parts.append(jnp.where(low, a0, b1) + pltpu.roll(jnp.where(low, b0, a1), 64, 1))
        whole = jnp.concatenate(parts, axis=1).astype(BF)
        for r in range(NY):
            out_parts[lax.rem(y + r, NY), :, pl.ds(pl.multiple_of(n * 512, 512), 512)] = whole[r * 32:r * 32 + 32, :]
        return carry

    lax.fori_loop(0, 8, step, 0)


def forward(pieces, pg, pu, pd):
    lin = pltpu.VMEM((TOK, WIDE), F32)
    return pl.pallas_call(
        forward_kernel,
        in_specs=vm(7),
        out_specs=vm(6),
        out_shape=[
            shape(FEAT, TOK), shape(256, TOK), shape(FEAT + 256, TOK), lin, lin, shape(NY, 32, D)
        ],
        scratch_shapes=[
            pltpu.VMEM((TOK, D), BF),
            pltpu.VMEM((256, FEAT), BF),
            pltpu.VMEM((TOK, 1024), BF),
            pltpu.VMEM((256, 256), BF),
        ],
        compiler_params=params(24),
        cost_estimate=cost(8),
        name="forward",
    )(*pieces, pg, pu, pd)


def emit(wswap, tiles, parts, row):
    turned = mm(wswap, tiles[...]).astype(BF)
    for rel, dst in enumerate(parts):
        for k in range(4):
            top = (rel * 4 + k) * 16
            for half in range(2):
                dst[row + half * 16:row + half * 16 + 16, k * 128:k * 128 + 128] = turned[
                    top:top + 16, half * 128:half * 128 + 128
                ]


def down_kernel(idx, cots, ht_own, sib_oth, w0, w1, w2, w3, both, part, tiles, sems):
    wswap = wire_swap(place()[1])
    def fetch(n):
        lanes = pl.ds(n * 1024, 1024)
        return pltpu.make_async_copy(cots.at[:, lanes], both.at[:, lanes], sems.at[n])

    for n in range(4):
        fetch(n).start()
    hidden = jnp.concatenate([ht_own[...], sib_oth[FEAT:, :]], axis=1)
    for n in range(8):
        if n % 2 == 0:
            fetch(n // 2).wait()
        lanes = slice(n * 512, n * 512 + 512)
        part[:, lanes] = mm(hidden, both[:, lanes]).astype(BF)
    side = lax.broadcasted_iota(jnp.int32, (16, 128), 1) // 64
    for j in range(COLS):
        for q in range(KEEP):
            i = idx[2, j * KEEP + q]
            odd = lax.rem(i, 2)
            lanes = pl.ds(pl.multiple_of((i // 2) * 128, 128), 128)
            near = part[pl.ds(pl.multiple_of(odd * 128 + j * 16, 16), 16), lanes].astype(F32)
            far = part[pl.ds(pl.multiple_of((1 - odd) * 128 + j * 16, 16), 16), lanes].astype(F32)
            tile = jnp.where(side == odd, near, pltpu.roll(far, 64, 1)).astype(BF)
            tiles[j, (q % 16) * 16:(q % 16) * 16 + 16, (q // 16) * 128:(q // 16) * 128 + 128] = tile
        emit(wswap, tiles.at[j], (w0, w1, w2, w3), j * KEEP)


def down_grads(idx, cots, ht_own, sib_oth):
    return pl.pallas_call(
        down_kernel,
        in_specs=smem(1) + far(1) + vm(2),
        out_specs=vm(4),
        out_shape=[pltpu.HBM((SLOT, 512), BF)] * 4,
        scratch_shapes=[
            pltpu.VMEM((256, D), BF),
            pltpu.VMEM((256, D), BF),
            pltpu.VMEM((COLS, 256, 256), BF),
            pltpu.SemaphoreType.DMA((4,)),
        ],
        compiler_params=params(14),
        cost_estimate=cost(0.2),
        name="down_grads",
    )(idx, cots, ht_own, sib_oth)


def back_kernel(c0, c1, c2, c3, d0, d1, d2, d3, pd, gl2, ul2, pg, pu, out_parts,
                own, parts, cots, cxt, gdt, udt, ins, part_sems, cot_sems):
    y = place()[2]
    at = cols_of(512)
    hjoin = one_hot(split_index(rows_of(256), 128), (at >> 7) * 128 + (at & 63))
    fjoin = one_hot(split_index(rows_of(256), 64), cols_of(256))
    share = pltpu.make_async_copy(out_parts, parts.at[:, :32, :], part_sems.at[4])
    share.start()
    bundle = [
        pltpu.make_async_copy(piece, cots.at[pl.ds(n * 32, 32), :], cot_sems.at[n])
        for n, piece in enumerate((c0, c1, c2, c3, d0, d1, d2, d3))
    ]
    for copy in bundle:
        copy.start()
    zero = jnp.zeros((64, TOK), BF)
    for m in range(32):
        lanes = slice(m * 128, m * 128 + 128)
        turned = jnp.concatenate([c[:, lanes] for c in (c0, c1, c2, c3)], axis=0).T
        for e in range(2):
            row = (2 * m + e) * 128
            half = turned[e * 64:e * 64 + 64, :]
            cxt[row:row + 64, :TOK] = half
            cxt[row:row + 64, TOK:] = zero
            cxt[row + 64:row + 128, :TOK] = zero
            cxt[row + 64:row + 128, TOK:] = half
    hd = mm(pd[...], cxt[...])
    high = hd.astype(BF)
    rest = (hd - high.astype(F32)).astype(BF)
    low = low_half((TOK, 128))
    for g in range(2):
        rows = slice(g * 128, g * 128 + 128)
        joined = sum(
            mm_tn(jnp.concatenate([part[rows, :TOK], part[rows, TOK:]], axis=0), hjoin) for part in (high, rest)
        )
        before = None
        for jl in range(4):
            j = g * 4 + jl
            if j == COLS:
                break
            lanes = slice(j * 128, j * 128 + 128)
            delta = joined[:, jl * 128:jl * 128 + 128]
            gl, ul = gl2[:, lanes], ul2[:, lanes]
            sig = 1.0 / (1.0 + jnp.exp(-gl))
            gd = delta * ul * sig * (1.0 + gl * (1.0 - sig))
            ud = delta * gl * sig
            for dst, val in ((gdt, gd), (udt, ud)):
                turned = val.astype(BF).T
                row = j * 128
                dst[row:row + 64, :TOK] = turned[:64, :]
                dst[row:row + 64, TOK:] = zero
                dst[row + 64:row + 128, :TOK] = zero
                dst[row + 64:row + 128, TOK:] = turned[64:, :]
            pair = slice((j // 2) * 128, (j // 2) * 128 + 128)
            if j % 2:
                own[:TOK, pair] = jnp.where(low, before[0], gd).astype(BF)
                own[TOK:, pair] = jnp.where(low, before[1], ud).astype(BF)
            elif j == COLS - 1:
                own[:TOK, pair] = jnp.where(low, gd, 0.0).astype(BF)
                own[TOK:, pair] = jnp.where(low, ud, 0.0).astype(BF)
            before = (gd, ud)
    sends = []
    for n in range(4):
        rows = slice(n * 512, n * 512 + 512)
        acc = (mm(pg[rows, :], gdt[...]) + mm(pu[rows, :], udt[...])).astype(BF)
        turned = acc.T
        pairs = [
            jnp.concatenate([turned[p * TOK:p * TOK + TOK, c * 128:c * 128 + 128] for p in range(2)], axis=1)
            for c in range(4)
        ]
        whole = mm(jnp.concatenate(pairs, axis=0), fjoin).astype(BF)
        for c in range(4):
            lanes = slice(n * 1024 + c * 256, n * 1024 + c * 256 + 256)
            for r in range(NY):
                ins[lax.rem(y + r, NY), :, lanes] = whole[c * TOK + r * 32:c * TOK + r * 32 + 32, :]
        lanes = pl.ds(n * 1024, 1024)
        sends.append(pltpu.make_async_copy(ins.at[:, :, lanes], parts.at[:, 32:, lanes], part_sems.at[n]))
        sends[-1].start()
    for copy in sends + bundle + [share]:
        copy.wait()


def backward(pieces, others, pd, gl2, ul2, pg, pu, out_parts):
    return pl.pallas_call(
        back_kernel,
        in_specs=vm(4) + far(4) + vm(5) + far(1),
        out_specs=vm(1) + far(2),
        out_shape=[shape(256, 512), pltpu.HBM((NY, 64, D), BF), pltpu.HBM((256, D), BF)],
        scratch_shapes=[
            pltpu.VMEM((2 * D, 256), BF),
            pltpu.VMEM((WIDE, 256), BF),
            pltpu.VMEM((WIDE, 256), BF),
            pltpu.VMEM((NY, 32, D), BF),
            pltpu.SemaphoreType.DMA((5,)),
            pltpu.SemaphoreType.DMA((8,)),
        ],
        compiler_params=params(26),
        cost_estimate=cost(9),
        name="backward",
    )(*pieces, *others, pd, gl2, ul2, pg, pu, out_parts)


def merge_kernel(got, both):
    for n in range(0, D, 512):
        lanes = slice(n, n + 512)
        total = sum(got[r, :, lanes].astype(F32) for r in range(1, NY)) + got[0, :, lanes].astype(F32)
        for z in range(NZ):
            both[z, :, lanes] = jnp.concatenate(
                [total[z * 4:z * 4 + 4], total[32 + z * 4:36 + z * 4]], axis=0
            ).astype(BF)


def merge_y(got):
    return pl.pallas_call(
        merge_kernel,
        in_specs=vm(1),
        out_specs=vm(1)[0],
        out_shape=shape(NZ, 8, D),
        compiler_params=params(10),
        cost_estimate=cost(0.2),
        name="merge_y",
    )(got)


def inward_kernel(idx, xt_own, sib_oth, d_own, d_oth, w0, w1, w2, w3, part, tiles):
    wswap = wire_swap(place()[1])
    low = low_half((16, 128))
    for m in range(2):
        delta = jnp.concatenate([d[m * TOK:m * TOK + TOK, :] for d in (d_own, d_oth)], axis=0)

        for n in range(8):
            rows = slice(n * 256, n * 256 + 256)
            tokens = jnp.concatenate([xt_own[rows, :], sib_oth[rows, :]], axis=1)
            part[rows, :] = mm(tokens, delta).astype(BF)
        for j in range(COLS):
            odd = j % 2
            lanes = slice((j // 2) * 128, (j // 2) * 128 + 128)
            for q in range(KEEP):
                i = idx[m, j * KEEP + q]
                first = part[pl.ds(pl.multiple_of(i * 16, 16), 16), lanes].astype(F32)
                second = part[pl.ds(pl.multiple_of(1024 + i * 16, 16), 16), lanes].astype(F32)
                if odd:
                    first = pltpu.roll(first, 64, 1)
                else:
                    second = pltpu.roll(second, 64, 1)
                tile = jnp.where(low, first, second).astype(BF)
                tiles[j, (q % 16) * 16:(q % 16) * 16 + 16, (q // 16) * 128:(q // 16) * 128 + 128] = tile
            emit(wswap, tiles.at[j], (w0, w1, w2, w3), m * SLOT + j * KEEP)


def inward_grads(idx, xt_own, sib_oth, d_own, d_oth):
    return pl.pallas_call(
        inward_kernel,
        in_specs=smem(1) + vm(4),
        out_specs=vm(4),
        out_shape=[pltpu.HBM((2 * SLOT, 512), BF)] * 4,
        scratch_shapes=[pltpu.VMEM((FEAT, 512), BF), pltpu.VMEM((COLS, 256, 256), BF)],
        compiler_params=params(14),
        cost_estimate=cost(0.2),
        name="inward_grads",
    )(idx, xt_own, sib_oth, d_own, d_oth)


def from_y(value, step):
    pairs = [((y + step) % NY * NZ + z, y * NZ + z) for y in range(NY) for z in range(NZ)]
    return lax.ppermute(value, "fsdp", pairs)


def from_x(value, other):
    pairs = [((x ^ other) * NC + c, x * NC + c) for x in range(NX) for c in range(NC)]
    return lax.ppermute(value, "dp", pairs)


def from_core(value):
    pairs = [(x * NC + 1 - c, x * NC + c) for x in range(NX) for c in range(NC)]
    return lax.ppermute(value, "dp", pairs)


def z_groups():
    return [[y * NZ + z for z in range(NZ)] for y in range(NY)]


def y_groups():
    return [[y * NZ + z for y in range(NY)] for z in range(NZ)]


def over_z(value):
    return lax.all_to_all(value, "fsdp", 0, 0, axis_index_groups=z_groups(), tiled=True)


def over_y(value):
    return lax.all_to_all(value, "fsdp", 0, 0, axis_index_groups=y_groups(), tiled=True)


def copies_over_z(value):
    return over_z(jnp.broadcast_to(value[None], (NZ,) + value.shape))


def after(value, *others):
    return lax.optimization_barrier((value,) + others)[0]


def exchange_x(parts):
    return [parts[0]] + [from_x(parts[d], d) for d in range(1, NX)]


def mean_of(*parts):
    total = sum((p.astype(F32) for p in parts[1:]), parts[0].astype(F32))
    return (total * (1.0 / (NX * NC))).astype(BF)


def inward_mean_kernel(a, b, c, d, gate, up):
    for n, dst in enumerate((gate, up)):
        rows = slice(n * SLOT, n * SLOT + SLOT)
        dst[...] = mean_of(*(p[rows, :] for p in (a, b, c, d)))


def inward_mean(*parts):
    return pl.pallas_call(
        inward_mean_kernel,
        in_specs=vm(4),
        out_specs=vm(2),
        out_shape=[shape(SLOT, 512)] * 2,
        compiler_params=params(10),
        cost_estimate=cost(20),
        name="inward_mean",
    )(*parts)


def body(tokens, cotangent, gate_blocks, up_blocks, down_blocks, block_index):
    rows = tokens.shape[0]
    ring = copies_over_z(jnp.concatenate([tokens, cotangent], axis=0))
    tok_z = ring[:, :rows].reshape(NZ * rows, D)
    cot_z = ring[:, rows:].reshape(NZ * rows, D)
    tok = [tok_z] + [from_y(tok_z, s) for s in range(1, NY)]
    idx = after(block_index, tok_z, cot_z)
    pg, pu = inward_panels(idx, gate_blocks, up_blocks)
    cot_z = after(cot_z, pg)
    pd = outward_panel(idx, down_blocks)
    cot = [cot_z] + [from_y(cot_z, s) for s in range(1, NY)]

    xt_own, ht_own, sib, gl2, ul2, out_parts = forward(tok, pg, pu, pd)
    sib_oth = from_core(after(sib, *cot))
    cot_oth = [from_core(after(c, ht_own)) for c in cot]
    own, parts, cots = backward(cot, cot_oth, pd, after(gl2, sib_oth), ul2, pg, pu, out_parts)
    oth = from_core(own)
    parts_got = over_y(parts)
    down_wire = down_grads(block_index, hbm(cots), after(ht_own, parts), sib_oth)
    down_got = exchange_x(down_wire)
    wire = inward_grads(block_index, xt_own, sib_oth, after(own, down_wire[0]), oth)
    got = exchange_x(wire)
    down_grad = mean_of(*down_got)
    both = merge_y(after(parts_got, wire[0], down_grad))
    gate_grad, up_grad = inward_mean(*got)
    total = after(over_z(both), gate_grad).astype(F32).sum(axis=0).astype(BF)
    return (total[:rows], total[rows:], gate_grad, up_grad, down_grad)


def solution(mesh):
    return jax.shard_map(
        body,
        mesh=mesh,
        in_specs=(
            P(("dp", "fsdp"), None),
            P(("dp", "fsdp"), None),
            P("fsdp", None),
            P("fsdp", None),
            P("fsdp", None),
            P(None, "fsdp"),
        ),
        out_specs=(
            P(("dp", "fsdp"), None),
            P(("dp", "fsdp"), None),
            P("fsdp", "dp"),
            P("fsdp", "dp"),
            P("fsdp", "dp"),
        ),
        check_vma=False,
    )
```

```python
import jax
import jax.numpy as jnp
from jax import lax
from jax.experimental import pallas as pl
from jax.experimental.pallas import tpu as pltpu
from jax.sharding import PartitionSpec as P

D = 4096
BLK = 64
KEEP = 32
COLS = 7
SLOT = COLS * KEEP
TOK = 128
FEAT = 2048
WIDE = COLS * 128
NX, NC, NY, NZ = 4, 2, 4, 8
BF = jnp.bfloat16
F32 = jnp.float32

TILE_ROWS = [[8 * x + 4 * c + k4 for x in range(NX) for k4 in range(4)] for c in range(NC)]


def rows_of(n):
    return lax.broadcasted_iota(jnp.int32, (n, 1), 0)


def cols_of(n):
    return lax.broadcasted_iota(jnp.int32, (1, n), 1)


def one_hot(left, right):
    return jnp.where(left == right, 1.0, 0.0).astype(BF)


def split_index(at, stride):
    k = 8 * ((at >> 2) & 3) + 4 * ((at >> 4) & 1) + (at & 3)
    return ((at >> 5) & 3) * stride + 2 * k + (at >> 7)


def turn_index(at, core, stride):
    k = 8 * ((at >> 2) & 3) + 4 * (core ^ (at >> 7)) + (at & 3)
    return ((at >> 4) & 3) * stride + 2 * k + ((at >> 6) & 1)


def swap_matrix():
    at = cols_of(256)
    return one_hot(rows_of(256), (at & 15) * 16 + (at >> 4))


def wire_swap(x):
    at = rows_of(256)
    return one_hot((at & 15) * 16 + ((at >> 6) ^ x) * 4 + ((at >> 4) & 3), cols_of(256))


def place():
    dp, fsdp = lax.axis_index("dp"), lax.axis_index("fsdp")
    return lax.rem(dp, NC), dp // NC, fsdp // NZ


def mm(a, b):
    return jnp.dot(a, b, preferred_element_type=F32)


def mm_nt(a, b):
    return lax.dot_general(a, b, (((1,), (1,)), ((), ())), preferred_element_type=F32)


def mm_tn(a, b):
    return lax.dot_general(a, b, (((0,), (0,)), ((), ())), preferred_element_type=F32)


def low_half(shape):
    return lax.broadcasted_iota(jnp.int32, shape, 1) < 64


def vm(n):
    return [pl.BlockSpec(memory_space=pltpu.VMEM)] * n


def smem(n):
    return [pl.BlockSpec(memory_space=pltpu.SMEM)] * n


def params(mib):
    return pltpu.CompilerParams(vmem_limit_bytes=mib << 20)


def cost(us):
    return pl.CostEstimate(flops=int(us * 1_000_000_000), bytes_accessed=1000, transcendentals=0)


def shape(*dims, dtype=BF):
    return jax.ShapeDtypeStruct(dims, dtype)


def unfold(src, row, swap):
    rows = pl.ds(pl.multiple_of(row, 16), 16)
    halves = [jnp.concatenate([src[rows, k * 128:k * 128 + 128] for k in TILE_ROWS[c]], axis=0) for c in range(2)]
    return mm(swap, jnp.concatenate(halves, axis=1)).astype(BF)


def inward_panels_kernel(idx, gate, up, pg, pu, held, tiles, sems):
    fetches = [pltpu.make_async_copy(src, held.at[m], sems.at[m]) for m, src in enumerate((gate, up))]
    for fetch in fetches:
        fetch.start()
    swap = swap_matrix()
    for m, dst in enumerate((pg, pu)):
        dst[...] = jnp.zeros_like(dst)
        fetches[m].wait()

        def column(j, carry):
            lanes = pl.ds(pl.multiple_of(j * 128, 128), 128)
            for half in range(2):
                tiles[half, :, :] = unfold(held.at[m], j * KEEP + half * 16, swap)
                for q in range(16):
                    i = idx[m, j * KEEP + half * 16 + q]
                    for c in range(2):
                        dst[pl.ds(pl.multiple_of(i * 32 + c * 16, 16), 16), lanes] = tiles[
                            half, q * 16:q * 16 + 16, c * 128:c * 128 + 128
                        ]
            return carry

        lax.fori_loop(0, COLS, column, 0)


def outward_panel_kernel(idx, down, pd, held, tiles, sem):
    fetch = pltpu.make_async_copy(down, held, sem)
    fetch.start()
    swap = swap_matrix()
    pd[...] = jnp.zeros_like(pd)
    fetch.wait()

    def column(j, carry):
        for half in range(2):
            tiles[half, :, :] = unfold(held, j * KEEP + half * 16, swap)
            for q in range(16):
                i = idx[2, j * KEEP + half * 16 + q]
                for c in range(2):
                    rows = pl.ds(pl.multiple_of(j * 32 + c * 16, 16), 16)
                    pd[rows, pl.ds(pl.multiple_of(i * 128, 128), 128)] = tiles[
                        half, q * 16:q * 16 + 16, c * 128:c * 128 + 128
                    ]
        return carry

    lax.fori_loop(0, COLS, column, 0)


def hbm(value):
    return pltpu.with_memory_space_constraint(value, pltpu.HBM)


def far(n):
    return [pl.BlockSpec(memory_space=pl.ANY)] * n


def inward_panels(idx, gate, up):
    return pl.pallas_call(
        inward_panels_kernel,
        in_specs=smem(1) + far(2),
        out_specs=vm(2),
        out_shape=[pltpu.VMEM((FEAT, WIDE), BF), pltpu.VMEM((FEAT, WIDE), BF)],
        scratch_shapes=[
            pltpu.VMEM((2, SLOT, D), BF),
            pltpu.VMEM((2, 256, 256), BF),
            pltpu.SemaphoreType.DMA((2,)),
        ],
        compiler_params=params(14),
        cost_estimate=cost(6),
        name="inward_panels",
    )(idx, hbm(gate), hbm(up))


def outward_panel(idx, down):
    return pl.pallas_call(
        outward_panel_kernel,
        in_specs=smem(1) + far(1),
        out_specs=vm(1)[0],
        out_shape=pltpu.VMEM((256, 2 * D), BF),
        scratch_shapes=[pltpu.VMEM((SLOT, D), BF), pltpu.VMEM((2, 256, 256), BF), pltpu.SemaphoreType.DMA],
        compiler_params=params(10),
        cost_estimate=cost(3),
        name="outward_panel",
    )(idx, hbm(down))


def forward_kernel(t0, t1, t2, t3, pg, pu, pd, xt_own, ht_own, sib, gl2, ul2, out_parts, tok, xx, hid, hh):
    core, _, y = place()
    fsplit = one_hot(rows_of(256), split_index(cols_of(256), 64))
    fturn = one_hot(turn_index(rows_of(256), core, 64), cols_of(256))
    hsplit = one_hot(rows_of(512), split_index(cols_of(256), 128))
    hturn = one_hot(turn_index(rows_of(256), core, 128), cols_of(512))
    for n, piece in enumerate((t0, t1, t2, t3)):
        tok[n * 32:n * 32 + 32, :] = piece[...]
    for c in range(16):
        chunk = tok[:, c * 256:c * 256 + 256]
        split = mm(chunk, fsplit).astype(BF)
        turned = mm_nt(fturn, chunk).astype(BF)
        for p in range(2):
            xx[p * 128:p * 128 + 128, c * 128:c * 128 + 128] = split[:, p * 128:p * 128 + 128]
            at = p * 1024 + c * 64
            xt_own[at:at + 64, :] = turned[p * 64:p * 64 + 64, :]
            sib[at:at + 64, :] = turned[128 + p * 64:128 + p * 64 + 64, :]
    low = low_half((TOK, 128))
    hid[:, WIDE:] = jnp.zeros((TOK, 128), BF)
    for n in range(0, WIDE, 256):
        width = min(256, WIDE - n)
        gate = mm(xx[...], pg[:, n:n + width])
        up = mm(xx[...], pu[:, n:n + width])
        for s in range(0, width, 128):
            cols = slice(n + s, n + s + 128)
            gl = jnp.where(low, gate[:TOK, s:s + 128], gate[TOK:, s:s + 128])
            gl = gl + pltpu.roll(gl, 64, 1)
            ul = jnp.where(low, up[:TOK, s:s + 128], up[TOK:, s:s + 128])
            ul = ul + pltpu.roll(ul, 64, 1)
            gl2[:, cols] = gl
            ul2[:, cols] = ul
            hid[:, cols] = (gl * (1.0 / (1.0 + jnp.exp(-gl))) * ul).astype(BF)
    for g in range(2):
        group = hid[:, g * 512:g * 512 + 512]
        split = mm(group, hsplit).astype(BF)
        turned = mm_nt(hturn, group).astype(BF)
        for p in range(2):
            hh[p * 128:p * 128 + 128, g * 128:g * 128 + 128] = split[:, p * 128:p * 128 + 128]
            at = p * 128 + g * 64
            ht_own[at:at + 64, :] = turned[p * 64:p * 64 + 64, :]
            sib[FEAT + at:FEAT + at + 64, :] = turned[128 + p * 64:128 + p * 64 + 64, :]

    def step(n, carry):
        out = mm(hh[...], pd[:, pl.ds(pl.multiple_of(n * 1024, 1024), 1024)])
        parts = []
        for m in range(4):
            a0, a1 = out[:TOK, m * 256:m * 256 + 128], out[TOK:, m * 256:m * 256 + 128]
            b0, b1 = out[:TOK, m * 256 + 128:m * 256 + 256], out[TOK:, m * 256 + 128:m * 256 + 256]
            parts.append(jnp.where(low, a0, b1) + pltpu.roll(jnp.where(low, b0, a1), 64, 1))
        whole = jnp.concatenate(parts, axis=1).astype(BF)
        for r in range(NY):
            out_parts[lax.rem(y + r, NY), :, pl.ds(pl.multiple_of(n * 512, 512), 512)] = whole[r * 32:r * 32 + 32, :]
        return carry

    lax.fori_loop(0, 8, step, 0)


def forward(pieces, pg, pu, pd):
    lin = pltpu.VMEM((TOK, WIDE), F32)
    return pl.pallas_call(
        forward_kernel,
        in_specs=vm(7),
        out_specs=vm(6),
        out_shape=[
            shape(FEAT, TOK), shape(256, TOK), shape(FEAT + 256, TOK), lin, lin, shape(NY, 32, D)
        ],
        scratch_shapes=[
            pltpu.VMEM((TOK, D), BF),
            pltpu.VMEM((256, FEAT), BF),
            pltpu.VMEM((TOK, 1024), BF),
            pltpu.VMEM((256, 256), BF),
        ],
        compiler_params=params(24),
        cost_estimate=cost(8),
        name="forward",
    )(*pieces, pg, pu, pd)


def emit(wswap, tiles, parts, row):
    turned = mm(wswap, tiles[...]).astype(BF)
    for rel, dst in enumerate(parts):
        for k in range(4):
            top = (rel * 4 + k) * 16
            for half in range(2):
                dst[row + half * 16:row + half * 16 + 16, k * 128:k * 128 + 128] = turned[
                    top:top + 16, half * 128:half * 128 + 128
                ]


def down_kernel(idx, cots, ht_own, sib_oth, w0, w1, w2, w3, both, part, tiles, sems):
    wswap = wire_swap(place()[1])
    def fetch(n):
        lanes = pl.ds(n * 1024, 1024)
        return pltpu.make_async_copy(cots.at[:, lanes], both.at[:, lanes], sems.at[n])

    for n in range(4):
        fetch(n).start()
    hidden = jnp.concatenate([ht_own[...], sib_oth[FEAT:, :]], axis=1)
    for n in range(8):
        if n % 2 == 0:
            fetch(n // 2).wait()
        lanes = slice(n * 512, n * 512 + 512)
        part[:, lanes] = mm(hidden, both[:, lanes]).astype(BF)
    side = lax.broadcasted_iota(jnp.int32, (16, 128), 1) // 64
    for j in range(COLS):
        for q in range(KEEP):
            i = idx[2, j * KEEP + q]
            odd = lax.rem(i, 2)
            lanes = pl.ds(pl.multiple_of((i // 2) * 128, 128), 128)
            near = part[pl.ds(pl.multiple_of(odd * 128 + j * 16, 16), 16), lanes].astype(F32)
            far = part[pl.ds(pl.multiple_of((1 - odd) * 128 + j * 16, 16), 16), lanes].astype(F32)
            tile = jnp.where(side == odd, near, pltpu.roll(far, 64, 1)).astype(BF)
            tiles[j, (q % 16) * 16:(q % 16) * 16 + 16, (q // 16) * 128:(q // 16) * 128 + 128] = tile
        emit(wswap, tiles.at[j], (w0, w1, w2, w3), j * KEEP)


def down_grads(idx, cots, ht_own, sib_oth):
    return pl.pallas_call(
        down_kernel,
        in_specs=smem(1) + far(1) + vm(2),
        out_specs=vm(4),
        out_shape=[pltpu.HBM((SLOT, 512), BF)] * 4,
        scratch_shapes=[
            pltpu.VMEM((256, D), BF),
            pltpu.VMEM((256, D), BF),
            pltpu.VMEM((COLS, 256, 256), BF),
            pltpu.SemaphoreType.DMA((4,)),
        ],
        compiler_params=params(14),
        cost_estimate=cost(0.2),
        name="down_grads",
    )(idx, cots, ht_own, sib_oth)


def back_kernel(c0, c1, c2, c3, d0, d1, d2, d3, pd, gl2, ul2, pg, pu, out_parts,
                own, parts, cots, cxt, gdt, udt, ins, part_sems, cot_sems):
    y = place()[2]
    at = cols_of(512)
    hjoin = one_hot(split_index(rows_of(256), 128), (at >> 7) * 128 + (at & 63))
    fjoin = one_hot(split_index(rows_of(256), 64), cols_of(256))
    share = pltpu.make_async_copy(out_parts, parts.at[:, :32, :], part_sems.at[4])
    share.start()
    bundle = [
        pltpu.make_async_copy(piece, cots.at[pl.ds(n * 32, 32), :], cot_sems.at[n])
        for n, piece in enumerate((c0, c1, c2, c3, d0, d1, d2, d3))
    ]
    for copy in bundle:
        copy.start()
    zero = jnp.zeros((64, TOK), BF)
    for m in range(32):
        lanes = slice(m * 128, m * 128 + 128)
        turned = jnp.concatenate([c[:, lanes] for c in (c0, c1, c2, c3)], axis=0).T
        for e in range(2):
            row = (2 * m + e) * 128
            half = turned[e * 64:e * 64 + 64, :]
            cxt[row:row + 64, :TOK] = half
            cxt[row:row + 64, TOK:] = zero
            cxt[row + 64:row + 128, :TOK] = zero
            cxt[row + 64:row + 128, TOK:] = half
    hd = mm(pd[...], cxt[...])
    high = hd.astype(BF)
    rest = (hd - high.astype(F32)).astype(BF)
    low = low_half((TOK, 128))
    for g in range(2):
        rows = slice(g * 128, g * 128 + 128)
        joined = sum(
            mm_tn(jnp.concatenate([part[rows, :TOK], part[rows, TOK:]], axis=0), hjoin) for part in (high, rest)
        )
        before = None
        for jl in range(4):
            j = g * 4 + jl
            if j == COLS:
                break
            lanes = slice(j * 128, j * 128 + 128)
            delta = joined[:, jl * 128:jl * 128 + 128]
            gl, ul = gl2[:, lanes], ul2[:, lanes]
            sig = 1.0 / (1.0 + jnp.exp(-gl))
            gd = delta * ul * sig * (1.0 + gl * (1.0 - sig))
            ud = delta * gl * sig
            for dst, val in ((gdt, gd), (udt, ud)):
                turned = val.astype(BF).T
                row = j * 128
                dst[row:row + 64, :TOK] = turned[:64, :]
                dst[row:row + 64, TOK:] = zero
                dst[row + 64:row + 128, :TOK] = zero
                dst[row + 64:row + 128, TOK:] = turned[64:, :]
            pair = slice((j // 2) * 128, (j // 2) * 128 + 128)
            if j % 2:
                own[:TOK, pair] = jnp.where(low, before[0], gd).astype(BF)
                own[TOK:, pair] = jnp.where(low, before[1], ud).astype(BF)
            elif j == COLS - 1:
                own[:TOK, pair] = jnp.where(low, gd, 0.0).astype(BF)
                own[TOK:, pair] = jnp.where(low, ud, 0.0).astype(BF)
            before = (gd, ud)
    sends = []
    for n in range(2):
        rows = slice(n * 1024, n * 1024 + 1024)
        acc = (mm(pg[rows, :], gdt[...]) + mm(pu[rows, :], udt[...])).astype(BF)
        turned = acc.T
        pairs = [
            jnp.concatenate([turned[p * TOK:p * TOK + TOK, c * 128:c * 128 + 128] for p in range(2)], axis=1)
            for c in range(8)
        ]
        whole = mm(jnp.concatenate(pairs, axis=0), fjoin).astype(BF)
        for c in range(8):
            lanes = slice(n * 2048 + c * 256, n * 2048 + c * 256 + 256)
            for r in range(NY):
                ins[lax.rem(y + r, NY), :, lanes] = whole[c * TOK + r * 32:c * TOK + r * 32 + 32, :]
        lanes = pl.ds(n * 2048, 2048)
        sends.append(pltpu.make_async_copy(ins.at[:, :, lanes], parts.at[:, 32:, lanes], part_sems.at[n]))
        sends[-1].start()
    for copy in sends + bundle + [share]:
        copy.wait()


def backward(pieces, others, pd, gl2, ul2, pg, pu, out_parts):
    return pl.pallas_call(
        back_kernel,
        in_specs=vm(4) + far(4) + vm(5) + far(1),
        out_specs=vm(1) + far(2),
        out_shape=[shape(256, 512), pltpu.HBM((NY, 64, D), BF), pltpu.HBM((256, D), BF)],
        scratch_shapes=[
            pltpu.VMEM((2 * D, 256), BF),
            pltpu.VMEM((WIDE, 256), BF),
            pltpu.VMEM((WIDE, 256), BF),
            pltpu.VMEM((NY, 32, D), BF),
            pltpu.SemaphoreType.DMA((5,)),
            pltpu.SemaphoreType.DMA((8,)),
        ],
        compiler_params=params(26),
        cost_estimate=cost(9),
        name="backward",
    )(*pieces, *others, pd, gl2, ul2, pg, pu, out_parts)


def merge_kernel(got, both):
    for n in range(0, D, 512):
        lanes = slice(n, n + 512)
        total = sum(got[r, :, lanes].astype(F32) for r in range(1, NY)) + got[0, :, lanes].astype(F32)
        for z in range(NZ):
            both[z, :, lanes] = jnp.concatenate(
                [total[z * 4:z * 4 + 4], total[32 + z * 4:36 + z * 4]], axis=0
            ).astype(BF)


def merge_y(got):
    return pl.pallas_call(
        merge_kernel,
        in_specs=vm(1),
        out_specs=vm(1)[0],
        out_shape=shape(NZ, 8, D),
        compiler_params=params(10),
        cost_estimate=cost(0.2),
        name="merge_y",
    )(got)


def inward_kernel(idx, xt_own, sib_oth, d_own, d_oth, w0, w1, w2, w3, part, tiles):
    wswap = wire_swap(place()[1])
    low = low_half((16, 128))
    for m in range(2):
        delta = jnp.concatenate([d[m * TOK:m * TOK + TOK, :] for d in (d_own, d_oth)], axis=0)

        for n in range(8):
            rows = slice(n * 256, n * 256 + 256)
            tokens = jnp.concatenate([xt_own[rows, :], sib_oth[rows, :]], axis=1)
            part[rows, :] = mm(tokens, delta).astype(BF)
        for j in range(COLS):
            odd = j % 2
            lanes = slice((j // 2) * 128, (j // 2) * 128 + 128)
            for q in range(KEEP):
                i = idx[m, j * KEEP + q]
                first = part[pl.ds(pl.multiple_of(i * 16, 16), 16), lanes].astype(F32)
                second = part[pl.ds(pl.multiple_of(1024 + i * 16, 16), 16), lanes].astype(F32)
                if odd:
                    first = pltpu.roll(first, 64, 1)
                else:
                    second = pltpu.roll(second, 64, 1)
                tile = jnp.where(low, first, second).astype(BF)
                tiles[j, (q % 16) * 16:(q % 16) * 16 + 16, (q // 16) * 128:(q // 16) * 128 + 128] = tile
            emit(wswap, tiles.at[j], (w0, w1, w2, w3), m * SLOT + j * KEEP)


def inward_grads(idx, xt_own, sib_oth, d_own, d_oth):
    return pl.pallas_call(
        inward_kernel,
        in_specs=smem(1) + vm(4),
        out_specs=vm(4),
        out_shape=[pltpu.HBM((2 * SLOT, 512), BF)] * 4,
        scratch_shapes=[pltpu.VMEM((FEAT, 512), BF), pltpu.VMEM((COLS, 256, 256), BF)],
        compiler_params=params(14),
        cost_estimate=cost(0.2),
        name="inward_grads",
    )(idx, xt_own, sib_oth, d_own, d_oth)


def from_y(value, step):
    pairs = [((y + step) % NY * NZ + z, y * NZ + z) for y in range(NY) for z in range(NZ)]
    return lax.ppermute(value, "fsdp", pairs)


def from_x(value, other):
    pairs = [((x ^ other) * NC + c, x * NC + c) for x in range(NX) for c in range(NC)]
    return lax.ppermute(value, "dp", pairs)


def from_core(value):
    pairs = [(x * NC + 1 - c, x * NC + c) for x in range(NX) for c in range(NC)]
    return lax.ppermute(value, "dp", pairs)


def z_groups():
    return [[y * NZ + z for z in range(NZ)] for y in range(NY)]


def y_groups():
    return [[y * NZ + z for y in range(NY)] for z in range(NZ)]


def over_z(value):
    return lax.all_to_all(value, "fsdp", 0, 0, axis_index_groups=z_groups(), tiled=True)


def over_y(value):
    return lax.all_to_all(value, "fsdp", 0, 0, axis_index_groups=y_groups(), tiled=True)


def copies_over_z(value):
    return over_z(jnp.broadcast_to(value[None], (NZ,) + value.shape))


def after(value, *others):
    return lax.optimization_barrier((value,) + others)[0]


def exchange_x(parts):
    return [parts[0]] + [from_x(parts[d], d) for d in range(1, NX)]


def mean_of(*parts):
    total = sum((p.astype(F32) for p in parts[1:]), parts[0].astype(F32))
    return (total * (1.0 / (NX * NC))).astype(BF)


def inward_mean_kernel(a, b, c, d, gate, up):
    for n, dst in enumerate((gate, up)):
        rows = slice(n * SLOT, n * SLOT + SLOT)
        dst[...] = mean_of(*(p[rows, :] for p in (a, b, c, d)))


def inward_mean(*parts):
    return pl.pallas_call(
        inward_mean_kernel,
        in_specs=vm(4),
        out_specs=vm(2),
        out_shape=[shape(SLOT, 512)] * 2,
        compiler_params=params(10),
        cost_estimate=cost(20),
        name="inward_mean",
    )(*parts)


def body(tokens, cotangent, gate_blocks, up_blocks, down_blocks, block_index):
    rows = tokens.shape[0]
    ring = copies_over_z(jnp.concatenate([tokens, cotangent], axis=0))
    tok_z = ring[:, :rows].reshape(NZ * rows, D)
    cot_z = ring[:, rows:].reshape(NZ * rows, D)
    tok = [tok_z] + [from_y(tok_z, s) for s in range(1, NY)]
    idx = after(block_index, tok_z, cot_z)
    pg, pu = inward_panels(idx, gate_blocks, up_blocks)
    cot_z = after(cot_z, pg)
    pd = outward_panel(idx, down_blocks)
    cot = [cot_z] + [from_y(cot_z, s) for s in range(1, NY)]

    xt_own, ht_own, sib, gl2, ul2, out_parts = forward(tok, pg, pu, pd)
    sib_oth = from_core(after(sib, *cot))
    cot_oth = [from_core(after(c, ht_own)) for c in cot]
    own, parts, cots = backward(cot, cot_oth, pd, after(gl2, sib_oth), ul2, pg, pu, out_parts)
    oth = from_core(own)
    parts_got = over_y(parts)
    down_wire = down_grads(block_index, hbm(cots), after(ht_own, parts), sib_oth)
    down_got = exchange_x(down_wire)
    wire = inward_grads(block_index, xt_own, sib_oth, after(own, down_wire[0]), oth)
    got = exchange_x(wire)
    down_grad = mean_of(*down_got)
    both = merge_y(after(parts_got, wire[0], down_grad))
    gate_grad, up_grad = inward_mean(*got)
    total = after(over_z(both), gate_grad).astype(F32).sum(axis=0).astype(BF)
    return (total[:rows], total[rows:], gate_grad, up_grad, down_grad)


def solution(mesh):
    return jax.shard_map(
        body,
        mesh=mesh,
        in_specs=(
            P(("dp", "fsdp"), None),
            P(("dp", "fsdp"), None),
            P("fsdp", None),
            P("fsdp", None),
            P("fsdp", None),
            P(None, "fsdp"),
        ),
        out_specs=(
            P(("dp", "fsdp"), None),
            P(("dp", "fsdp"), None),
            P("fsdp", "dp"),
            P("fsdp", "dp"),
            P("fsdp", "dp"),
        ),
        check_vma=False,
    )
```
